32 devices in a mesh: tok: 8 (over z, x), hd: 4 (over y, core).
Axes of the slice: x: 2, y: 2, z: 4, core: 2. Of those that a mesh axis runs over, the one named last changes fastest.
Arguments:
- residual_in: bfloat16 [2048, 2048], P('tok'), may hold values from -6 to 6
- queries: bfloat16 [2048, 2048], P('tok', 'hd'), may hold values from -11 to 11
- keys: bfloat16 [2048, 2048], P('tok', 'hd'), may hold values from -11 to 11
- values: bfloat16 [2048, 2048], P('tok', 'hd'), may hold values from -12 to 12
- segment_ids: int32 [2048], replicated, may hold values from 0 to 3, never falling along the last dimension, each value on 1 to 1024 neighbouring positions
- out_proj: bfloat16 [2048, 2048], P('hd'), may hold values from -0.125 to 0.125
- norm_gain: float32 [2048], replicated, may hold values from 0.1 to 1.9
- shared_gate: bfloat16 [2048, 2816], P(None, 'hd'), may hold values from -0.125 to 0.125
- shared_up: bfloat16 [2048, 2816], P(None, 'hd'), may hold values from -0.125 to 0.125
- shared_down: bfloat16 [2816, 2048], P('hd'), may hold values from -0.109375 to 0.109375
- expert_gate: bfloat16 [2048, 90112], P(None, ('tok', 'hd')), may hold values from -0.125 to 0.125
- expert_up: bfloat16 [2048, 90112], P(None, ('tok', 'hd')), may hold values from -0.125 to 0.125
- expert_down: bfloat16 [90112, 2048], P(('tok', 'hd')), may hold values from -0.15625 to 0.15625
- expert_ids: int32 [2048, 6], P('tok'), may hold values from 0 to 63, all different within a row; in each aligned block of 256 rows (0 to 255, 256 to 511, ...) at most 48 rows name the same one
- route_weight: float32 [2048, 6], P('tok'), may hold values from 0.05 to 0.4
- block_table: int32 [128], P('tok'), may hold values from 0 to 127, as said below
Outputs:
- output: bfloat16 [2048, 2048], P(('tok', 'hd'))
- kv_cache: bfloat16 [128, 16, 4096], P('tok', None, 'hd')
The draws below stay inside these ranges and needn't reach their ends.
Inputs may be any that keep to these rules, and one draw needn't show every extreme that they name: `segment_ids`: never falling; each prompt has 1 to 1024 tokens, one exactly 1024. `expert_ids`: each row names 6 different experts; in each aligned block of 256 rows (the rows of one index of tok) no expert is named by more than 48 rows, a bound that some block reaches. `block_table`: each aligned run of 16 entries is a permutation of its own index range.
All inputs are finite; a program needn't handle non-finite values.
Results may differ from the reference program's by a relative error of at most 0.02.
Values may be sent and summed in bfloat16 or wider, within the bound.
No kernel may reach another device: no remote copies, remote signals or barrier semaphores. Data moves between devices by JAX's collectives and lax.ppermute only.
A program may use at most 128 MiB of HBM per device.

```python
import math
import jax
import jax.numpy as jnp
import numpy as np
from jax import lax

D = 2048
HEADS = 16
HD = 128
EXPERTS = 64
FF_E = 1408
TOPK = 6
PAGE = 16
TOK_BLK = 256
TOKENS = 2048
MAXLEN = 1024
NSEQ = 4
CAP = 48
SHARED_FF = 2816
SPLIT = 1


def query_key_pair(key):
    row_width = HEADS * HD
    first_key, second_key = jax.random.split(jax.random.fold_in(key, 71), 2)
    query_out = jnp.clip(1.4 * jax.random.normal(first_key, (TOKENS, row_width), jnp.float32), -8.0, 8.0)
    key_out = jnp.clip(1.4 * jax.random.normal(second_key, (TOKENS, row_width), jnp.float32), -8.0, 8.0)
    return (query_out.astype(jnp.bfloat16), key_out.astype(jnp.bfloat16))


def draw_queries(key, part):
    return query_key_pair(key)[0]


def draw_keys(key, part):
    return query_key_pair(key)[1]


def draw_block_table(key, part):
    per_block = TOK_BLK // PAGE
    block_count = TOKENS // TOK_BLK
    block_keys = jax.random.split(jax.random.fold_in(key, 13), block_count)
    shuffled = jax.vmap(lambda single_key: jax.random.permutation(single_key, per_block))(block_keys)
    offsets = (lax.iota(jnp.int32, block_count) * per_block)[:, None]
    return (shuffled.astype(jnp.int32) + offsets).reshape(-1).astype(jnp.int32)


def steps_of(rng, dims, pieces, smallest, largest):
    factor_of, own = 1.0, jax.random.fold_in(rng, 6)
    for dim, blocks in pieces:
        steps = jnp.exp(jax.random.uniform(jax.random.fold_in(own, dim), (blocks,), jnp.float32, smallest / len(pieces), largest / len(pieces)))
        factor_of = factor_of * jnp.repeat(steps, dims[dim] // blocks).reshape([-1 if axis == dim else 1 for axis in range(len(dims))])
    return factor_of


def split_up(count, total, bound, lean):
    weights = [(1 << 20) // math.isqrt(rank ** lean) + 1 for rank in range(2, count + 1)]
    surplus, given = total - bound - (count - 1), [1] * (count - 1)
    while surplus > 0:
        movable = [i for i in range(count - 1) if given[i] < bound]
        pool, budget = sum([weights[i] for i in movable]), surplus
        for i in movable:
            extra = min(bound - given[i], max(1, budget * weights[i] // pool), surplus)
            given[i] = given[i] + extra
            surplus = surplus - extra
    return np.array([bound] + given)


def ragged(key, amount, total, reach, lean):
    if amount == 2:
        one = jax.random.randint(key, (), max(1, total - reach), min(reach, total - 1) + 1)
        return jnp.stack([one, total - one])
    sizes = jnp.asarray(split_up(amount, total, reach, lean), jnp.int32)
    couples = (amount - 1) // 2
    donor, receiver = sizes[1:1 + 2 * couples:2], sizes[2:2 + 2 * couples:2]
    margin = jnp.minimum(donor - 1, reach - receiver)
    shifted = jax.random.randint(jax.random.fold_in(key, 1), (couples,), 0, 1 << 20) % (margin + 1)
    sizes = sizes.at[1:1 + 2 * couples:2].set(donor - shifted).at[2:2 + 2 * couples:2].set(receiver + shifted)
    return sizes[jax.random.permutation(jax.random.fold_in(key, 2), amount)]


def routed_block(key, own, number, rows, amount, top, reach, skew):
    sequence = jax.random.permutation(key, amount)
    packed, common = shares(amount, rows * top, reach, skew, True), shares(amount, rows * top, reach, skew, False)
    places = jnp.arange(amount)

    def named(lengths, turn):
        used = int((lengths > 0).sum())
        fixed = max(1, used // 4)
        moved = fixed + (places - fixed + turn * (used - fixed)) % max(1, amount - fixed)
        return jnp.zeros((amount,), jnp.int32).at[sequence[jnp.where(places < fixed, places, moved)]].set(jnp.asarray(lengths, jnp.int32))

    lengths = jnp.where(number % 4 == 0, named(packed, number // 4), named(common, number - number // 4 - 1))
    mixed = jax.random.permutation(jax.random.fold_in(own, 3), amount)
    source_of, taker = mixed[0:amount // 2 * 2:2], mixed[1:amount // 2 * 2:2]
    margin = jnp.minimum(lengths[source_of] - 1, reach - lengths[taker]) // 2
    margin = jnp.where((source_of == sequence[0]) | (taker == sequence[0]) | (lengths[taker] == 0), 0, jnp.maximum(margin, 0))
    moved = jax.random.randint(jax.random.fold_in(own, 4), (amount // 2,), 0, 1 << 20) % (margin + 1)
    lengths = lengths.at[source_of].add(-moved).at[taker].add(moved)
    labels = jnp.searchsorted(jnp.cumsum(lengths), jnp.arange(rows * top), side="right").astype(jnp.int32)
    listing = labels.reshape(top, rows).T
    listing = listing[jax.random.permutation(jax.random.fold_in(own, 1), rows)]
    turn = jax.random.randint(jax.random.fold_in(own, 2), (rows, 1), 0, top)
    return jnp.take_along_axis(listing, (jnp.arange(top)[None, :] + turn) % top, axis=1)


def shares(amount, total, most, lean, full):
    loads = [(1 << 20) // math.isqrt(standing ** lean) + 1 for standing in range(1, amount + 1)]
    largest = most if full else min(most, max(-(-total // amount), total * loads[0] // sum(loads)))
    least = 1 if total - largest >= amount - 1 else 0
    counts, surplus = [largest] + [least] * (amount - 1), total - largest - least * (amount - 1)
    while surplus > 0:
        candidates = [i for i in range(1, amount) if counts[i] < largest] or [i for i in range(1, amount) if counts[i] < most]
        mass, left = sum([loads[i] for i in candidates]), surplus
        for i in candidates:
            addition = min(most - counts[i], max(1, left * loads[i] // mass), surplus)
            counts[i] = counts[i] + addition
            surplus = surplus - addition
    return np.array(counts)


def centred(key, shape, spread, bound, shards=(), held_as=jnp.bfloat16):
    values = spread * jax.random.normal(key, shape, jnp.float32)
    if shards:
        values = values * steps_of(key, shape, shards, -0.22, 0.18)
    return jnp.clip(values, -bound, bound).astype(held_as)


def setup_inputs(seed: int = 0) -> dict:
    splits = jax.random.split(jax.random.key(seed), 17)
    residual_in = centred(splits[0], (TOKENS, D), 1.0, 6.0, ((0, 8),))
    queries = draw_queries(jax.random.fold_in(splits[16], 71), 0)
    keys = draw_keys(jax.random.fold_in(splits[16], 71), 0)
    values = centred(splits[3], (TOKENS, HEADS * HD), 2.0, 12.0, ((0, 8), (1, 4)))
    segment_ids = jnp.searchsorted(jnp.cumsum(ragged(splits[4], NSEQ, TOKENS, MAXLEN, 2)), jnp.arange(TOKENS), side="right").astype(jnp.int32)
    out_proj = centred(splits[5], (HEADS * HD, D), (HEADS * HD) ** -0.5, 0.125, ((0, 4),))
    norm_gain = jnp.clip(1.0 + 0.18 * jax.random.normal(splits[6], (D,), jnp.float32), 0.1, 1.9)
    shared_gate = centred(splits[7], (D, SHARED_FF), D ** -0.5, 0.125, ((1, 4),))
    shared_up = centred(splits[8], (D, SHARED_FF), D ** -0.5, 0.125, ((1, 4),))
    shared_down = centred(splits[9], (SHARED_FF, D), SHARED_FF ** -0.5, 0.109375, ((0, 4),))
    expert_gate = centred(splits[10], (D, EXPERTS * FF_E), D ** -0.5, 0.125, ((1, 32),))
    expert_up = centred(splits[11], (D, EXPERTS * FF_E), D ** -0.5, 0.125, ((1, 32),))
    expert_down = centred(splits[12], (EXPERTS * FF_E, D), FF_E ** -0.5, 0.15625, ((0, 32),))
    expert_ids_keys = jax.random.split(jax.random.fold_in(splits[13], 1), TOKENS // TOK_BLK)
    expert_ids_turns = jax.random.permutation(jax.random.fold_in(splits[13], 3), TOKENS // TOK_BLK)
    expert_ids = jax.vmap(lambda own, number: routed_block(jax.random.fold_in(splits[13], 2), own, number, TOK_BLK, EXPERTS, TOPK, CAP, 2))(expert_ids_keys, expert_ids_turns).reshape((TOKENS, TOPK))
    route_weight = jnp.clip(0.05 + 0.35 * jax.random.uniform(splits[14], (TOKENS, TOPK), jnp.float32) ** steps_of(splits[14], (TOKENS, TOPK), ((0, 8),), -0.2, 0.2), 0.05, 0.4)
    block_table = draw_block_table(jax.random.fold_in(splits[16], 71), 0)
    return dict(residual_in=residual_in, queries=queries, keys=keys, values=values, segment_ids=segment_ids, out_proj=out_proj, norm_gain=norm_gain, shared_gate=shared_gate, shared_up=shared_up, shared_down=shared_down, expert_gate=expert_gate, expert_up=expert_up, expert_down=expert_down, expert_ids=expert_ids, route_weight=route_weight, block_table=block_table)


MASKED_SCORE = -1e+30
NORM_EPSILON = 1e-06

def attention(queries, keys, values, segment_ids):
    row_width = HEADS * HD
    key_all = keys.reshape(TOKENS, HEADS, HD).astype(jnp.float32)
    value_all = values.reshape(TOKENS, HEADS, HD).astype(jnp.float32)
    positions = lax.iota(jnp.int32, TOKENS)

    def one_block(blk_index):
        blk_start = (blk_index * TOK_BLK).astype(jnp.int32)
        query_blk = lax.dynamic_slice_in_dim(queries, blk_start, TOK_BLK, 0).reshape(TOK_BLK, HEADS, HD).astype(jnp.float32)
        query_pos = blk_start + lax.iota(jnp.int32, TOK_BLK)
        query_seg = lax.dynamic_slice_in_dim(segment_ids, blk_start, TOK_BLK, 0)
        scores = jnp.einsum('qhd,khd->hqk', query_blk, key_all) / math.sqrt(HD)
        allowed = (segment_ids[None, :] == query_seg[:, None]) & (positions[None, :] <= query_pos[:, None])
        scores = jnp.where(allowed[None], scores, MASKED_SCORE)
        row_max = lax.optimization_barrier(jnp.max(scores, axis=2, keepdims=True))
        exp_scores = jnp.where(allowed[None], jnp.exp(scores - row_max), 0.0)
        denom_sum = lax.optimization_barrier(jnp.sum(exp_scores, axis=2))
        prob_bf = lax.optimization_barrier(exp_scores.astype(jnp.bfloat16)).astype(jnp.float32)
        mixed_heads = jnp.einsum('hqk,khd->qhd', prob_bf, value_all) / jnp.transpose(denom_sum)[:, :, None]
        return mixed_heads.reshape(TOK_BLK, row_width).astype(jnp.bfloat16)
    blocks_out = lax.map(one_block, lax.iota(jnp.int32, TOKENS // TOK_BLK))
    return blocks_out.reshape(TOKENS, row_width)

def routed_sum(normed, expert_gate, expert_up, expert_down, expert_ids, route_weight):
    row_limit = TOKENS // TOK_BLK * CAP
    part_width = FF_E // SPLIT

    def one_expert(carried, expert):
        is_hit = expert_ids == expert
        chosen = jnp.any(is_hit, axis=1)
        weight_row = lax.optimization_barrier(jnp.sum(jnp.where(is_hit, route_weight, 0.0), axis=1))
        row_order = jnp.argsort(jnp.where(chosen, 0, 1).astype(jnp.int32), stable=True)[:row_limit].astype(jnp.int32)
        is_valid = chosen[row_order]
        sel_rows = normed[row_order]
        gate_cols = lax.dynamic_slice_in_dim(expert_gate, expert * FF_E, FF_E, 1)
        up_cols = lax.dynamic_slice_in_dim(expert_up, expert * FF_E, FF_E, 1)
        down_rows = lax.dynamic_slice_in_dim(expert_down, expert * FF_E, FF_E, 0)
        result = jnp.zeros((row_limit, D), jnp.float32)
        for part_index in range(SPLIT):
            lower = part_index * part_width
            gate_val = jnp.dot(sel_rows, gate_cols[:, lower:lower + part_width], preferred_element_type=jnp.float32)
            up_val = jnp.dot(sel_rows, up_cols[:, lower:lower + part_width], preferred_element_type=jnp.float32)
            hidden = (jax.nn.silu(gate_val) * up_val).astype(jnp.bfloat16)
            part_out = jnp.dot(hidden, down_rows[lower:lower + part_width], preferred_element_type=jnp.float32).astype(jnp.bfloat16)
            result = result + lax.optimization_barrier(part_out).astype(jnp.float32)
        pick_scale = jnp.where(is_valid, weight_row[row_order], 0.0)
        carried = carried.at[row_order].add(result * pick_scale[:, None])
        return (carried, None)
    total_out, _ = lax.scan(one_expert, jnp.zeros((TOKENS, D), jnp.float32), lax.iota(jnp.int32, EXPERTS))
    return total_out

def reference(residual_in, queries, keys, values, segment_ids, out_proj, norm_gain, shared_gate, shared_up, shared_down, expert_gate, expert_up, expert_down, expert_ids, route_weight, block_table):
    attended = attention(queries, keys, values, segment_ids)
    resid_state = residual_in.astype(jnp.float32) + jnp.dot(attended, out_proj, preferred_element_type=jnp.float32)
    mean_square = lax.optimization_barrier(jnp.mean(resid_state * resid_state, axis=1, keepdims=True))
    normed = (resid_state * lax.rsqrt(mean_square + NORM_EPSILON) * norm_gain).astype(jnp.bfloat16)
    gate_val = jnp.dot(normed, shared_gate, preferred_element_type=jnp.float32)
    up_val = jnp.dot(normed, shared_up, preferred_element_type=jnp.float32)
    shared_hidden = (jax.nn.silu(gate_val) * up_val).astype(jnp.bfloat16)
    shared_out = jnp.dot(shared_hidden, shared_down, preferred_element_type=jnp.float32)
    routed = routed_sum(normed, expert_gate, expert_up, expert_down, expert_ids, route_weight)
    output = (resid_state + shared_out + routed).astype(jnp.bfloat16)
    page_data = jnp.stack([keys.reshape(TOKENS, HEADS, HD), values.reshape(TOKENS, HEADS, HD)], axis=2)
    page_data = page_data.reshape(TOKENS // PAGE, PAGE, 2 * HEADS * HD)
    kv_pages = jnp.zeros_like(page_data).at[block_table].set(page_data)
    return (output, kv_pages)
```

```python
import math

import jax
import jax.numpy as jnp
import numpy as np
from jax import lax
from jax.experimental import pallas as pl
from jax.experimental.pallas import tpu as pltpu
from jax.sharding import PartitionSpec as P

HD = 128
EXPERTS = 64
FF_E = 1408
PAGE = 16
CAP = 48


MASKED_SCORE = -1e30
NORM_EPSILON = 1e-06


def from_behind(array, axis, by):
    length = lax.axis_size(axis)
    pairs = [(i, i + by) for i in range(length) if 0 <= i + by < length]
    return lax.ppermute(array, axis, pairs)


def rms_normed(resid_state, norm_gain):
    mean_square = jnp.mean(resid_state * resid_state, axis=1, keepdims=True)
    return (resid_state * lax.rsqrt(mean_square + NORM_EPSILON) * norm_gain).astype(jnp.bfloat16)


def general_body(
    residual_in,
    queries,
    keys,
    values,
    segment_ids,
    out_proj,
    norm_gain,
    shared_gate,
    shared_up,
    shared_down,
    expert_gate,
    expert_up,
    expert_down,
    expert_ids,
    route_weight,
    block_table,
):
    block_len = residual_in.shape[0]
    model_width = residual_in.shape[1]
    tok_count = lax.axis_size("tok")
    hd_count = lax.axis_size("hd")
    tok_here = lax.axis_index("tok")
    hd_here = lax.axis_index("hd")
    heads_here = queries.shape[1] // HD
    query_three = queries.reshape(block_len, heads_here, HD)
    offsets = lax.iota(jnp.int32, block_len)
    query_pos = tok_here * block_len + offsets
    query_seg = lax.dynamic_slice_in_dim(segment_ids, tok_here * block_len, block_len, 0)

    def attend(carried, key_blk, value_blk, source):
        safe_source = jnp.maximum(source, 0)
        key_seg = lax.dynamic_slice_in_dim(segment_ids, safe_source * block_len, block_len, 0)
        key_pos = source * block_len + offsets

        def compute(current):
            running_max, denom_sum, weighted_sum = current
            scores = jnp.einsum(
                "qhd,khd->hqk",
                query_three,
                key_blk.reshape(block_len, heads_here, HD),
                preferred_element_type=jnp.float32,
            ) / math.sqrt(HD)
            allowed = (key_seg[None, :] == query_seg[:, None]) & (
                key_pos[None, :] <= query_pos[:, None]
            )
            scores = jnp.where(allowed[None], scores, MASKED_SCORE)
            new_max = jnp.maximum(running_max, jnp.max(scores, axis=2))
            shrink = jnp.exp(running_max - new_max)
            exp_scores = jnp.where(allowed[None], jnp.exp(scores - new_max[:, :, None]), 0.0)
            denom_sum = denom_sum * shrink + jnp.sum(exp_scores, axis=2)
            update = jnp.einsum(
                "hqk,khd->qhd",
                exp_scores.astype(jnp.bfloat16),
                value_blk.reshape(block_len, heads_here, HD),
                preferred_element_type=jnp.float32,
            )
            weighted_sum = weighted_sum * jnp.transpose(shrink)[:, :, None] + update
            return (new_max, denom_sum, weighted_sum)

        is_live = (source >= 0) & (
            segment_ids[safe_source * block_len + block_len - 1] >= query_seg[0]
        )
        return lax.cond(is_live, compute, lambda unchanged: unchanged, carried)

    initial = (
        jnp.full((heads_here, block_len), MASKED_SCORE, jnp.float32),
        jnp.zeros((heads_here, block_len), jnp.float32),
        jnp.zeros((block_len, heads_here, HD), jnp.float32),
    )
    carried = attend(initial, keys, values, tok_here)

    def relay(relay_step, loop_carry):
        moving, inner_state = loop_carry
        moving = from_behind(moving, "tok", 1)
        inner_state = attend(inner_state, moving[0], moving[1], tok_here - relay_step - 1)
        return (moving, inner_state)

    _, final_state = lax.fori_loop(0, tok_count // 2, relay, (jnp.stack([keys, values]), carried))
    weighted_sum = final_state[2]
    denom_sum = final_state[1]
    attended = (
        (weighted_sum / jnp.transpose(denom_sum)[:, :, None])
        .astype(jnp.bfloat16)
        .reshape(block_len, heads_here * HD)
    )
    row_count = block_len // hd_count
    row_start = hd_here * row_count
    head_terms = jnp.dot(attended, out_proj, preferred_element_type=jnp.float32)
    resid_full = residual_in.astype(jnp.float32) + lax.psum(
        head_terms.astype(jnp.bfloat16), "hd"
    ).astype(jnp.float32)
    normed = rms_normed(resid_full, norm_gain)
    resid_rows = lax.dynamic_slice_in_dim(resid_full, row_start, row_count, 0)
    shared_gate_val = jnp.dot(normed, shared_gate, preferred_element_type=jnp.float32)
    shared_up_val = jnp.dot(normed, shared_up, preferred_element_type=jnp.float32)
    shared_hidden = (jax.nn.silu(shared_gate_val) * shared_up_val).astype(jnp.bfloat16)
    partial_out = jnp.dot(shared_hidden, shared_down, preferred_element_type=jnp.float32)
    slice_width = expert_gate.shape[1]
    held_count = max(1, slice_width // FF_E)
    part_width = slice_width // held_count
    per_group = slice_width * hd_count // FF_E
    first_local = hd_here * slice_width // FF_E
    expert_range = lax.iota(jnp.int32, EXPERTS)
    onehot = jnp.sum(
        (expert_ids[:, :, None] == expert_range[None, None, :]).astype(jnp.int32), axis=1
    )
    earlier = jnp.cumsum(onehot, axis=0) - onehot
    slot_index = jnp.take_along_axis(earlier, expert_ids, axis=1)
    flat_expert = expert_ids.reshape(-1)
    flat_slot = slot_index.reshape(-1)
    row_source = jnp.repeat(offsets, expert_ids.shape[1])
    row_table = (
        jnp.full((EXPERTS, CAP), block_len, jnp.int32).at[flat_expert, flat_slot].set(row_source)
    )
    weight_table = (
        jnp.zeros((EXPERTS, CAP), jnp.float32)
        .at[flat_expert, flat_slot]
        .set(route_weight.reshape(-1))
    )
    send_rows = lax.dynamic_slice_in_dim(
        row_table.reshape(tok_count, per_group, CAP), first_local, held_count, 1
    )
    send_weight = lax.dynamic_slice_in_dim(
        weight_table.reshape(tok_count, per_group, CAP), first_local, held_count, 1
    )
    padded_rows = jnp.concatenate([normed, jnp.zeros((1, model_width), jnp.bfloat16)], axis=0)
    outgoing = padded_rows[send_rows]
    gate_three = expert_gate.reshape(model_width, held_count, part_width)
    up_three = expert_up.reshape(model_width, held_count, part_width)
    down_three = expert_down.reshape(held_count, part_width, model_width)
    incoming = lax.all_to_all(outgoing, "tok", split_axis=0, concat_axis=0, tiled=True)
    gate_val = jnp.einsum(
        "secd,def->secf", incoming, gate_three, preferred_element_type=jnp.float32
    )
    up_val = jnp.einsum("secd,def->secf", incoming, up_three, preferred_element_type=jnp.float32)
    hidden = (jax.nn.silu(gate_val) * up_val).astype(jnp.bfloat16)
    result = jnp.einsum(
        "secf,efd->secd", hidden, down_three, preferred_element_type=jnp.float32
    ).astype(jnp.bfloat16)
    returned_rows = lax.all_to_all(result, "tok", split_axis=0, concat_axis=0, tiled=True)
    weighted_rows = returned_rows.astype(jnp.float32) * send_weight[:, :, :, None]
    routed = (
        jnp.zeros((block_len + 1, model_width), jnp.float32)
        .at[send_rows.reshape(-1)]
        .add(weighted_rows.reshape(-1, model_width))[:block_len]
    )
    summed_rows = lax.psum_scatter(
        (partial_out + routed).astype(jnp.bfloat16), "hd", scatter_dimension=0, tiled=True
    ).astype(jnp.float32)
    output = (resid_rows + summed_rows).astype(jnp.bfloat16)
    page_count = block_len // PAGE
    page_data = jnp.stack(
        [keys.reshape(block_len, heads_here, HD), values.reshape(block_len, heads_here, HD)], axis=2
    )
    page_data = page_data.reshape(page_count, PAGE, heads_here * 2 * HD)
    local_pages = block_table - tok_here * page_count
    kv_pages = jnp.zeros_like(page_data).at[local_pages].set(page_data)
    return (output, kv_pages)


NZ = 4
BOTH = ("tok", "hd")
ROWS = 64
BLOCK = 256
GROUP_ROWS = 1024
SLOTS = 4 * CAP
NEXT_Z = {0: 1, 1: 3, 3: 2, 2: 0}
BACK_Z = {after: before for before, after in NEXT_Z.items()}
DEVICES = [(z, x, y, c) for z in range(NZ) for x in range(2) for y in range(2) for c in range(2)]


def flat_index(z, x, y, c):
    return (z * 2 + x) * 4 + y * 2 + c


def pairs_of(target):
    return [(flat_index(*device), flat_index(*target(*device))) for device in DEVICES]


Z_ON = pairs_of(lambda z, x, y, c: (NEXT_Z[z], x, y, c))
Z_BACK = pairs_of(lambda z, x, y, c: (BACK_Z[z], x, y, c))
Z_TWO = pairs_of(lambda z, x, y, c: (NEXT_Z[NEXT_Z[z]], x, y, c))
CORE_SWAP = pairs_of(lambda z, x, y, c: (z, x, y, 1 - c))
Y_SWAP = pairs_of(lambda z, x, y, c: (z, x, 1 - y, c))
X_THEN_Y = pairs_of(lambda z, x, y, c: (z, 1 - x, y, c) if c == 0 else (z, x, 1 - y, c))
Y_THEN_X = pairs_of(lambda z, x, y, c: (z, x, 1 - y, c) if c == 0 else (z, 1 - x, y, c))


def slice_order():
    order = np.zeros((len(DEVICES), 2, 16), np.int32)
    for z, x, y, c in DEVICES:
        at_step = [z]
        for _ in range(3):
            at_step.append(BACK_Z[at_step[-1]])
        mine = {
            0: [(1 - x, y, 0), (1 - x, y, 1), (1 - x, 1 - y, 0)],
            1: [(x, 1 - y, 1), (x, 1 - y, 0), (1 - x, 1 - y, 1)],
        }
        places = [(x, y, c), (x, y, 1 - c)] + mine[c] + mine[1 - c]
        for group in range(2):
            listed = [
                flat_index(at_step[2 * group + part], *place) for place in places for part in range(2)
            ]
            order[flat_index(z, x, y, c), group] = listed
    return order


def send(array, pairs):
    return lax.ppermute(array, BOTH, pairs)


def added(first, second):
    return (first.astype(jnp.float32) + second.astype(jnp.float32)).astype(jnp.bfloat16)


def whole(space=pltpu.VMEM):
    return pl.BlockSpec(memory_space=space)


def pages_kernel(table, keys, values, joined, pages):
    heads = keys.shape[1] // HD
    for head in range(heads):
        lanes = slice(head * HD, (head + 1) * HD)
        joined[:, 2 * head * HD : (2 * head + 1) * HD] = keys[:, lanes]
        joined[:, (2 * head + 1) * HD : (2 * head + 2) * HD] = values[:, lanes]
    for page in range(keys.shape[0] // PAGE):
        pages[table[page]] = joined[page * PAGE : (page + 1) * PAGE, :]


def write_pages(keys, values, local_pages):
    rows, width = keys.shape
    return pl.pallas_call(
        pages_kernel,
        out_shape=(
            jax.ShapeDtypeStruct((rows, 2 * width), keys.dtype),
            jax.ShapeDtypeStruct((rows // PAGE, PAGE, 2 * width), keys.dtype),
        ),
        in_specs=[whole(pltpu.SMEM), whole(), whole()],
        out_specs=(whole(), whole()),
    )(local_pages, keys, values)


HEADS_HERE = 4


def attend_block(segments, query_segment, queries, block, source, diagonal, top, total, mixed):
    allowed = segments[pl.ds(source, 1), :] == query_segment[...]
    if diagonal:
        rows = lax.broadcasted_iota(jnp.int32, (BLOCK, BLOCK), 0)
        columns = lax.broadcasted_iota(jnp.int32, (BLOCK, BLOCK), 1)
        allowed = allowed & (columns <= rows)
    for head in range(HEADS_HERE):
        key = block[:, 2 * head * HD : (2 * head + 1) * HD]
        value = block[:, (2 * head + 1) * HD : (2 * head + 2) * HD]
        scores = lax.dot_general(
            queries[:, head * HD : (head + 1) * HD],
            key,
            (((1,), (1,)), ((), ())),
            preferred_element_type=jnp.float32,
        ) * (1.0 / math.sqrt(HD))
        scores = jnp.where(allowed, scores, MASKED_SCORE)
        largest = jnp.max(scores, axis=1, keepdims=True)
        if not diagonal:
            largest = jnp.maximum(largest, top[head][:, :1])
        exp_scores = jnp.exp(scores - largest)
        update = jnp.dot(exp_scores.astype(jnp.bfloat16), value, preferred_element_type=jnp.float32)
        added_up = jnp.sum(exp_scores, axis=1, keepdims=True)
        if diagonal:
            total[head] = jnp.broadcast_to(added_up, (BLOCK, HD))
            mixed[head] = update
        else:
            shrink = jnp.exp(top[head] - largest)
            total[head] = total[head] * shrink + added_up
            mixed[head] = mixed[head] * shrink + update
        top[head] = jnp.broadcast_to(largest, (BLOCK, HD))


def attend_earlier(place, segment_list, segments, query_segment, queries, blocks, top, total, mixed):
    for block, source in blocks:
        safe = jnp.maximum(source, 0)
        live = (source >= 0) & (
            segment_list[safe * BLOCK + BLOCK - 1] == segment_list[place[0] * BLOCK]
        )

        @pl.when(live)
        def _():
            attend_block(
                segments, query_segment, queries, block, safe, False, top, total, mixed
            )


def attention_first(place, segment_list, segments, query_segment, queries, own, near_x, near_z, top, total, mixed):
    here = place[0]
    attend_block(segments, query_segment, queries, own, here, True, top, total, mixed)
    odd = here % 2
    blocks = [(near_x, jnp.where(odd == 1, here - 1, -1)), (near_z, here - 2)]
    attend_earlier(
        place, segment_list, segments, query_segment, queries, blocks, top, total, mixed
    )


def attention_second(
    place, segment_list, segments, query_segment, queries, cross, far, far_cross, projection,
    top_in, total_in, mixed_in, sent, kept, top, total, mixed, attended,
):
    here, hd = place[0], place[1]
    odd = here % 2
    top[...] = top_in[...]
    total[...] = total_in[...]
    mixed[...] = mixed_in[...]
    blocks = [
        (cross, jnp.where(odd == 1, here - 3, here - 1)),
        (far, here - 4),
        (far_cross, jnp.where(odd == 1, -1, here - 3)),
    ]
    attend_earlier(
        place, segment_list, segments, query_segment, queries, blocks, top, total, mixed
    )
    for head in range(HEADS_HERE):
        attended[:, head * HD : (head + 1) * HD] = (mixed[head] / total[head]).astype(jnp.bfloat16)
    mate, across = hd ^ 1, hd ^ 2

    def rows_of(first, second):
        return jnp.concatenate(
            [
                attended[pl.ds(pl.multiple_of(quarter * ROWS, ROWS), ROWS), :]
                for quarter in (first, second)
            ],
            axis=0,
        )

    sent[...] = jnp.dot(
        rows_of(mate, mate ^ 2), projection[...], preferred_element_type=jnp.float32
    ).astype(jnp.bfloat16)
    kept[...] = jnp.dot(rows_of(hd, across), projection[...], preferred_element_type=jnp.float32)


def attention(place, segment_ids, query_segment, queries, own, near_x, near_z, cross, far, far_cross, out_proj):
    segments = segment_ids.reshape(-1, BLOCK)
    state = jax.ShapeDtypeStruct((HEADS_HERE, BLOCK, HD), jnp.float32)
    smem, vmem = whole(pltpu.SMEM), whole()
    first = pl.pallas_call(
        attention_first,
        out_shape=(state, state, state),
        in_specs=[smem, smem] + [vmem] * 6,
        out_specs=(vmem, vmem, vmem),
        cost_estimate=pl.CostEstimate(flops=6 * 10**8, bytes_accessed=4 * 10**6, transcendentals=6 * 10**5),
    )(place, segment_ids, segments, query_segment, queries, own, near_x, near_z)
    return pl.pallas_call(
        attention_second,
        out_shape=(
            jax.ShapeDtypeStruct((2 * ROWS, out_proj.shape[1]), jnp.bfloat16),
            jax.ShapeDtypeStruct((2 * ROWS, out_proj.shape[1]), jnp.float32),
        ),
        in_specs=[smem, smem] + [vmem] * 10,
        out_specs=(vmem, vmem),
        scratch_shapes=[pltpu.VMEM(state.shape, jnp.float32)] * 3
        + [pltpu.VMEM((BLOCK, HEADS_HERE * HD), jnp.bfloat16)],
        compiler_params=pltpu.CompilerParams(vmem_limit_bytes=32 * 2**20),
    )(place, segment_ids, segments, query_segment, queries, cross, far, far_cross, out_proj, *first)


CHUNK = 256
DEPTH = 4


def expert_chunks():
    chunks = []
    for expert in range(2):
        for low in range(0, FF_E, CHUNK):
            chunks.append((expert, expert * FF_E + low, min(CHUNK, FF_E - low)))
    return chunks


def gated(rows, gate, up):
    gate_val = jnp.dot(rows, gate, preferred_element_type=jnp.float32)
    up_val = jnp.dot(rows, up, preferred_element_type=jnp.float32)
    return (gate_val / (1.0 + jnp.exp(-gate_val)) * up_val).astype(jnp.bfloat16)


def experts_kernel(with_shared, *refs):
    (place, slot_row, weight_row, slot_column, own_rows, near_rows, mate_rows, gate, up, down) = refs[:10]
    refs = refs[10:]
    if with_shared:
        shared_gate, shared_up, shared_down = refs[:3]
        refs = refs[3:]
    sent, kept, gate_buf, up_buf, down_buf, arrived, rows, results, scaled = refs[:9]
    refs = refs[9:]
    chunks = expert_chunks()

    def copies(number):
        expert, low, size = chunks[number]
        slot = number % DEPTH
        return (
            pltpu.make_async_copy(
                gate.at[:, pl.ds(low, size)], gate_buf.at[slot, :, pl.ds(0, size)], arrived.at[slot, 0]
            ),
            pltpu.make_async_copy(
                up.at[:, pl.ds(low, size)], up_buf.at[slot, :, pl.ds(0, size)], arrived.at[slot, 1]
            ),
            pltpu.make_async_copy(
                down.at[pl.ds(low, size), :], down_buf.at[slot, pl.ds(0, size), :], arrived.at[slot, 2]
            ),
        )

    for number in range(DEPTH):
        for copy in copies(number):
            copy.start()
    if with_shared:
        s_gate, s_up, s_down, s_arrived, s_rows, s_result = refs
        shared_copies = [
            pltpu.make_async_copy(source, target, s_arrived.at[number])
            for number, (source, target) in enumerate(
                ((shared_gate, s_gate), (shared_up, s_up), (shared_down, s_down))
            )
        ]
        for copy in shared_copies:
            copy.start()
        upper = place[1] % 2 == 1
        s_rows[0:ROWS] = own_rows[0:ROWS]
        s_rows[ROWS : 2 * ROWS] = own_rows[2 * ROWS : 3 * ROWS]
        for part in range(2):
            taken = slice(part * 2 * ROWS, part * 2 * ROWS + ROWS)

            @pl.when(upper)
            def _():
                s_rows[(2 + part) * ROWS : (3 + part) * ROWS] = near_rows[taken]

            @pl.when(jnp.logical_not(upper))
            def _():
                s_rows[(2 + part) * ROWS : (3 + part) * ROWS] = mate_rows[taken]

    slot_numbers = lax.broadcasted_iota(jnp.int32, (SLOTS, GROUP_ROWS), 0)
    slot_weight = []
    for expert in range(2):
        hit = slot_row[expert : expert + 1, :] == slot_numbers
        slot_weight.append(
            jnp.sum(jnp.where(hit, weight_row[expert : expert + 1, :], 0.0), axis=1, keepdims=True)
        )
        pick = jnp.where(hit, 1.0, 0.0).astype(jnp.bfloat16)
        rows[expert] = (
            jnp.dot(pick[:, :256], own_rows[...], preferred_element_type=jnp.float32)
            + jnp.dot(pick[:, 256:640], near_rows[...], preferred_element_type=jnp.float32)
            + jnp.dot(pick[:, 640:], mate_rows[...], preferred_element_type=jnp.float32)
        ).astype(jnp.bfloat16)

    for number, (expert, low, size) in enumerate(chunks):
        slot = number % DEPTH
        for copy in copies(number):
            copy.wait()
        hidden = gated(rows[expert], gate_buf[slot, :, :size], up_buf[slot, :, :size])
        term = jnp.dot(hidden, down_buf[slot, :size, :], preferred_element_type=jnp.float32)
        if low == expert * FF_E:
            results[...] = term
        elif low + size < (expert + 1) * FF_E:
            results[...] += term
        else:
            scaled[expert * SLOTS : (expert + 1) * SLOTS] = (
                (results[...] + term) * slot_weight[expert]
            ).astype(jnp.bfloat16)
        if number + DEPTH < len(chunks):
            for copy in copies(number + DEPTH):
                copy.start()

    if with_shared:
        for copy in shared_copies:
            copy.wait()
        s_result[...] = jnp.dot(
            gated(s_rows[...], s_gate[...], s_up[...]), s_down[...], preferred_element_type=jnp.float32
        )

    slot_lanes = lax.broadcasted_iota(jnp.int32, (2 * ROWS, 2 * SLOTS), 1)
    targets = [(kept, 3), (sent, 3), (kept, 0), (kept, 1), (kept, 2), (sent, 0), (sent, 1), (sent, 2)]
    for part, (target, index) in enumerate(targets):
        taken = slice(part * 2 * ROWS, (part + 1) * 2 * ROWS)
        first, second = slot_column[taken, 0:1], slot_column[taken, 1:2]
        hit = (first == slot_lanes) | ((second >= 0) & (second + SLOTS == slot_lanes))
        value = jnp.dot(
            jnp.where(hit, 1.0, 0.0).astype(jnp.bfloat16), scaled[...], preferred_element_type=jnp.float32
        )
        base = index * 2 * ROWS
        term = None
        if with_shared and part < 2:
            term = s_result[part * ROWS : (part + 1) * ROWS]
        elif with_shared and part in (2, 3, 5, 6):
            here = upper if part < 4 else jnp.logical_not(upper)
            place_of = 2 + (part - 2) % 3
            term = jnp.where(here, s_result[place_of * ROWS : (place_of + 1) * ROWS], 0.0)
        low_rows = value[:ROWS] if term is None else value[:ROWS] + term
        target[base : base + ROWS] = low_rows.astype(jnp.bfloat16)
        target[base + ROWS : base + 2 * ROWS] = value[ROWS:].astype(jnp.bfloat16)


def experts(place, tables, gathered, weights, shared):
    slot_row, weight_row, slot_column = tables
    width = weights[0].shape[0]
    hbm, vmem = whole(pl.ANY), whole()
    scratch = [
        pltpu.VMEM((DEPTH, width, CHUNK), jnp.bfloat16),
        pltpu.VMEM((DEPTH, width, CHUNK), jnp.bfloat16),
        pltpu.VMEM((DEPTH, CHUNK, width), jnp.bfloat16),
        pltpu.SemaphoreType.DMA((DEPTH, 3)),
        pltpu.VMEM((2, SLOTS, width), jnp.bfloat16),
        pltpu.VMEM((SLOTS, width), jnp.float32),
        pltpu.VMEM((2 * SLOTS, width), jnp.bfloat16),
    ]
    operands = [place, slot_row, weight_row, slot_column, *gathered, *weights]
    if shared is not None:
        operands += list(shared)
        scratch += [pltpu.VMEM(array.shape, array.dtype) for array in shared]
        scratch += [
            pltpu.SemaphoreType.DMA((3,)),
            pltpu.VMEM((BLOCK, width), jnp.bfloat16),
            pltpu.VMEM((BLOCK, width), jnp.float32),
        ]
    half = jax.ShapeDtypeStruct((GROUP_ROWS // 2, width), jnp.bfloat16)
    return pl.pallas_call(
        lambda *refs: experts_kernel(shared is not None, *refs),
        out_shape=(half, half),
        in_specs=[whole(pltpu.SMEM)] + [vmem] * 6 + [hbm] * (len(operands) - 7),
        out_specs=(vmem, vmem),
        scratch_shapes=scratch,
        compiler_params=pltpu.CompilerParams(vmem_limit_bytes=56 * 2**20),
        cost_estimate=pl.CostEstimate(
            flops=8 * 10**9, bytes_accessed=44 * 10**6, transcendentals=10**6
        ),
    )(*operands)


def gather_plane(rows):
    count = rows.shape[0]
    own = jnp.concatenate([rows, send(rows, CORE_SWAP)], axis=0)
    near = send(own, X_THEN_Y)
    corner = send(near[:count], Y_THEN_X)
    fetched = jnp.concatenate([near, corner], axis=0)
    return own, fetched, send(fetched, CORE_SWAP)


def sum_plane(sent, kept):
    kept = added(kept, send(sent, CORE_SWAP))
    count = kept.shape[0] // 4
    near = jnp.concatenate(
        [added(kept[:count], send(kept[2 * count : 3 * count], Y_THEN_X)), kept[count : 2 * count]], axis=0
    )
    from_near = send(near, X_THEN_Y)
    return (
        kept[3 * count :].astype(jnp.float32)
        + from_near[:count].astype(jnp.float32)
        + send(from_near[count:], CORE_SWAP).astype(jnp.float32)
    )


def routing_tables(expert_ids, route_weight, device):
    packed = jnp.concatenate([expert_ids.astype(jnp.float32), route_weight], axis=1)
    packed = lax.all_gather(packed.T, "tok")
    count = expert_ids.shape[1]
    slices = packed.reshape(-1, 2 * count, BLOCK // ROWS, ROWS).transpose(0, 2, 1, 3)
    slices = slices.reshape(-1, 2 * count, ROWS)
    order = lax.dynamic_index_in_dim(jnp.asarray(slice_order()), device, 0, keepdims=False)
    listed = slices[order.reshape(-1)].reshape(2, 16, 2 * count, ROWS)
    local = (2 * device + lax.iota(jnp.int32, 2)).astype(jnp.float32)
    match = listed[:, None, :, :count] == local[None, :, None, None, None]
    hit = jnp.any(match, axis=3).reshape(2, 2, GROUP_ROWS)
    weight = jnp.sum(jnp.where(match, listed[:, None, :, count:], 0.0), axis=3)
    weight = weight.reshape(2, 2, GROUP_ROWS)
    ones = hit.astype(jnp.int32)
    slot = jnp.where(hit, jnp.cumsum(ones, axis=2) - 1, -1)
    return [(slot[group], weight[group], slot[group].T) for group in range(2)]


def block_pairs(target):
    pairs = []
    for z in range(NZ):
        for x in range(2):
            aim = target(z, x)
            if aim is not None and aim[0] < NZ:
                pairs.append((z * 2 + x, aim[0] * 2 + aim[1]))
    return pairs


def sliced_body(
    residual_in,
    queries,
    keys,
    values,
    segment_ids,
    out_proj,
    norm_gain,
    shared_gate,
    shared_up,
    shared_down,
    expert_gate,
    expert_up,
    expert_down,
    expert_ids,
    route_weight,
    block_table,
):
    tok_here = lax.axis_index("tok")
    hd_here = lax.axis_index("hd")
    place = jnp.stack([tok_here, hd_here]).astype(jnp.int32)
    page_count = BLOCK // PAGE
    own, kv_pages = write_pages(keys, values, block_table - tok_here * page_count)

    def move(array, target):
        return lax.ppermute(array, "tok", block_pairs(target))

    near_z = move(own, lambda z, x: (z + 1, x))
    near_x = move(own, lambda z, x: (z, 1) if x == 0 else None)
    cross = move(near_z, lambda z, x: (z, 1 - x))
    far = move(near_z, lambda z, x: (z + 1, x))
    far_cross = move(far, lambda z, x: (z, 0) if x == 1 else None)

    tables = routing_tables(expert_ids, route_weight, tok_here * 4 + hd_here)
    query_segment = lax.dynamic_slice_in_dim(segment_ids, tok_here * BLOCK, BLOCK, 0)[:, None]
    sent, kept = attention(
        place, segment_ids, query_segment, queries, own, near_x, near_z, cross, far, far_cross, out_proj
    )
    kept = kept + send(sent, CORE_SWAP).astype(jnp.float32)
    resid_rows = (
        lax.dynamic_slice_in_dim(residual_in, hd_here * ROWS, ROWS, 0).astype(jnp.float32)
        + kept[:ROWS]
        + send(kept[ROWS:].astype(jnp.bfloat16), Y_SWAP).astype(jnp.float32)
    )
    normed = rms_normed(resid_rows, norm_gain)

    steps = [normed]
    for _ in range(3):
        steps.append(send(steps[-1], Z_ON))
    weights = (expert_gate, expert_up, expert_down)
    shared = (shared_gate, shared_up, shared_down)
    sums = []
    for group in range(2):
        gathered = gather_plane(jnp.concatenate(steps[2 * group : 2 * group + 2], axis=0))
        terms = experts(place, tables[group], gathered, weights, shared if group == 0 else None)
        sums.append(sum_plane(*terms))
    returned = [
        send(part.astype(jnp.bfloat16), pairs).astype(jnp.float32)
        for part, pairs in ((sums[0][ROWS:], Z_BACK), (sums[1][:ROWS], Z_TWO), (sums[1][ROWS:], Z_ON))
    ]
    output = resid_rows + sums[0][:ROWS] + returned[0] + returned[1] + returned[2]
    return (output.astype(jnp.bfloat16), kv_pages)


def solution(mesh):
    placed = (
        P("tok", None),
        P("tok", "hd"),
        P("tok", "hd"),
        P("tok", "hd"),
        P(),
        P("hd", None),
        P(),
        P(None, "hd"),
        P(None, "hd"),
        P("hd", None),
        P(None, ("tok", "hd")),
        P(None, ("tok", "hd")),
        P(("tok", "hd"), None),
        P("tok", None),
        P("tok", None),
        P("tok"),
    )
    return jax.shard_map(
        sliced_body if dict(mesh.shape) == {"tok": 2 * NZ, "hd": 4} else general_body,
        mesh=mesh,
        in_specs=placed,
        out_specs=(P(("tok", "hd"), None), P("tok", None, "hd")),
        check_vma=False,
    )
```

```python
import math

import jax
import jax.numpy as jnp
import numpy as np
from jax import lax
from jax.experimental import pallas as pl
from jax.experimental.pallas import tpu as pltpu
from jax.sharding import PartitionSpec as P

HD = 128
EXPERTS = 64
FF_E = 1408
PAGE = 16
CAP = 48


MASKED_SCORE = -1e30
NORM_EPSILON = 1e-06


def from_behind(array, axis, by):
    length = lax.axis_size(axis)
    pairs = [(i, i + by) for i in range(length) if 0 <= i + by < length]
    return lax.ppermute(array, axis, pairs)


def rms_normed(resid_state, norm_gain):
    mean_square = jnp.mean(resid_state * resid_state, axis=1, keepdims=True)
    return (resid_state * lax.rsqrt(mean_square + NORM_EPSILON) * norm_gain).astype(jnp.bfloat16)


def general_body(
    residual_in,
    queries,
    keys,
    values,
    segment_ids,
    out_proj,
    norm_gain,
    shared_gate,
    shared_up,
    shared_down,
    expert_gate,
    expert_up,
    expert_down,
    expert_ids,
    route_weight,
    block_table,
):
    block_len = residual_in.shape[0]
    model_width = residual_in.shape[1]
    tok_count = lax.axis_size("tok")
    hd_count = lax.axis_size("hd")
    tok_here = lax.axis_index("tok")
    hd_here = lax.axis_index("hd")
    heads_here = queries.shape[1] // HD
    query_three = queries.reshape(block_len, heads_here, HD)
    offsets = lax.iota(jnp.int32, block_len)
    query_pos = tok_here * block_len + offsets
    query_seg = lax.dynamic_slice_in_dim(segment_ids, tok_here * block_len, block_len, 0)

    def attend(carried, key_blk, value_blk, source):
        safe_source = jnp.maximum(source, 0)
        key_seg = lax.dynamic_slice_in_dim(segment_ids, safe_source * block_len, block_len, 0)
        key_pos = source * block_len + offsets

        def compute(current):
            running_max, denom_sum, weighted_sum = current
            scores = jnp.einsum(
                "qhd,khd->hqk",
                query_three,
                key_blk.reshape(block_len, heads_here, HD),
                preferred_element_type=jnp.float32,
            ) / math.sqrt(HD)
            allowed = (key_seg[None, :] == query_seg[:, None]) & (
                key_pos[None, :] <= query_pos[:, None]
            )
            scores = jnp.where(allowed[None], scores, MASKED_SCORE)
            new_max = jnp.maximum(running_max, jnp.max(scores, axis=2))
            shrink = jnp.exp(running_max - new_max)
            exp_scores = jnp.where(allowed[None], jnp.exp(scores - new_max[:, :, None]), 0.0)
            denom_sum = denom_sum * shrink + jnp.sum(exp_scores, axis=2)
            update = jnp.einsum(
                "hqk,khd->qhd",
                exp_scores.astype(jnp.bfloat16),
                value_blk.reshape(block_len, heads_here, HD),
                preferred_element_type=jnp.float32,
            )
            weighted_sum = weighted_sum * jnp.transpose(shrink)[:, :, None] + update
            return (new_max, denom_sum, weighted_sum)

        is_live = (source >= 0) & (
            segment_ids[safe_source * block_len + block_len - 1] >= query_seg[0]
        )
        return lax.cond(is_live, compute, lambda unchanged: unchanged, carried)

    initial = (
        jnp.full((heads_here, block_len), MASKED_SCORE, jnp.float32),
        jnp.zeros((heads_here, block_len), jnp.float32),
        jnp.zeros((block_len, heads_here, HD), jnp.float32),
    )
    carried = attend(initial, keys, values, tok_here)

    def relay(relay_step, loop_carry):
        moving, inner_state = loop_carry
        moving = from_behind(moving, "tok", 1)
        inner_state = attend(inner_state, moving[0], moving[1], tok_here - relay_step - 1)
        return (moving, inner_state)

    _, final_state = lax.fori_loop(0, tok_count // 2, relay, (jnp.stack([keys, values]), carried))
    weighted_sum = final_state[2]
    denom_sum = final_state[1]
    attended = (
        (weighted_sum / jnp.transpose(denom_sum)[:, :, None])
        .astype(jnp.bfloat16)
        .reshape(block_len, heads_here * HD)
    )
    row_count = block_len // hd_count
    row_start = hd_here * row_count
    head_terms = jnp.dot(attended, out_proj, preferred_element_type=jnp.float32)
    resid_full = residual_in.astype(jnp.float32) + lax.psum(
        head_terms.astype(jnp.bfloat16), "hd"
    ).astype(jnp.float32)
    normed = rms_normed(resid_full, norm_gain)
    resid_rows = lax.dynamic_slice_in_dim(resid_full, row_start, row_count, 0)
    shared_gate_val = jnp.dot(normed, shared_gate, preferred_element_type=jnp.float32)
    shared_up_val = jnp.dot(normed, shared_up, preferred_element_type=jnp.float32)
    shared_hidden = (jax.nn.silu(shared_gate_val) * shared_up_val).astype(jnp.bfloat16)
    partial_out = jnp.dot(shared_hidden, shared_down, preferred_element_type=jnp.float32)
    slice_width = expert_gate.shape[1]
    held_count = max(1, slice_width // FF_E)
    part_width = slice_width // held_count
    per_group = slice_width * hd_count // FF_E
    first_local = hd_here * slice_width // FF_E
    expert_range = lax.iota(jnp.int32, EXPERTS)
    onehot = jnp.sum(
        (expert_ids[:, :, None] == expert_range[None, None, :]).astype(jnp.int32), axis=1
    )
    earlier = jnp.cumsum(onehot, axis=0) - onehot
    slot_index = jnp.take_along_axis(earlier, expert_ids, axis=1)
    flat_expert = expert_ids.reshape(-1)
    flat_slot = slot_index.reshape(-1)
    row_source = jnp.repeat(offsets, expert_ids.shape[1])
    row_table = (
        jnp.full((EXPERTS, CAP), block_len, jnp.int32).at[flat_expert, flat_slot].set(row_source)
    )
    weight_table = (
        jnp.zeros((EXPERTS, CAP), jnp.float32)
        .at[flat_expert, flat_slot]
        .set(route_weight.reshape(-1))
    )
    send_rows = lax.dynamic_slice_in_dim(
        row_table.reshape(tok_count, per_group, CAP), first_local, held_count, 1
    )
    send_weight = lax.dynamic_slice_in_dim(
        weight_table.reshape(tok_count, per_group, CAP), first_local, held_count, 1
    )
    padded_rows = jnp.concatenate([normed, jnp.zeros((1, model_width), jnp.bfloat16)], axis=0)
    outgoing = padded_rows[send_rows]
    gate_three = expert_gate.reshape(model_width, held_count, part_width)
    up_three = expert_up.reshape(model_width, held_count, part_width)
    down_three = expert_down.reshape(held_count, part_width, model_width)
    incoming = lax.all_to_all(outgoing, "tok", split_axis=0, concat_axis=0, tiled=True)
    gate_val = jnp.einsum(
        "secd,def->secf", incoming, gate_three, preferred_element_type=jnp.float32
    )
    up_val = jnp.einsum("secd,def->secf", incoming, up_three, preferred_element_type=jnp.float32)
    hidden = (jax.nn.silu(gate_val) * up_val).astype(jnp.bfloat16)
    result = jnp.einsum(
        "secf,efd->secd", hidden, down_three, preferred_element_type=jnp.float32
    ).astype(jnp.bfloat16)
    returned_rows = lax.all_to_all(result, "tok", split_axis=0, concat_axis=0, tiled=True)
    weighted_rows = returned_rows.astype(jnp.float32) * send_weight[:, :, :, None]
    routed = (
        jnp.zeros((block_len + 1, model_width), jnp.float32)
        .at[send_rows.reshape(-1)]
        .add(weighted_rows.reshape(-1, model_width))[:block_len]
    )
    summed_rows = lax.psum_scatter(
        (partial_out + routed).astype(jnp.bfloat16), "hd", scatter_dimension=0, tiled=True
    ).astype(jnp.float32)
    output = (resid_rows + summed_rows).astype(jnp.bfloat16)
    page_count = block_len // PAGE
    page_data = jnp.stack(
        [keys.reshape(block_len, heads_here, HD), values.reshape(block_len, heads_here, HD)], axis=2
    )
    page_data = page_data.reshape(page_count, PAGE, heads_here * 2 * HD)
    local_pages = block_table - tok_here * page_count
    kv_pages = jnp.zeros_like(page_data).at[local_pages].set(page_data)
    return (output, kv_pages)


NZ = 4
BOTH = ("tok", "hd")
ROWS = 64
BLOCK = 256
GROUP_ROWS = 1024
SLOTS = 4 * CAP
NEXT_Z = {0: 1, 1: 3, 3: 2, 2: 0}
BACK_Z = {after: before for before, after in NEXT_Z.items()}
DEVICES = [(z, x, y, c) for z in range(NZ) for x in range(2) for y in range(2) for c in range(2)]


def flat_index(z, x, y, c):
    return (z * 2 + x) * 4 + y * 2 + c


def pairs_of(target):
    return [(flat_index(*device), flat_index(*target(*device))) for device in DEVICES]


Z_ON = pairs_of(lambda z, x, y, c: (NEXT_Z[z], x, y, c))
Z_BACK = pairs_of(lambda z, x, y, c: (BACK_Z[z], x, y, c))
Z_TWO = pairs_of(lambda z, x, y, c: (NEXT_Z[NEXT_Z[z]], x, y, c))
CORE_SWAP = pairs_of(lambda z, x, y, c: (z, x, y, 1 - c))
X_SWAP = pairs_of(lambda z, x, y, c: (z, 1 - x, y, c))
Y_SWAP = pairs_of(lambda z, x, y, c: (z, x, 1 - y, c))
X_THEN_Y = pairs_of(lambda z, x, y, c: (z, 1 - x, y, c) if c == 0 else (z, x, 1 - y, c))
Y_THEN_X = pairs_of(lambda z, x, y, c: (z, x, 1 - y, c) if c == 0 else (z, 1 - x, y, c))


def slice_order():
    order = np.zeros((4, 2, 16), np.int32)
    for y in range(2):
        for c in range(2):
            mine = {
                0: [(1, y, 0), (1, y, 1), (1, 1 - y, 0)],
                1: [(0, 1 - y, 1), (0, 1 - y, 0), (1, 1 - y, 1)],
            }
            places = [(0, y, c), (0, y, 1 - c)] + mine[c] + mine[1 - c]
            for group in range(2):
                order[y * 2 + c, group] = [
                    ((2 * group + part) * 2 + other) * 4 + at_y * 2 + at_c
                    for other, at_y, at_c in places
                    for part in range(2)
                ]
    return order


def send(array, pairs):
    return lax.ppermute(array, BOTH, pairs)


def added(first, second):
    return (first.astype(jnp.float32) + second.astype(jnp.float32)).astype(jnp.bfloat16)


def whole(space=pltpu.VMEM):
    return pl.BlockSpec(memory_space=space)


def pages_kernel(table, keys, values, joined, pages):
    heads = keys.shape[1] // HD
    for head in range(heads):
        lanes = slice(head * HD, (head + 1) * HD)
        joined[:, 2 * head * HD : (2 * head + 1) * HD] = keys[:, lanes]
        joined[:, (2 * head + 1) * HD : (2 * head + 2) * HD] = values[:, lanes]
    for page in range(keys.shape[0] // PAGE):
        pages[table[page]] = joined[page * PAGE : (page + 1) * PAGE, :]


def write_pages(keys, values, local_pages):
    rows, width = keys.shape
    return pl.pallas_call(
        pages_kernel,
        out_shape=(
            jax.ShapeDtypeStruct((rows, 2 * width), keys.dtype),
            jax.ShapeDtypeStruct((rows // PAGE, PAGE, 2 * width), keys.dtype),
        ),
        in_specs=[whole(pltpu.SMEM), whole(), whole()],
        out_specs=(whole(), whole()),
    )(local_pages, keys, values)


HEADS_HERE = 4


def attend_block(segments, query_segment, queries, block, source, diagonal, top, total, mixed):
    allowed = segments[pl.ds(source, 1), :] == query_segment[...]
    if diagonal:
        rows = lax.broadcasted_iota(jnp.int32, (BLOCK, BLOCK), 0)
        columns = lax.broadcasted_iota(jnp.int32, (BLOCK, BLOCK), 1)
        allowed = allowed & (columns <= rows)
    for head in range(HEADS_HERE):
        lane = slice(head, head + 1)
        key = block[:, 2 * head * HD : (2 * head + 1) * HD]
        value = block[:, (2 * head + 1) * HD : (2 * head + 2) * HD]
        scores = lax.dot_general(
            queries[:, head * HD : (head + 1) * HD],
            key,
            (((1,), (1,)), ((), ())),
            preferred_element_type=jnp.float32,
        ) * (1.0 / math.sqrt(HD))
        scores = jnp.where(allowed, scores, MASKED_SCORE)
        largest = jnp.max(scores, axis=1, keepdims=True)
        if not diagonal:
            before = top[:, lane]
            largest = jnp.maximum(largest, before)
        exp_scores = jnp.exp(scores - largest)
        update = jnp.dot(exp_scores.astype(jnp.bfloat16), value, preferred_element_type=jnp.float32)
        added_up = jnp.sum(exp_scores, axis=1, keepdims=True)
        if not diagonal:
            shrink = jnp.exp(before - largest)
            added_up += total[:, lane] * shrink
            update += mixed[head] * shrink
        top[:, lane] = largest
        total[:, lane] = added_up
        mixed[head] = update


def attend_earlier(place, segment_list, segments, query_segment, queries, blocks, top, total, mixed):
    for block, source in blocks:
        safe = jnp.maximum(source, 0)
        live = (source >= 0) & (
            segment_list[safe * BLOCK + BLOCK - 1] == segment_list[place[0] * BLOCK]
        )

        @pl.when(live)
        def _():
            attend_block(
                segments, query_segment, queries, block, safe, False, top, total, mixed
            )


def attention_first(
    place, segment_list, segments, query_segment, queries, own, near_x, near_z, top, total, mixed
):
    here = place[0]
    top[...] = jnp.zeros_like(top)
    total[...] = jnp.ones_like(total)
    attend_block(segments, query_segment, queries, own, here, True, top, total, mixed)
    odd = here % 2
    blocks = [(near_x, jnp.where(odd == 1, here - 1, -1)), (near_z, here - 2)]
    attend_earlier(
        place, segment_list, segments, query_segment, queries, blocks, top, total, mixed
    )


def attention_second(
    place, segment_list, segments, query_segment, queries, cross, far, far_cross, projection,
    top_in, total_in, mixed_in, after, sent, kept, top, total, mixed, attended,
):
    here, hd = place[0], place[1]
    odd = here % 2
    top[...] = top_in[...]
    total[...] = total_in[...]
    mixed[...] = mixed_in[...]
    blocks = [
        (cross, jnp.where(odd == 1, here - 3, here - 1)),
        (far, here - 4),
        (far_cross, jnp.where(odd == 1, -1, here - 3)),
    ]
    attend_earlier(
        place, segment_list, segments, query_segment, queries, blocks, top, total, mixed
    )
    for head in range(HEADS_HERE):
        attended[:, head * HD : (head + 1) * HD] = (
            mixed[head] / total[:, head : head + 1]
        ).astype(jnp.bfloat16)
    mate, across = hd ^ 1, hd ^ 2

    def rows_of(first, second):
        return jnp.concatenate(
            [
                attended[pl.ds(pl.multiple_of(quarter * ROWS, ROWS), ROWS), :]
                for quarter in (first, second)
            ],
            axis=0,
        )

    sent[...] = jnp.dot(
        rows_of(mate, mate ^ 2), projection[...], preferred_element_type=jnp.float32
    ).astype(jnp.bfloat16)
    kept[...] = jnp.dot(rows_of(hd, across), projection[...], preferred_element_type=jnp.float32)


def attention(
    place, segment_ids, query_segment, queries, own, near_x, near_z, cross, far, far_cross, out_proj, after
):
    segments = segment_ids.reshape(-1, BLOCK)
    state = (
        jax.ShapeDtypeStruct((BLOCK, HD), jnp.float32),
        jax.ShapeDtypeStruct((BLOCK, HD), jnp.float32),
        jax.ShapeDtypeStruct((HEADS_HERE, BLOCK, HD), jnp.float32),
    )
    smem, vmem, anywhere = whole(pltpu.SMEM), whole(), whole(pl.ANY)
    limit = pltpu.CompilerParams(vmem_limit_bytes=16 * 2**20)
    first = pl.pallas_call(
        attention_first,
        out_shape=state,
        in_specs=[smem, smem] + [vmem] * 6,
        out_specs=(vmem, vmem, vmem),
        compiler_params=limit,
        cost_estimate=pl.CostEstimate(flops=6 * 10**8, bytes_accessed=4 * 10**6, transcendentals=6 * 10**5),
    )(place, segment_ids, segments, query_segment, queries, own, near_x, near_z)
    return pl.pallas_call(
        attention_second,
        out_shape=(
            jax.ShapeDtypeStruct((2 * ROWS, out_proj.shape[1]), jnp.bfloat16),
            jax.ShapeDtypeStruct((2 * ROWS, out_proj.shape[1]), jnp.float32),
        ),
        in_specs=[smem, smem] + [vmem] * 10 + [anywhere],
        out_specs=(vmem, vmem),
        scratch_shapes=[pltpu.VMEM(array.shape, jnp.float32) for array in state]
        + [pltpu.VMEM((BLOCK, HEADS_HERE * HD), jnp.bfloat16)],
        compiler_params=limit,
    )(
        place, segment_ids, segments, query_segment, queries, cross, far, far_cross, out_proj, *first,
        after,
    )


CHUNK = 256
WIDE = 512
PIECE = 2 * ROWS
PIECES = 8


def silu_times(gate_val, up_val):
    return (gate_val / (1.0 + jnp.exp(-gate_val)) * up_val).astype(jnp.bfloat16)


def experts_kernel(with_shared, *refs):
    place, slot_row, weight_row, slot_column = refs[:4]
    pieces, refs = refs[4 : 4 + PIECES], refs[4 + PIECES :]
    gate, up, down = refs[:3]
    refs = refs[3:]
    if with_shared:
        shared, refs = refs[:3], refs[3:]
    targets, refs = refs[:PIECES], refs[PIECES:]
    rows, picked, hidden, spread, arrived, gate_held, up_held, down_held, gate_up_arrived, down_arrived = refs[:10]
    width = rows.shape[1]
    steps = range(0, FF_E, CHUNK)
    wide_steps = range(0, width, WIDE)

    def unit_lanes(expert, low):
        return pl.ds(expert * FF_E + low, min(CHUNK, FF_E - low))

    def gate_up_copies(expert, low):
        lanes = unit_lanes(expert, low)
        return [
            pltpu.make_async_copy(
                source.at[:, lanes], held.at[:, lanes], gate_up_arrived.at[expert, low // CHUNK, number]
            )
            for number, (source, held) in enumerate(((gate, gate_held), (up, up_held)))
        ]

    def down_copy(expert, low):
        place_of = (pl.ds(expert * FF_E, FF_E), pl.ds(low, WIDE))
        return pltpu.make_async_copy(
            down.at[place_of], down_held.at[place_of], down_arrived.at[expert, low // WIDE]
        )

    copies = [
        pltpu.make_async_copy(piece, rows.at[pl.ds(number * PIECE, PIECE), :], arrived.at[number])
        for number, piece in enumerate(pieces)
    ]
    for copy in copies:
        copy.start()
    for expert in range(2):
        for low in steps:
            for copy in gate_up_copies(expert, low):
                copy.start()
        for low in wide_steps:
            down_copy(expert, low).start()
    if with_shared:
        s_down, s_arrived, s_rows, s_hidden = refs[10:]
        units = s_down.shape[0]
        s_gate, s_up = down_held.at[pl.ds(0, units), :], down_held.at[pl.ds(units, units), :]
        s_copies = [
            pltpu.make_async_copy(source, target, s_arrived.at[number])
            for number, (source, target) in enumerate(zip(shared, (s_gate, s_up, s_down)))
        ]
        s_copies[2].start()

    slot_numbers = lax.broadcasted_iota(jnp.int32, (SLOTS, GROUP_ROWS), 0)
    slot_weight, picks = [], []
    for expert in range(2):
        hit = slot_row[expert : expert + 1, :] == slot_numbers
        slot_weight.append(
            jnp.sum(jnp.where(hit, weight_row[expert : expert + 1, :], 0.0), axis=1, keepdims=True)
        )
        picks.append(jnp.where(hit, 1.0, 0.0).astype(jnp.bfloat16))
    pick = jnp.concatenate(picks, axis=0)
    slot_lanes = lax.broadcasted_iota(jnp.int32, (GROUP_ROWS, 2 * SLOTS), 1)
    first, second = slot_column[:, 0:1], slot_column[:, 1:2]
    hit = (first == slot_lanes) | ((second >= 0) & (second + SLOTS == slot_lanes))
    spread[...] = jnp.where(hit, 1.0, 0.0).astype(jnp.bfloat16)

    for copy in copies:
        copy.wait()
    for low in range(0, width, WIDE):
        lanes = slice(low, low + WIDE)
        picked[:, lanes] = jnp.dot(pick, rows[:, lanes], preferred_element_type=jnp.float32).astype(
            jnp.bfloat16
        )
    for expert in range(2):
        held = slice(expert * SLOTS, (expert + 1) * SLOTS)
        for low in steps:
            for copy in gate_up_copies(expert, low):
                copy.wait()
            lanes = unit_lanes(expert, low)
            gate_val = jnp.dot(picked[held], gate_held[:, lanes], preferred_element_type=jnp.float32)
            up_val = jnp.dot(picked[held], up_held[:, lanes], preferred_element_type=jnp.float32)
            hidden[:, low : low + lanes.size] = silu_times(gate_val, up_val)
        for low in wide_steps:
            down_copy(expert, low).wait()
            lanes = slice(low, low + WIDE)
            result = jnp.dot(
                hidden[...],
                down_held[expert * FF_E : (expert + 1) * FF_E, lanes],
                preferred_element_type=jnp.float32,
            )
            picked[held, lanes] = (result * slot_weight[expert]).astype(jnp.bfloat16)
        if with_shared and expert == 0:
            for copy in s_copies[:2]:
                copy.start()

    if with_shared:
        upper = place[1] % 2 == 1
        s_rows[0:ROWS] = rows[0:ROWS]
        s_rows[ROWS : 2 * ROWS] = rows[PIECE : PIECE + ROWS]
        base = pl.multiple_of(jnp.where(upper, 2, 5) * PIECE, PIECE)
        s_rows[2 * ROWS : 3 * ROWS] = rows[pl.ds(base, ROWS), :]
        s_rows[3 * ROWS : 4 * ROWS] = rows[pl.ds(base + PIECE, ROWS), :]
        for copy in s_copies:
            copy.wait()
        turned = (((1,), (1,)), ((), ()))
        for low in range(0, units, CHUNK):
            size = min(CHUNK, units - low)
            gate_val, up_val = [
                lax.dot_general(
                    s_rows[...],
                    down_held[start + low : start + low + size, :],
                    turned,
                    preferred_element_type=jnp.float32,
                )
                for start in (0, units)
            ]
            s_hidden[:, low : low + size] = silu_times(gate_val, up_val)

    for low in range(0, width, CHUNK):
        lanes = slice(low, low + CHUNK)
        value = jnp.dot(spread[...], picked[:, lanes], preferred_element_type=jnp.float32)
        if with_shared:
            s_result = jnp.dot(s_hidden[...], s_down[:, lanes], preferred_element_type=jnp.float32)
        for part, target in enumerate(targets):
            mine = value[part * PIECE : (part + 1) * PIECE]
            if with_shared and part in (0, 1, 2, 3, 5, 6):
                if part < 2:
                    term = s_result[part * ROWS : (part + 1) * ROWS]
                else:
                    start = (2 + (part - 2) % 3) * ROWS
                    here = upper if part < 4 else jnp.logical_not(upper)
                    term = jnp.where(here, s_result[start : start + ROWS], 0.0)
                target[:ROWS, lanes] = (mine[:ROWS] + term).astype(jnp.bfloat16)
                target[ROWS:, lanes] = mine[ROWS:].astype(jnp.bfloat16)
            else:
                target[:, lanes] = mine.astype(jnp.bfloat16)


def experts(place, tables, pieces, weights, shared):
    width = pieces[0].shape[1]
    hbm, vmem = whole(pl.ANY), whole()
    scratch = [
        pltpu.VMEM((GROUP_ROWS, width), jnp.bfloat16),
        pltpu.VMEM((2 * SLOTS, width), jnp.bfloat16),
        pltpu.VMEM((SLOTS, FF_E), jnp.bfloat16),
        pltpu.VMEM((GROUP_ROWS, 2 * SLOTS), jnp.bfloat16),
        pltpu.SemaphoreType.DMA((PIECES,)),
        *[pltpu.VMEM(array.shape, array.dtype) for array in weights],
        pltpu.SemaphoreType.DMA((2, pl.cdiv(FF_E, CHUNK), 2)),
        pltpu.SemaphoreType.DMA((2, width // WIDE)),
    ]
    operands = [place, *tables, *pieces, *weights]
    if shared is not None:
        operands += list(shared)
        scratch += [
            pltpu.VMEM(shared[2].shape, shared[2].dtype),
            pltpu.SemaphoreType.DMA((3,)),
            pltpu.VMEM((BLOCK, width), jnp.bfloat16),
            pltpu.VMEM((BLOCK, shared[2].shape[0]), jnp.bfloat16),
        ]
    in_specs = [whole(pltpu.SMEM)] + [vmem] * 3
    in_specs += [hbm] * (len(operands) - len(in_specs))
    return pl.pallas_call(
        lambda *refs: experts_kernel(shared is not None, *refs),
        out_shape=(jax.ShapeDtypeStruct((PIECE, width), jnp.bfloat16),) * PIECES,
        in_specs=in_specs,
        out_specs=(vmem,) * PIECES,
        scratch_shapes=scratch,
        compiler_params=pltpu.CompilerParams(vmem_limit_bytes=58 * 2**20),
        cost_estimate=pl.CostEstimate(
            flops=10**10, bytes_accessed=44 * 10**6, transcendentals=10**6
        ),
    )(*operands)


def gather_plane(rows):
    mate = send(rows, CORE_SWAP)
    near = send(rows, X_THEN_Y)
    near_mate = send(mate, X_THEN_Y)
    corner = send(near, Y_THEN_X)
    fetched = (near, near_mate, corner)
    return (rows, mate, *fetched, *[send(piece, CORE_SWAP) for piece in fetched])


def sum_plane(own, mate, near, near_mate, corner, mate_near, mate_near_mate, mate_corner):
    corner = added(corner, send(mate_corner, CORE_SWAP))
    from_corner = send(corner, Y_THEN_X)
    near_mate = added(near_mate, send(mate_near_mate, CORE_SWAP))
    from_near_mate = send(near_mate, X_THEN_Y)
    near = near.astype(jnp.float32) + send(mate_near, CORE_SWAP).astype(jnp.float32)
    from_near = send(added(near, from_corner), X_THEN_Y)
    return (
        own.astype(jnp.float32)
        + send(mate, CORE_SWAP).astype(jnp.float32)
        + send(from_near_mate, CORE_SWAP).astype(jnp.float32)
        + from_near.astype(jnp.float32)
    )


def routing_tables(expert_ids, route_weight, place):
    count = expert_ids.shape[1]
    packed = jnp.concatenate([expert_ids.T.astype(jnp.float32), route_weight.T], axis=0)
    pair = jnp.stack([packed, send(packed, X_SWAP)])
    steps = [pair]
    for _ in range(3):
        steps.append(send(steps[-1], Z_ON))
    slices = jnp.stack(steps).reshape(NZ, 2, 2 * count, 4, ROWS).transpose(0, 1, 3, 2, 4)
    slices = slices.reshape(-1, 2 * count, ROWS)
    order = lax.dynamic_index_in_dim(jnp.asarray(slice_order()), place[1], 0, keepdims=False)
    listed = slices[order.reshape(-1)].reshape(2, 16, 2 * count, ROWS)
    first_expert = 2 * (place[0] * 4 + place[1])
    local = (first_expert + lax.iota(jnp.int32, 2)).astype(jnp.float32)
    match = listed[:, None, :, :count] == local[None, :, None, None, None]
    hit = jnp.any(match, axis=3).reshape(2, 2, GROUP_ROWS)
    weight = jnp.sum(jnp.where(match, listed[:, None, :, count:], 0.0), axis=3)
    weight = weight.reshape(2, 2, GROUP_ROWS)
    ones = hit.astype(jnp.int32)
    slot = jnp.where(hit, jnp.cumsum(ones, axis=2) - 1, -1)
    return [(slot[group], weight[group], slot[group].T) for group in range(2)]


def block_pairs(target):
    pairs = []
    for z in range(NZ):
        for x in range(2):
            aim = target(z, x)
            if aim is not None and aim[0] < NZ:
                pairs.append((z * 2 + x, aim[0] * 2 + aim[1]))
    return pairs


def sliced_body(
    residual_in,
    queries,
    keys,
    values,
    segment_ids,
    out_proj,
    norm_gain,
    shared_gate,
    shared_up,
    shared_down,
    expert_gate,
    expert_up,
    expert_down,
    expert_ids,
    route_weight,
    block_table,
):
    tok_here = lax.axis_index("tok")
    hd_here = lax.axis_index("hd")
    place = jnp.stack([tok_here, hd_here]).astype(jnp.int32)
    page_count = BLOCK // PAGE
    own, kv_pages = write_pages(keys, values, block_table - tok_here * page_count)

    def move(array, target):
        return lax.ppermute(array, "tok", block_pairs(target))

    near_z = move(own, lambda z, x: (z + 1, x))
    near_x = move(own, lambda z, x: (z, 1) if x == 0 else None)
    cross = move(near_z, lambda z, x: (z, 1 - x))
    far = move(near_z, lambda z, x: (z + 1, x))
    far_cross = move(near_z, lambda z, x: (z + 1, 0) if x == 1 else None)

    tables = routing_tables(expert_ids, route_weight, place)
    query_segment = lax.dynamic_slice_in_dim(segment_ids, tok_here * BLOCK, BLOCK, 0)[:, None]
    sent, kept = attention(
        place, segment_ids, query_segment, queries, own, near_x, near_z, cross, far, far_cross, out_proj,
        tables[0][0],
    )
    kept = kept + send(sent, CORE_SWAP).astype(jnp.float32)
    resid_rows = (
        lax.dynamic_slice_in_dim(residual_in, hd_here * ROWS, ROWS, 0).astype(jnp.float32)
        + kept[:ROWS]
        + send(kept[ROWS:].astype(jnp.bfloat16), Y_SWAP).astype(jnp.float32)
    )
    normed = rms_normed(resid_rows, norm_gain)

    steps = [normed]
    for _ in range(3):
        steps.append(send(steps[-1], Z_ON))
    weights = (expert_gate, expert_up, expert_down)
    shared = (shared_gate.T, shared_up.T, shared_down)
    sums = []
    for group in range(2):
        gathered = gather_plane(jnp.concatenate(steps[2 * group : 2 * group + 2], axis=0))
        terms = experts(place, tables[group], gathered, weights, shared if group == 0 else None)
        sums.append(sum_plane(*terms))
    returned = [
        send(part.astype(jnp.bfloat16), pairs).astype(jnp.float32)
        for part, pairs in ((sums[0][ROWS:], Z_BACK), (sums[1][:ROWS], Z_TWO), (sums[1][ROWS:], Z_ON))
    ]
    output = resid_rows + sums[0][:ROWS] + returned[0] + returned[1] + returned[2]
    return (output.astype(jnp.bfloat16), kv_pages)


def solution(mesh):
    placed = (
        P("tok", None),
        P("tok", "hd"),
        P("tok", "hd"),
        P("tok", "hd"),
        P(),
        P("hd", None),
        P(),
        P(None, "hd"),
        P(None, "hd"),
        P("hd", None),
        P(None, ("tok", "hd")),
        P(None, ("tok", "hd")),
        P(("tok", "hd"), None),
        P("tok", None),
        P("tok", None),
        P("tok"),
    )
    return jax.shard_map(
        sliced_body if dict(mesh.shape) == {"tok": 2 * NZ, "hd": 4} else general_body,
        mesh=mesh,
        in_specs=placed,
        out_specs=(P(("tok", "hd"), None), P("tok", None, "hd")),
        check_vma=False,
    )
```

```python
import math

import jax
import jax.numpy as jnp
import numpy as np
from jax import lax
from jax.experimental import pallas as pl
from jax.experimental.pallas import tpu as pltpu
from jax.sharding import PartitionSpec as P

HD = 128
EXPERTS = 64
FF_E = 1408
PAGE = 16
CAP = 48


MASKED_SCORE = -1e30
NORM_EPSILON = 1e-06


def from_behind(array, axis, by):
    length = lax.axis_size(axis)
    pairs = [(i, i + by) for i in range(length) if 0 <= i + by < length]
    return lax.ppermute(array, axis, pairs)


def rms_normed(resid_state, norm_gain):
    mean_square = jnp.mean(resid_state * resid_state, axis=1, keepdims=True)
    return (resid_state * lax.rsqrt(mean_square + NORM_EPSILON) * norm_gain).astype(jnp.bfloat16)


def general_body(
    residual_in,
    queries,
    keys,
    values,
    segment_ids,
    out_proj,
    norm_gain,
    shared_gate,
    shared_up,
    shared_down,
    expert_gate,
    expert_up,
    expert_down,
    expert_ids,
    route_weight,
    block_table,
):
    block_len = residual_in.shape[0]
    model_width = residual_in.shape[1]
    tok_count = lax.axis_size("tok")
    hd_count = lax.axis_size("hd")
    tok_here = lax.axis_index("tok")
    hd_here = lax.axis_index("hd")
    heads_here = queries.shape[1] // HD
    query_three = queries.reshape(block_len, heads_here, HD)
    offsets = lax.iota(jnp.int32, block_len)
    query_pos = tok_here * block_len + offsets
    query_seg = lax.dynamic_slice_in_dim(segment_ids, tok_here * block_len, block_len, 0)

    def attend(carried, key_blk, value_blk, source):
        safe_source = jnp.maximum(source, 0)
        key_seg = lax.dynamic_slice_in_dim(segment_ids, safe_source * block_len, block_len, 0)
        key_pos = source * block_len + offsets

        def compute(current):
            running_max, denom_sum, weighted_sum = current
            scores = jnp.einsum(
                "qhd,khd->hqk",
                query_three,
                key_blk.reshape(block_len, heads_here, HD),
                preferred_element_type=jnp.float32,
            ) / math.sqrt(HD)
            allowed = (key_seg[None, :] == query_seg[:, None]) & (
                key_pos[None, :] <= query_pos[:, None]
            )
            scores = jnp.where(allowed[None], scores, MASKED_SCORE)
            new_max = jnp.maximum(running_max, jnp.max(scores, axis=2))
            shrink = jnp.exp(running_max - new_max)
            exp_scores = jnp.where(allowed[None], jnp.exp(scores - new_max[:, :, None]), 0.0)
            denom_sum = denom_sum * shrink + jnp.sum(exp_scores, axis=2)
            update = jnp.einsum(
                "hqk,khd->qhd",
                exp_scores.astype(jnp.bfloat16),
                value_blk.reshape(block_len, heads_here, HD),
                preferred_element_type=jnp.float32,
            )
            weighted_sum = weighted_sum * jnp.transpose(shrink)[:, :, None] + update
            return (new_max, denom_sum, weighted_sum)

        is_live = (source >= 0) & (
            segment_ids[safe_source * block_len + block_len - 1] >= query_seg[0]
        )
        return lax.cond(is_live, compute, lambda unchanged: unchanged, carried)

    initial = (
        jnp.full((heads_here, block_len), MASKED_SCORE, jnp.float32),
        jnp.zeros((heads_here, block_len), jnp.float32),
        jnp.zeros((block_len, heads_here, HD), jnp.float32),
    )
    carried = attend(initial, keys, values, tok_here)

    def relay(relay_step, loop_carry):
        moving, inner_state = loop_carry
        moving = from_behind(moving, "tok", 1)
        inner_state = attend(inner_state, moving[0], moving[1], tok_here - relay_step - 1)
        return (moving, inner_state)

    _, final_state = lax.fori_loop(0, tok_count // 2, relay, (jnp.stack([keys, values]), carried))
    weighted_sum = final_state[2]
    denom_sum = final_state[1]
    attended = (
        (weighted_sum / jnp.transpose(denom_sum)[:, :, None])
        .astype(jnp.bfloat16)
        .reshape(block_len, heads_here * HD)
    )
    row_count = block_len // hd_count
    row_start = hd_here * row_count
    head_terms = jnp.dot(attended, out_proj, preferred_element_type=jnp.float32)
    resid_full = residual_in.astype(jnp.float32) + lax.psum(
        head_terms.astype(jnp.bfloat16), "hd"
    ).astype(jnp.float32)
    normed = rms_normed(resid_full, norm_gain)
    resid_rows = lax.dynamic_slice_in_dim(resid_full, row_start, row_count, 0)
    shared_gate_val = jnp.dot(normed, shared_gate, preferred_element_type=jnp.float32)
    shared_up_val = jnp.dot(normed, shared_up, preferred_element_type=jnp.float32)
    shared_hidden = (jax.nn.silu(shared_gate_val) * shared_up_val).astype(jnp.bfloat16)
    partial_out = jnp.dot(shared_hidden, shared_down, preferred_element_type=jnp.float32)
    slice_width = expert_gate.shape[1]
    held_count = max(1, slice_width // FF_E)
    part_width = slice_width // held_count
    per_group = slice_width * hd_count // FF_E
    first_local = hd_here * slice_width // FF_E
    expert_range = lax.iota(jnp.int32, EXPERTS)
    onehot = jnp.sum(
        (expert_ids[:, :, None] == expert_range[None, None, :]).astype(jnp.int32), axis=1
    )
    earlier = jnp.cumsum(onehot, axis=0) - onehot
    slot_index = jnp.take_along_axis(earlier, expert_ids, axis=1)
    flat_expert = expert_ids.reshape(-1)
    flat_slot = slot_index.reshape(-1)
    row_source = jnp.repeat(offsets, expert_ids.shape[1])
    row_table = (
        jnp.full((EXPERTS, CAP), block_len, jnp.int32).at[flat_expert, flat_slot].set(row_source)
    )
    weight_table = (
        jnp.zeros((EXPERTS, CAP), jnp.float32)
        .at[flat_expert, flat_slot]
        .set(route_weight.reshape(-1))
    )
    send_rows = lax.dynamic_slice_in_dim(
        row_table.reshape(tok_count, per_group, CAP), first_local, held_count, 1
    )
    send_weight = lax.dynamic_slice_in_dim(
        weight_table.reshape(tok_count, per_group, CAP), first_local, held_count, 1
    )
    padded_rows = jnp.concatenate([normed, jnp.zeros((1, model_width), jnp.bfloat16)], axis=0)
    outgoing = padded_rows[send_rows]
    gate_three = expert_gate.reshape(model_width, held_count, part_width)
    up_three = expert_up.reshape(model_width, held_count, part_width)
    down_three = expert_down.reshape(held_count, part_width, model_width)
    incoming = lax.all_to_all(outgoing, "tok", split_axis=0, concat_axis=0, tiled=True)
    gate_val = jnp.einsum(
        "secd,def->secf", incoming, gate_three, preferred_element_type=jnp.float32
    )
    up_val = jnp.einsum("secd,def->secf", incoming, up_three, preferred_element_type=jnp.float32)
    hidden = (jax.nn.silu(gate_val) * up_val).astype(jnp.bfloat16)
    result = jnp.einsum(
        "secf,efd->secd", hidden, down_three, preferred_element_type=jnp.float32
    ).astype(jnp.bfloat16)
    returned_rows = lax.all_to_all(result, "tok", split_axis=0, concat_axis=0, tiled=True)
    weighted_rows = returned_rows.astype(jnp.float32) * send_weight[:, :, :, None]
    routed = (
        jnp.zeros((block_len + 1, model_width), jnp.float32)
        .at[send_rows.reshape(-1)]
        .add(weighted_rows.reshape(-1, model_width))[:block_len]
    )
    summed_rows = lax.psum_scatter(
        (partial_out + routed).astype(jnp.bfloat16), "hd", scatter_dimension=0, tiled=True
    ).astype(jnp.float32)
    output = (resid_rows + summed_rows).astype(jnp.bfloat16)
    page_count = block_len // PAGE
    page_data = jnp.stack(
        [keys.reshape(block_len, heads_here, HD), values.reshape(block_len, heads_here, HD)], axis=2
    )
    page_data = page_data.reshape(page_count, PAGE, heads_here * 2 * HD)
    local_pages = block_table - tok_here * page_count
    kv_pages = jnp.zeros_like(page_data).at[local_pages].set(page_data)
    return (output, kv_pages)


NZ = 4
BOTH = ("tok", "hd")
ROWS = 64
BLOCK = 256
GROUP_ROWS = 1024
SLOTS = 4 * CAP
NEXT_Z = {0: 1, 1: 3, 3: 2, 2: 0}
BACK_Z = {after: before for before, after in NEXT_Z.items()}
DEVICES = [(z, x, y, c) for z in range(NZ) for x in range(2) for y in range(2) for c in range(2)]


def flat_index(z, x, y, c):
    return (z * 2 + x) * 4 + y * 2 + c


def pairs_of(target):
    return [(flat_index(*device), flat_index(*target(*device))) for device in DEVICES]


Z_ON = pairs_of(lambda z, x, y, c: (NEXT_Z[z], x, y, c))
Z_BACK = pairs_of(lambda z, x, y, c: (BACK_Z[z], x, y, c))
Z_TWO = pairs_of(lambda z, x, y, c: (NEXT_Z[NEXT_Z[z]], x, y, c))
CORE_SWAP = pairs_of(lambda z, x, y, c: (z, x, y, 1 - c))
X_SWAP = pairs_of(lambda z, x, y, c: (z, 1 - x, y, c))
Y_SWAP = pairs_of(lambda z, x, y, c: (z, x, 1 - y, c))
X_THEN_Y = pairs_of(lambda z, x, y, c: (z, 1 - x, y, c) if c == 0 else (z, x, 1 - y, c))
Y_THEN_X = pairs_of(lambda z, x, y, c: (z, x, 1 - y, c) if c == 0 else (z, 1 - x, y, c))


def slice_order():
    order = np.zeros((4, 2, 16), np.int32)
    for y in range(2):
        for c in range(2):
            mine = {
                0: [(1, y, 0), (1, y, 1), (1, 1 - y, 0)],
                1: [(0, 1 - y, 1), (0, 1 - y, 0), (1, 1 - y, 1)],
            }
            places = [(0, y, c), (0, y, 1 - c)] + mine[c] + mine[1 - c]
            for group in range(2):
                order[y * 2 + c, group] = [
                    ((2 * group + part) * 2 + other) * 4 + at_y * 2 + at_c
                    for other, at_y, at_c in places
                    for part in range(2)
                ]
    return order


def send(array, pairs):
    return lax.ppermute(array, BOTH, pairs)


def added(first, second):
    return (first.astype(jnp.float32) + second.astype(jnp.float32)).astype(jnp.bfloat16)


def whole(space=pltpu.VMEM):
    return pl.BlockSpec(memory_space=space)


def pages_kernel(table, keys, values, joined, pages):
    heads = keys.shape[1] // HD
    for head in range(heads):
        lanes = slice(head * HD, (head + 1) * HD)
        joined[:, 2 * head * HD : (2 * head + 1) * HD] = keys[:, lanes]
        joined[:, (2 * head + 1) * HD : (2 * head + 2) * HD] = values[:, lanes]
    for page in range(keys.shape[0] // PAGE):
        pages[table[page]] = joined[page * PAGE : (page + 1) * PAGE, :]


def write_pages(keys, values, local_pages):
    rows, width = keys.shape
    return pl.pallas_call(
        pages_kernel,
        out_shape=(
            jax.ShapeDtypeStruct((rows, 2 * width), keys.dtype),
            jax.ShapeDtypeStruct((rows // PAGE, PAGE, 2 * width), keys.dtype),
        ),
        in_specs=[whole(pltpu.SMEM), whole(), whole()],
        out_specs=(whole(), whole()),
    )(local_pages, keys, values)


HEADS_HERE = 4


def attend_block(segments, query_segment, queries, block, source, diagonal, top, total, mixed):
    allowed = segments[pl.ds(source, 1), :] == query_segment[...]
    if diagonal:
        rows = lax.broadcasted_iota(jnp.int32, (BLOCK, BLOCK), 0)
        columns = lax.broadcasted_iota(jnp.int32, (BLOCK, BLOCK), 1)
        allowed = allowed & (columns <= rows)
    for head in range(HEADS_HERE):
        lane = slice(head, head + 1)
        key = block[:, 2 * head * HD : (2 * head + 1) * HD]
        value = block[:, (2 * head + 1) * HD : (2 * head + 2) * HD]
        scores = lax.dot_general(
            queries[:, head * HD : (head + 1) * HD],
            key,
            (((1,), (1,)), ((), ())),
            preferred_element_type=jnp.float32,
        ) * (1.0 / math.sqrt(HD))
        scores = jnp.where(allowed, scores, MASKED_SCORE)
        largest = jnp.max(scores, axis=1, keepdims=True)
        if not diagonal:
            before = top[:, lane]
            largest = jnp.maximum(largest, before)
        exp_scores = jnp.exp(scores - largest)
        update = jnp.dot(exp_scores.astype(jnp.bfloat16), value, preferred_element_type=jnp.float32)
        added_up = jnp.sum(exp_scores, axis=1, keepdims=True)
        if not diagonal:
            shrink = jnp.exp(before - largest)
            added_up += total[:, lane] * shrink
            update += mixed[head] * shrink
        top[:, lane] = largest
        total[:, lane] = added_up
        mixed[head] = update


def attend_earlier(place, segment_list, segments, query_segment, queries, blocks, top, total, mixed):
    for block, source in blocks:
        safe = jnp.maximum(source, 0)
        live = (source >= 0) & (
            segment_list[safe * BLOCK + BLOCK - 1] == segment_list[place[0] * BLOCK]
        )

        @pl.when(live)
        def _():
            attend_block(
                segments, query_segment, queries, block, safe, False, top, total, mixed
            )


def attention_first(
    place, segment_list, segments, query_segment, queries, own, near_x, near_z, top, total, mixed
):
    here = place[0]
    top[...] = jnp.zeros_like(top)
    total[...] = jnp.ones_like(total)
    attend_block(segments, query_segment, queries, own, here, True, top, total, mixed)
    odd = here % 2
    blocks = [(near_x, jnp.where(odd == 1, here - 1, -1)), (near_z, here - 2)]
    attend_earlier(
        place, segment_list, segments, query_segment, queries, blocks, top, total, mixed
    )


def attention_second(
    place, segment_list, segments, query_segment, queries, cross, far, far_cross, projection,
    top_in, total_in, mixed_in, sent, kept, top, total, mixed, attended,
):
    here, hd = place[0], place[1]
    odd = here % 2
    top[...] = top_in[...]
    total[...] = total_in[...]
    mixed[...] = mixed_in[...]
    blocks = [
        (cross, jnp.where(odd == 1, here - 3, here - 1)),
        (far, here - 4),
        (far_cross, jnp.where(odd == 1, -1, here - 3)),
    ]
    attend_earlier(
        place, segment_list, segments, query_segment, queries, blocks, top, total, mixed
    )
    for head in range(HEADS_HERE):
        attended[:, head * HD : (head + 1) * HD] = (
            mixed[head] / total[:, head : head + 1]
        ).astype(jnp.bfloat16)
    mate, across = hd ^ 1, hd ^ 2

    def rows_of(first, second):
        return jnp.concatenate(
            [
                attended[pl.ds(pl.multiple_of(quarter * ROWS, ROWS), ROWS), :]
                for quarter in (first, second)
            ],
            axis=0,
        )

    sent[...] = jnp.dot(
        rows_of(mate, mate ^ 2), projection[...], preferred_element_type=jnp.float32
    ).astype(jnp.bfloat16)
    kept[...] = jnp.dot(rows_of(hd, across), projection[...], preferred_element_type=jnp.float32)


def attention(
    place, segment_ids, query_segment, queries, own, near_x, near_z, cross, far, far_cross, out_proj
):
    segments = segment_ids.reshape(-1, BLOCK)
    state = (
        jax.ShapeDtypeStruct((BLOCK, HD), jnp.float32),
        jax.ShapeDtypeStruct((BLOCK, HD), jnp.float32),
        jax.ShapeDtypeStruct((HEADS_HERE, BLOCK, HD), jnp.float32),
    )
    smem, vmem = whole(pltpu.SMEM), whole()
    limit = pltpu.CompilerParams(vmem_limit_bytes=16 * 2**20)
    first = pl.pallas_call(
        attention_first,
        out_shape=state,
        in_specs=[smem, smem] + [vmem] * 6,
        out_specs=(vmem, vmem, vmem),
        compiler_params=limit,
        cost_estimate=pl.CostEstimate(flops=6 * 10**8, bytes_accessed=4 * 10**6, transcendentals=6 * 10**5),
    )(place, segment_ids, segments, query_segment, queries, own, near_x, near_z)
    return pl.pallas_call(
        attention_second,
        out_shape=(
            jax.ShapeDtypeStruct((2 * ROWS, out_proj.shape[1]), jnp.bfloat16),
            jax.ShapeDtypeStruct((2 * ROWS, out_proj.shape[1]), jnp.float32),
        ),
        in_specs=[smem, smem] + [vmem] * 10,
        out_specs=(vmem, vmem),
        scratch_shapes=[pltpu.VMEM(array.shape, jnp.float32) for array in state]
        + [pltpu.VMEM((BLOCK, HEADS_HERE * HD), jnp.bfloat16)],
        compiler_params=limit,
    )(
        place, segment_ids, segments, query_segment, queries, cross, far, far_cross, out_proj, *first
    )


CHUNK = 256
WIDE = 512
PIECE = 2 * ROWS
PIECES = 8
DEPTH = 3


def silu_times(gate_val, up_val):
    return (gate_val / (1.0 + jnp.exp(-gate_val)) * up_val).astype(jnp.bfloat16)


def routing_kernel(slot_row, weight_row, slot_column, pick, spread, slot_weight):
    slot_numbers = lax.broadcasted_iota(jnp.int32, (SLOTS, GROUP_ROWS), 0)
    slot_lanes = lax.broadcasted_iota(jnp.int32, (GROUP_ROWS, 2 * SLOTS), 1)
    for group in range(2):
        for expert in range(2):
            line = slice(2 * group + expert, 2 * group + expert + 1)
            held = slice(expert * SLOTS, (expert + 1) * SLOTS)
            hit = slot_row[line, :] == slot_numbers
            pick[group, held] = jnp.where(hit, 1.0, 0.0).astype(jnp.bfloat16)
            slot_weight[group, held] = jnp.sum(
                jnp.where(hit, weight_row[line, :], 0.0), axis=1, keepdims=True
            )
        first, second = [slot_column[:, 2 * group + e : 2 * group + e + 1] for e in range(2)]
        hit = (first == slot_lanes) | ((second >= 0) & (second + SLOTS == slot_lanes))
        spread[group] = jnp.where(hit, 1.0, 0.0).astype(jnp.bfloat16)


def routing_matrices(slot, weight):
    return pl.pallas_call(
        routing_kernel,
        out_shape=(
            jax.ShapeDtypeStruct((2, 2 * SLOTS, GROUP_ROWS), jnp.bfloat16),
            jax.ShapeDtypeStruct((2, GROUP_ROWS, 2 * SLOTS), jnp.bfloat16),
            jax.ShapeDtypeStruct((2, 2 * SLOTS, 1), jnp.float32),
        ),
        in_specs=[whole()] * 3,
        out_specs=(whole(),) * 3,
        compiler_params=pltpu.CompilerParams(vmem_limit_bytes=16 * 2**20),
    )(slot, weight, slot.T)


def experts_kernel(group, with_shared, *refs):
    place, pick, spread, slot_weight = refs[:4]
    pieces, refs = refs[4 : 4 + PIECES], refs[4 + PIECES :]
    gate, up, down = refs[:3]
    refs = refs[3:]
    if with_shared:
        shared, refs = refs[:3], refs[3:]
    targets, refs = refs[:PIECES], refs[PIECES:]
    rows, picked, hidden, gate_held, up_held, down_held, arrived, gate_up_arrived, down_arrived = refs[:9]
    width = rows.shape[1]
    chunks = [
        (expert, low, min(CHUNK, FF_E - low)) for expert in range(2) for low in range(0, FF_E, CHUNK)
    ]

    def gate_up_copies(number):
        expert, low, size = chunks[number]
        lanes, slot = pl.ds(expert * FF_E + low, size), number % DEPTH
        return [
            pltpu.make_async_copy(
                source.at[:, lanes], held.at[slot, :, pl.ds(0, size)], gate_up_arrived.at[slot, which]
            )
            for which, (source, held) in enumerate(((gate, gate_held), (up, up_held)))
        ]

    def down_copy(expert):
        return pltpu.make_async_copy(
            down.at[pl.ds(expert * FF_E, FF_E), :], down_held.at[expert], down_arrived.at[expert]
        )

    copies = [
        pltpu.make_async_copy(piece, rows.at[pl.ds(number * PIECE, PIECE), :], arrived.at[number])
        for number, piece in enumerate(pieces)
    ]
    for copy in copies:
        copy.start()
    for number in range(DEPTH):
        for copy in gate_up_copies(number):
            copy.start()
    down_copy(0).start()
    if with_shared:
        s_gate, s_up, s_down, s_arrived, s_rows, s_hidden = refs[9:]
        s_copies = [
            pltpu.make_async_copy(source, target, s_arrived.at[number])
            for number, (source, target) in enumerate(zip(shared, (s_gate, s_up, s_down)))
        ]

    for copy in copies:
        copy.wait()
    for low in range(0, width, WIDE):
        lanes = slice(low, low + WIDE)
        picked[:, lanes] = jnp.dot(
            pick[group], rows[:, lanes], preferred_element_type=jnp.float32
        ).astype(jnp.bfloat16)
    for number, (expert, low, size) in enumerate(chunks):
        held, slot = slice(expert * SLOTS, (expert + 1) * SLOTS), number % DEPTH
        for copy in gate_up_copies(number):
            copy.wait()
        gate_val = jnp.dot(picked[held], gate_held[slot, :, :size], preferred_element_type=jnp.float32)
        up_val = jnp.dot(picked[held], up_held[slot, :, :size], preferred_element_type=jnp.float32)
        hidden[:, low : low + size] = silu_times(gate_val, up_val)
        if number + DEPTH < len(chunks):
            for copy in gate_up_copies(number + DEPTH):
                copy.start()
        if number == len(chunks) // 2:
            down_copy(1).start()
        if with_shared and number == len(chunks) - DEPTH:
            for copy in s_copies:
                copy.start()
        if low + size == FF_E:
            down_copy(expert).wait()
            for start in range(0, width, WIDE):
                lanes = slice(start, start + WIDE)
                result = jnp.dot(
                    hidden[...], down_held[expert, :, lanes], preferred_element_type=jnp.float32
                )
                picked[held, lanes] = (result * slot_weight[group, held]).astype(jnp.bfloat16)

    if with_shared:
        upper = place[1] % 2 == 1
        s_rows[0:ROWS] = rows[0:ROWS]
        s_rows[ROWS : 2 * ROWS] = rows[PIECE : PIECE + ROWS]
        base = pl.multiple_of(jnp.where(upper, 2, 5) * PIECE, PIECE)
        s_rows[2 * ROWS : 3 * ROWS] = rows[pl.ds(base, ROWS), :]
        s_rows[3 * ROWS : 4 * ROWS] = rows[pl.ds(base + PIECE, ROWS), :]
        for copy in s_copies:
            copy.wait()
        turned = (((1,), (1,)), ((), ()))
        units = s_gate.shape[0]
        for low in range(0, units, CHUNK):
            size = min(CHUNK, units - low)
            gate_val, up_val = [
                lax.dot_general(
                    s_rows[...], weight[low : low + size, :], turned, preferred_element_type=jnp.float32
                )
                for weight in (s_gate, s_up)
            ]
            s_hidden[:, low : low + size] = silu_times(gate_val, up_val)

    for low in range(0, width, CHUNK):
        lanes = slice(low, low + CHUNK)
        value = jnp.dot(spread[group], picked[:, lanes], preferred_element_type=jnp.float32)
        if with_shared:
            s_result = jnp.dot(s_hidden[...], s_down[:, lanes], preferred_element_type=jnp.float32)
        for part, target in enumerate(targets):
            mine = value[part * PIECE : (part + 1) * PIECE]
            if with_shared and part in (0, 1, 2, 3, 5, 6):
                if part < 2:
                    term = s_result[part * ROWS : (part + 1) * ROWS]
                else:
                    start = (2 + (part - 2) % 3) * ROWS
                    here = upper if part < 4 else jnp.logical_not(upper)
                    term = jnp.where(here, s_result[start : start + ROWS], 0.0)
                target[:ROWS, lanes] = (mine[:ROWS] + term).astype(jnp.bfloat16)
                target[ROWS:, lanes] = mine[ROWS:].astype(jnp.bfloat16)
            else:
                target[:, lanes] = mine.astype(jnp.bfloat16)


def experts(place, group, matrices, pieces, weights, shared):
    width = pieces[0].shape[1]
    hbm, vmem = whole(pl.ANY), whole()
    scratch = [
        pltpu.VMEM((GROUP_ROWS, width), jnp.bfloat16),
        pltpu.VMEM((2 * SLOTS, width), jnp.bfloat16),
        pltpu.VMEM((SLOTS, FF_E), jnp.bfloat16),
        pltpu.VMEM((DEPTH, width, CHUNK), jnp.bfloat16),
        pltpu.VMEM((DEPTH, width, CHUNK), jnp.bfloat16),
        pltpu.VMEM((2, FF_E, width), jnp.bfloat16),
        pltpu.SemaphoreType.DMA((PIECES,)),
        pltpu.SemaphoreType.DMA((DEPTH, 2)),
        pltpu.SemaphoreType.DMA((2,)),
    ]
    operands = [place, *matrices, *pieces, *weights]
    if shared is not None:
        operands += list(shared)
        scratch += [pltpu.VMEM(array.shape, array.dtype) for array in shared]
        scratch += [
            pltpu.SemaphoreType.DMA((3,)),
            pltpu.VMEM((BLOCK, width), jnp.bfloat16),
            pltpu.VMEM((BLOCK, shared[2].shape[0]), jnp.bfloat16),
        ]
    in_specs = [whole(pltpu.SMEM)] + [vmem] * 3
    in_specs += [hbm] * (len(operands) - len(in_specs))
    return pl.pallas_call(
        lambda *refs: experts_kernel(group, shared is not None, *refs),
        out_shape=(jax.ShapeDtypeStruct((PIECE, width), jnp.bfloat16),) * PIECES,
        in_specs=in_specs,
        out_specs=(vmem,) * PIECES,
        scratch_shapes=scratch,
        compiler_params=pltpu.CompilerParams(vmem_limit_bytes=SCOPED[shared is not None] * 2**20),
        cost_estimate=pl.CostEstimate(
            flops=10**10, bytes_accessed=44 * 10**6, transcendentals=10**6
        ),
    )(*operands)


SCOPED = {True: 50, False: 40}


def gather_plane(rows):
    mate = send(rows, CORE_SWAP)
    near = send(rows, X_THEN_Y)
    near_mate = send(mate, X_THEN_Y)
    corner = send(near, Y_THEN_X)
    fetched = (near, near_mate, corner)
    return (rows, mate, *fetched, *[send(piece, CORE_SWAP) for piece in fetched])


def sum_plane(own, mate, near, near_mate, corner, mate_near, mate_near_mate, mate_corner):
    corner = added(corner, send(mate_corner, CORE_SWAP))
    from_corner = send(corner, Y_THEN_X)
    near_mate = added(near_mate, send(mate_near_mate, CORE_SWAP))
    from_near_mate = send(near_mate, X_THEN_Y)
    near = near.astype(jnp.float32) + send(mate_near, CORE_SWAP).astype(jnp.float32)
    from_near = send(added(near, from_corner), X_THEN_Y)
    return (
        own.astype(jnp.float32)
        + send(mate, CORE_SWAP).astype(jnp.float32)
        + send(from_near_mate, CORE_SWAP).astype(jnp.float32)
        + from_near.astype(jnp.float32)
    )


def routing_tables(expert_ids, route_weight, place):
    count = expert_ids.shape[1]
    packed = jnp.concatenate([expert_ids.T.astype(jnp.float32), route_weight.T], axis=0)
    pair = jnp.stack([packed, send(packed, X_SWAP)])
    steps = [pair]
    for _ in range(3):
        steps.append(send(steps[-1], Z_ON))
    slices = jnp.stack(steps).reshape(NZ, 2, 2 * count, 4, ROWS).transpose(0, 1, 3, 2, 4)
    slices = slices.reshape(-1, 2 * count, ROWS)
    order = lax.dynamic_index_in_dim(jnp.asarray(slice_order()), place[1], 0, keepdims=False)
    listed = slices[order.reshape(-1)].reshape(2, 16, 2 * count, ROWS)
    first_expert = 2 * (place[0] * 4 + place[1])
    local = (first_expert + lax.iota(jnp.int32, 2)).astype(jnp.float32)
    match = listed[:, None, :, :count] == local[None, :, None, None, None]
    hit = jnp.any(match, axis=3).reshape(2, 2, GROUP_ROWS)
    weight = jnp.sum(jnp.where(match, listed[:, None, :, count:], 0.0), axis=3)
    weight = weight.reshape(2, 2, GROUP_ROWS)
    ones = hit.astype(jnp.int32)
    slot = jnp.where(hit, jnp.cumsum(ones, axis=2) - 1, -1)
    return routing_matrices(slot.reshape(4, GROUP_ROWS), weight.reshape(4, GROUP_ROWS))


def block_pairs(target):
    pairs = []
    for z in range(NZ):
        for x in range(2):
            aim = target(z, x)
            if aim is not None and aim[0] < NZ:
                pairs.append((z * 2 + x, aim[0] * 2 + aim[1]))
    return pairs


def sliced_body(
    residual_in,
    queries,
    keys,
    values,
    segment_ids,
    out_proj,
    norm_gain,
    shared_gate,
    shared_up,
    shared_down,
    expert_gate,
    expert_up,
    expert_down,
    expert_ids,
    route_weight,
    block_table,
):
    tok_here = lax.axis_index("tok")
    hd_here = lax.axis_index("hd")
    place = jnp.stack([tok_here, hd_here]).astype(jnp.int32)
    page_count = BLOCK // PAGE
    own, kv_pages = write_pages(keys, values, block_table - tok_here * page_count)

    def move(array, target):
        return lax.ppermute(array, "tok", block_pairs(target))

    near_z = move(own, lambda z, x: (z + 1, x))
    own_later, ids_later, _ = lax.optimization_barrier((own, expert_ids, near_z))
    near_x = move(own_later, lambda z, x: (z, 1) if x == 0 else None)
    cross = move(near_z, lambda z, x: (z, 1 - x))
    far = move(near_z, lambda z, x: (z + 1, x))
    far_cross = move(near_z, lambda z, x: (z + 1, 0) if x == 1 else None)

    tables = routing_tables(ids_later, route_weight, place)
    query_segment = lax.dynamic_slice_in_dim(segment_ids, tok_here * BLOCK, BLOCK, 0)[:, None]
    sent, kept = attention(
        place, segment_ids, query_segment, queries, own, near_x, near_z, cross, far, far_cross, out_proj,
    )
    kept = kept + send(sent, CORE_SWAP).astype(jnp.float32)
    resid_rows = (
        lax.dynamic_slice_in_dim(residual_in, hd_here * ROWS, ROWS, 0).astype(jnp.float32)
        + kept[:ROWS]
        + send(kept[ROWS:].astype(jnp.bfloat16), Y_SWAP).astype(jnp.float32)
    )
    normed = rms_normed(resid_rows, norm_gain)

    steps = [normed]
    for _ in range(3):
        steps.append(send(steps[-1], Z_ON))
    weights = (expert_gate, expert_up, expert_down)
    shared = (shared_gate.T, shared_up.T, shared_down)
    sums = []
    for group in range(2):
        gathered = gather_plane(jnp.concatenate(steps[2 * group : 2 * group + 2], axis=0))
        terms = experts(place, group, tables, gathered, weights, shared if group == 0 else None)
        sums.append(sum_plane(*terms))
    returned = [
        send(part.astype(jnp.bfloat16), pairs).astype(jnp.float32)
        for part, pairs in ((sums[0][ROWS:], Z_BACK), (sums[1][:ROWS], Z_TWO), (sums[1][ROWS:], Z_ON))
    ]
    output = resid_rows + sums[0][:ROWS] + returned[0] + returned[1] + returned[2]
    return (output.astype(jnp.bfloat16), kv_pages)


def solution(mesh):
    placed = (
        P("tok", None),
        P("tok", "hd"),
        P("tok", "hd"),
        P("tok", "hd"),
        P(),
        P("hd", None),
        P(),
        P(None, "hd"),
        P(None, "hd"),
        P("hd", None),
        P(None, ("tok", "hd")),
        P(None, ("tok", "hd")),
        P(("tok", "hd"), None),
        P("tok", None),
        P("tok", None),
        P("tok"),
    )
    return jax.shard_map(
        sliced_body if dict(mesh.shape) == {"tok": 2 * NZ, "hd": 4} else general_body,
        mesh=mesh,
        in_specs=placed,
        out_specs=(P(("tok", "hd"), None), P("tok", None, "hd")),
        check_vma=False,
    )
```

```python
import math

import jax
import jax.numpy as jnp
import numpy as np
from jax import lax
from jax.experimental import pallas as pl
from jax.experimental.pallas import tpu as pltpu
from jax.sharding import PartitionSpec as P

HD = 128
EXPERTS = 64
FF_E = 1408
PAGE = 16
CAP = 48


MASKED_SCORE = -1e30
NORM_EPSILON = 1e-06


def from_behind(array, axis, by):
    length = lax.axis_size(axis)
    pairs = [(i, i + by) for i in range(length) if 0 <= i + by < length]
    return lax.ppermute(array, axis, pairs)


def rms_normed(resid_state, norm_gain):
    mean_square = jnp.mean(resid_state * resid_state, axis=1, keepdims=True)
    return (resid_state * lax.rsqrt(mean_square + NORM_EPSILON) * norm_gain).astype(jnp.bfloat16)


def general_body(
    residual_in,
    queries,
    keys,
    values,
    segment_ids,
    out_proj,
    norm_gain,
    shared_gate,
    shared_up,
    shared_down,
    expert_gate,
    expert_up,
    expert_down,
    expert_ids,
    route_weight,
    block_table,
):
    block_len = residual_in.shape[0]
    model_width = residual_in.shape[1]
    tok_count = lax.axis_size("tok")
    hd_count = lax.axis_size("hd")
    tok_here = lax.axis_index("tok")
    hd_here = lax.axis_index("hd")
    heads_here = queries.shape[1] // HD
    query_three = queries.reshape(block_len, heads_here, HD)
    offsets = lax.iota(jnp.int32, block_len)
    query_pos = tok_here * block_len + offsets
    query_seg = lax.dynamic_slice_in_dim(segment_ids, tok_here * block_len, block_len, 0)

    def attend(carried, key_blk, value_blk, source):
        safe_source = jnp.maximum(source, 0)
        key_seg = lax.dynamic_slice_in_dim(segment_ids, safe_source * block_len, block_len, 0)
        key_pos = source * block_len + offsets

        def compute(current):
            running_max, denom_sum, weighted_sum = current
            scores = jnp.einsum(
                "qhd,khd->hqk",
                query_three,
                key_blk.reshape(block_len, heads_here, HD),
                preferred_element_type=jnp.float32,
            ) / math.sqrt(HD)
            allowed = (key_seg[None, :] == query_seg[:, None]) & (
                key_pos[None, :] <= query_pos[:, None]
            )
            scores = jnp.where(allowed[None], scores, MASKED_SCORE)
            new_max = jnp.maximum(running_max, jnp.max(scores, axis=2))
            shrink = jnp.exp(running_max - new_max)
            exp_scores = jnp.where(allowed[None], jnp.exp(scores - new_max[:, :, None]), 0.0)
            denom_sum = denom_sum * shrink + jnp.sum(exp_scores, axis=2)
            update = jnp.einsum(
                "hqk,khd->qhd",
                exp_scores.astype(jnp.bfloat16),
                value_blk.reshape(block_len, heads_here, HD),
                preferred_element_type=jnp.float32,
            )
            weighted_sum = weighted_sum * jnp.transpose(shrink)[:, :, None] + update
            return (new_max, denom_sum, weighted_sum)

        is_live = (source >= 0) & (
            segment_ids[safe_source * block_len + block_len - 1] >= query_seg[0]
        )
        return lax.cond(is_live, compute, lambda unchanged: unchanged, carried)

    initial = (
        jnp.full((heads_here, block_len), MASKED_SCORE, jnp.float32),
        jnp.zeros((heads_here, block_len), jnp.float32),
        jnp.zeros((block_len, heads_here, HD), jnp.float32),
    )
    carried = attend(initial, keys, values, tok_here)

    def relay(relay_step, loop_carry):
        moving, inner_state = loop_carry
        moving = from_behind(moving, "tok", 1)
        inner_state = attend(inner_state, moving[0], moving[1], tok_here - relay_step - 1)
        return (moving, inner_state)

    _, final_state = lax.fori_loop(0, tok_count // 2, relay, (jnp.stack([keys, values]), carried))
    weighted_sum = final_state[2]
    denom_sum = final_state[1]
    attended = (
        (weighted_sum / jnp.transpose(denom_sum)[:, :, None])
        .astype(jnp.bfloat16)
        .reshape(block_len, heads_here * HD)
    )
    row_count = block_len // hd_count
    row_start = hd_here * row_count
    head_terms = jnp.dot(attended, out_proj, preferred_element_type=jnp.float32)
    resid_full = residual_in.astype(jnp.float32) + lax.psum(
        head_terms.astype(jnp.bfloat16), "hd"
    ).astype(jnp.float32)
    normed = rms_normed(resid_full, norm_gain)
    resid_rows = lax.dynamic_slice_in_dim(resid_full, row_start, row_count, 0)
    shared_gate_val = jnp.dot(normed, shared_gate, preferred_element_type=jnp.float32)
    shared_up_val = jnp.dot(normed, shared_up, preferred_element_type=jnp.float32)
    shared_hidden = (jax.nn.silu(shared_gate_val) * shared_up_val).astype(jnp.bfloat16)
    partial_out = jnp.dot(shared_hidden, shared_down, preferred_element_type=jnp.float32)
    slice_width = expert_gate.shape[1]
    held_count = max(1, slice_width // FF_E)
    part_width = slice_width // held_count
    per_group = slice_width * hd_count // FF_E
    first_local = hd_here * slice_width // FF_E
    expert_range = lax.iota(jnp.int32, EXPERTS)
    onehot = jnp.sum(
        (expert_ids[:, :, None] == expert_range[None, None, :]).astype(jnp.int32), axis=1
    )
    earlier = jnp.cumsum(onehot, axis=0) - onehot
    slot_index = jnp.take_along_axis(earlier, expert_ids, axis=1)
    flat_expert = expert_ids.reshape(-1)
    flat_slot = slot_index.reshape(-1)
    row_source = jnp.repeat(offsets, expert_ids.shape[1])
    row_table = (
        jnp.full((EXPERTS, CAP), block_len, jnp.int32).at[flat_expert, flat_slot].set(row_source)
    )
    weight_table = (
        jnp.zeros((EXPERTS, CAP), jnp.float32)
        .at[flat_expert, flat_slot]
        .set(route_weight.reshape(-1))
    )
    send_rows = lax.dynamic_slice_in_dim(
        row_table.reshape(tok_count, per_group, CAP), first_local, held_count, 1
    )
    send_weight = lax.dynamic_slice_in_dim(
        weight_table.reshape(tok_count, per_group, CAP), first_local, held_count, 1
    )
    padded_rows = jnp.concatenate([normed, jnp.zeros((1, model_width), jnp.bfloat16)], axis=0)
    outgoing = padded_rows[send_rows]
    gate_three = expert_gate.reshape(model_width, held_count, part_width)
    up_three = expert_up.reshape(model_width, held_count, part_width)
    down_three = expert_down.reshape(held_count, part_width, model_width)
    incoming = lax.all_to_all(outgoing, "tok", split_axis=0, concat_axis=0, tiled=True)
    gate_val = jnp.einsum(
        "secd,def->secf", incoming, gate_three, preferred_element_type=jnp.float32
    )
    up_val = jnp.einsum("secd,def->secf", incoming, up_three, preferred_element_type=jnp.float32)
    hidden = (jax.nn.silu(gate_val) * up_val).astype(jnp.bfloat16)
    result = jnp.einsum(
        "secf,efd->secd", hidden, down_three, preferred_element_type=jnp.float32
    ).astype(jnp.bfloat16)
    returned_rows = lax.all_to_all(result, "tok", split_axis=0, concat_axis=0, tiled=True)
    weighted_rows = returned_rows.astype(jnp.float32) * send_weight[:, :, :, None]
    routed = (
        jnp.zeros((block_len + 1, model_width), jnp.float32)
        .at[send_rows.reshape(-1)]
        .add(weighted_rows.reshape(-1, model_width))[:block_len]
    )
    summed_rows = lax.psum_scatter(
        (partial_out + routed).astype(jnp.bfloat16), "hd", scatter_dimension=0, tiled=True
    ).astype(jnp.float32)
    output = (resid_rows + summed_rows).astype(jnp.bfloat16)
    page_count = block_len // PAGE
    page_data = jnp.stack(
        [keys.reshape(block_len, heads_here, HD), values.reshape(block_len, heads_here, HD)], axis=2
    )
    page_data = page_data.reshape(page_count, PAGE, heads_here * 2 * HD)
    local_pages = block_table - tok_here * page_count
    kv_pages = jnp.zeros_like(page_data).at[local_pages].set(page_data)
    return (output, kv_pages)


NZ = 4
BOTH = ("tok", "hd")
ROWS = 64
BLOCK = 256
GROUP_ROWS = 1024
SLOTS = 4 * CAP
NEXT_Z = {0: 1, 1: 3, 3: 2, 2: 0}
BACK_Z = {after: before for before, after in NEXT_Z.items()}
DEVICES = [(z, x, y, c) for z in range(NZ) for x in range(2) for y in range(2) for c in range(2)]


def flat_index(z, x, y, c):
    return (z * 2 + x) * 4 + y * 2 + c


def pairs_of(target):
    return [(flat_index(*device), flat_index(*target(*device))) for device in DEVICES]


Z_ON = pairs_of(lambda z, x, y, c: (NEXT_Z[z], x, y, c))
Z_BACK = pairs_of(lambda z, x, y, c: (BACK_Z[z], x, y, c))
Z_TWO = pairs_of(lambda z, x, y, c: (NEXT_Z[NEXT_Z[z]], x, y, c))
CORE_SWAP = pairs_of(lambda z, x, y, c: (z, x, y, 1 - c))
X_SWAP = pairs_of(lambda z, x, y, c: (z, 1 - x, y, c))
Y_SWAP = pairs_of(lambda z, x, y, c: (z, x, 1 - y, c))
X_THEN_Y = pairs_of(lambda z, x, y, c: (z, 1 - x, y, c) if c == 0 else (z, x, 1 - y, c))
Y_THEN_X = pairs_of(lambda z, x, y, c: (z, x, 1 - y, c) if c == 0 else (z, 1 - x, y, c))


def slice_order():
    order = np.zeros((4, 2, 16), np.int32)
    for y in range(2):
        for c in range(2):
            mine = {
                0: [(1, y, 0), (1, y, 1), (1, 1 - y, 0)],
                1: [(0, 1 - y, 1), (0, 1 - y, 0), (1, 1 - y, 1)],
            }
            places = [(0, y, c), (0, y, 1 - c)] + mine[c] + mine[1 - c]
            for group in range(2):
                order[y * 2 + c, group] = [
                    ((2 * group + part) * 2 + other) * 4 + at_y * 2 + at_c
                    for other, at_y, at_c in places
                    for part in range(2)
                ]
    return order


def send(array, pairs):
    return lax.ppermute(array, BOTH, pairs)


def added(first, second):
    return (first.astype(jnp.float32) + second.astype(jnp.float32)).astype(jnp.bfloat16)


def whole(space=pltpu.VMEM):
    return pl.BlockSpec(memory_space=space)


def pages_kernel(table, place, keys, values, joined, pages):
    heads = keys.shape[1] // HD
    for head in range(heads):
        lanes = slice(head * HD, (head + 1) * HD)
        joined[:, 2 * head * HD : (2 * head + 1) * HD] = keys[:, lanes]
        joined[:, (2 * head + 1) * HD : (2 * head + 2) * HD] = values[:, lanes]
    for page in range(keys.shape[0] // PAGE):
        pages[table[page] - place[0] * (keys.shape[0] // PAGE)] = joined[page * PAGE : (page + 1) * PAGE, :]


def write_pages(keys, values, block_table, place):
    rows, width = keys.shape
    return pl.pallas_call(
        pages_kernel,
        out_shape=(
            jax.ShapeDtypeStruct((rows, 2 * width), keys.dtype),
            jax.ShapeDtypeStruct((rows // PAGE, PAGE, 2 * width), keys.dtype),
        ),
        in_specs=[whole(pltpu.SMEM), whole(pltpu.SMEM), whole(), whole()],
        out_specs=(whole(), whole()),
    )(block_table, place, keys, values)


HEADS_HERE = 4


def attend(place, segments, query_segment, queries, blocks):
    offsets = lax.broadcasted_iota(jnp.int32, (1, BLOCK), 1)
    key_segment, key_place = [], []
    for _, source in blocks:
        line = segments[pl.ds(jnp.maximum(source, 0), 1), :]
        key_segment.append(jnp.where(source >= 0, line, -1))
        key_place.append(source * BLOCK + offsets)
    query_place = place[0] * BLOCK + lax.broadcasted_iota(jnp.int32, (BLOCK, 1), 0)
    allowed = (jnp.concatenate(key_segment, axis=1) == query_segment[...]) & (
        jnp.concatenate(key_place, axis=1) <= query_place
    )
    results = []
    for head in range(HEADS_HERE):
        key, value = [
            jnp.concatenate(
                [block[:, (2 * head + part) * HD : (2 * head + part + 1) * HD] for block, _ in blocks], axis=0
            )
            for part in range(2)
        ]
        scores = lax.dot_general(
            queries[:, head * HD : (head + 1) * HD],
            key,
            (((1,), (1,)), ((), ())),
            preferred_element_type=jnp.float32,
        ) * (1.0 / math.sqrt(HD))
        scores = jnp.where(allowed, scores, MASKED_SCORE)
        largest = jnp.max(scores, axis=1, keepdims=True)
        exp_scores = jnp.where(allowed, jnp.exp(scores - largest), 0.0)
        mixed = jnp.dot(exp_scores.astype(jnp.bfloat16), value, preferred_element_type=jnp.float32)
        results.append((largest, jnp.sum(exp_scores, axis=1, keepdims=True), mixed))
    return results


def attention_first(
    place, segments, query_segment, queries, own, near_x, near_z, after, top, total, mixed
):
    here = place[0]
    blocks = [(own, here), (near_x, jnp.where(here % 2 == 1, here - 1, -1)), (near_z, here - 2)]
    results = attend(place, segments, query_segment, queries, blocks)
    top[...] = jnp.concatenate([result[0] for result in results], axis=1)
    total[...] = jnp.concatenate([result[1] for result in results], axis=1)
    for head in range(HEADS_HERE):
        mixed[head] = results[head][2]


def attention_second(
    place, segments, query_segment, queries, cross, far, far_cross, projection,
    top, total, mixed, after, sent, kept, attended,
):
    here, hd = place[0], place[1]
    odd = here % 2
    blocks = [
        (cross, jnp.where(odd == 1, here - 3, here - 1)),
        (far, here - 4),
        (far_cross, jnp.where(odd == 1, -1, here - 3)),
    ]
    results = attend(place, segments, query_segment, queries, blocks)
    for head, (largest, added_up, update) in enumerate(results):
        before = top[:, head : head + 1]
        both = jnp.maximum(before, largest)
        old, new = jnp.exp(before - both), jnp.exp(largest - both)
        denom = total[:, head : head + 1] * old + added_up * new
        attended[:, head * HD : (head + 1) * HD] = (
            (mixed[head] * old + update * new) / denom
        ).astype(jnp.bfloat16)
    mate, across = hd ^ 1, hd ^ 2

    def rows_of(first, second):
        return jnp.concatenate(
            [
                attended[pl.ds(pl.multiple_of(quarter * ROWS, ROWS), ROWS), :]
                for quarter in (first, second)
            ],
            axis=0,
        )

    sent[...] = jnp.dot(
        rows_of(mate, mate ^ 2), projection[...], preferred_element_type=jnp.float32
    ).astype(jnp.bfloat16)
    kept[...] = jnp.dot(rows_of(hd, across), projection[...], preferred_element_type=jnp.float32)


def attention(
    place, segment_ids, query_segment, queries, own, near_x, near_z, cross, far, far_cross, out_proj, after
):
    segments = segment_ids.reshape(-1, BLOCK)
    state = (
        jax.ShapeDtypeStruct((BLOCK, HEADS_HERE), jnp.float32),
        jax.ShapeDtypeStruct((BLOCK, HEADS_HERE), jnp.float32),
        jax.ShapeDtypeStruct((HEADS_HERE, BLOCK, HD), jnp.float32),
    )
    smem, vmem, anywhere = whole(pltpu.SMEM), whole(), whole(pl.ANY)
    limit = pltpu.CompilerParams(vmem_limit_bytes=24 * 2**20)
    first = pl.pallas_call(
        attention_first,
        out_shape=state,
        in_specs=[smem] + [vmem] * 6 + [anywhere],
        out_specs=(vmem, vmem, vmem),
        compiler_params=limit,
        cost_estimate=pl.CostEstimate(flops=8 * 10**8, bytes_accessed=4 * 10**6, transcendentals=8 * 10**5),
    )(place, segments, query_segment, queries, own, near_x, near_z, after[0])
    return pl.pallas_call(
        attention_second,
        out_shape=(
            jax.ShapeDtypeStruct((2 * ROWS, out_proj.shape[1]), jnp.bfloat16),
            jax.ShapeDtypeStruct((2 * ROWS, out_proj.shape[1]), jnp.float32),
        ),
        in_specs=[smem] + [vmem] * 10 + [anywhere],
        out_specs=(vmem, vmem),
        scratch_shapes=[pltpu.VMEM((BLOCK, HEADS_HERE * HD), jnp.bfloat16)],
        compiler_params=limit,
        cost_estimate=pl.CostEstimate(flops=10**9, bytes_accessed=6 * 10**6, transcendentals=8 * 10**5),
    )(
        place, segments, query_segment, queries, cross, far, far_cross, out_proj, *first, after[1]
    )


def touch(arrays, after):
    count = len(arrays)

    def kernel(*refs):
        sources, token, strips, arrived = refs[:count], refs[count + 1], refs[count + 2 : -1], refs[-1]
        copies = [
            pltpu.make_async_copy(source.at[:, pl.ds(0, HD)], strip, arrived.at[number])
            for number, (source, strip) in enumerate(zip(sources, strips))
        ]
        for copy in copies:
            copy.start()
        token[...] = jnp.zeros_like(token)
        for copy in copies:
            copy.wait()

    return pl.pallas_call(
        kernel,
        out_shape=jax.ShapeDtypeStruct((8, HD), jnp.float32),
        in_specs=[whole(pltpu.HBM)] * count + [whole(pl.ANY)],
        out_specs=whole(),
        scratch_shapes=[pltpu.VMEM((array.shape[0], HD), array.dtype) for array in arrays]
        + [pltpu.SemaphoreType.DMA((count,))],
        compiler_params=pltpu.CompilerParams(vmem_limit_bytes=58 * 2**20),
        cost_estimate=pl.CostEstimate(flops=0, bytes_accessed=3 * 10**6, transcendentals=0),
    )(*arrays, after)


CHUNK = 256
WIDE = 512
PIECE = 2 * ROWS
PIECES = 8
DEPTH = 3


def silu_times(gate_val, up_val):
    return (gate_val / (1.0 + jnp.exp(-gate_val)) * up_val).astype(jnp.bfloat16)


def routing_kernel(slot_row, weight_row, slot_column, pick, spread, slot_weight):
    slot_numbers = lax.broadcasted_iota(jnp.int32, (SLOTS, GROUP_ROWS), 0)
    slot_lanes = lax.broadcasted_iota(jnp.int32, (GROUP_ROWS, 2 * SLOTS), 1)
    for group in range(2):
        for expert in range(2):
            line = slice(2 * group + expert, 2 * group + expert + 1)
            held = slice(expert * SLOTS, (expert + 1) * SLOTS)
            hit = slot_row[line, :] == slot_numbers
            pick[group, held] = jnp.where(hit, 1.0, 0.0).astype(jnp.bfloat16)
            slot_weight[group, held] = jnp.sum(
                jnp.where(hit, weight_row[line, :], 0.0), axis=1, keepdims=True
            )
        first, second = [slot_column[:, 2 * group + e : 2 * group + e + 1] for e in range(2)]
        hit = (first == slot_lanes) | ((second >= 0) & (second + SLOTS == slot_lanes))
        spread[group] = jnp.where(hit, 1.0, 0.0).astype(jnp.bfloat16)


def routing_matrices(slot, weight):
    return pl.pallas_call(
        routing_kernel,
        out_shape=(
            jax.ShapeDtypeStruct((2, 2 * SLOTS, GROUP_ROWS), jnp.bfloat16),
            jax.ShapeDtypeStruct((2, GROUP_ROWS, 2 * SLOTS), jnp.bfloat16),
            jax.ShapeDtypeStruct((2, 2 * SLOTS, 1), jnp.float32),
        ),
        in_specs=[whole()] * 3,
        out_specs=(whole(),) * 3,
        compiler_params=pltpu.CompilerParams(vmem_limit_bytes=16 * 2**20),
    )(slot, weight, slot.T)


def experts_kernel(group, with_shared, *refs):
    place, pick, spread, slot_weight = refs[:4]
    pieces, refs = refs[4 : 4 + PIECES], refs[4 + PIECES :]
    gate, up, down = refs[:3]
    refs = refs[3:]
    if with_shared:
        shared, refs = refs[:3], refs[3:]
    targets, refs = refs[:PIECES], refs[PIECES:]
    rows, picked, hidden, gate_held, up_held, down_held, arrived, gate_up_arrived, down_arrived = refs[:9]
    width = rows.shape[1]
    chunks = [
        (expert, low, min(CHUNK, FF_E - low)) for expert in range(2) for low in range(0, FF_E, CHUNK)
    ]

    def gate_up_copies(number):
        expert, low, size = chunks[number]
        lanes, slot = pl.ds(expert * FF_E + low, size), number % DEPTH
        return [
            pltpu.make_async_copy(
                source.at[:, lanes], held.at[slot, :, pl.ds(0, size)], gate_up_arrived.at[slot, which]
            )
            for which, (source, held) in enumerate(((gate, gate_held), (up, up_held)))
        ]

    def down_copy(expert):
        return pltpu.make_async_copy(
            down.at[pl.ds(expert * FF_E, FF_E), :], down_held.at[expert], down_arrived.at[expert]
        )

    copies = [
        pltpu.make_async_copy(piece, rows.at[pl.ds(number * PIECE, PIECE), :], arrived.at[number])
        for number, piece in enumerate(pieces)
    ]
    for copy in copies:
        copy.start()
    for number in range(DEPTH):
        for copy in gate_up_copies(number):
            copy.start()
    down_copy(0).start()
    if with_shared:
        s_gate, s_up, s_down, s_arrived, s_rows, s_hidden = refs[9:]
        s_copies = [
            pltpu.make_async_copy(source, target, s_arrived.at[number])
            for number, (source, target) in enumerate(zip(shared, (s_gate, s_up, s_down)))
        ]

    for copy in copies:
        copy.wait()
    for low in range(0, width, WIDE):
        lanes = slice(low, low + WIDE)
        picked[:, lanes] = jnp.dot(
            pick[group], rows[:, lanes], preferred_element_type=jnp.float32
        ).astype(jnp.bfloat16)
    for number, (expert, low, size) in enumerate(chunks):
        held, slot = slice(expert * SLOTS, (expert + 1) * SLOTS), number % DEPTH
        for copy in gate_up_copies(number):
            copy.wait()
        gate_val = jnp.dot(picked[held], gate_held[slot, :, :size], preferred_element_type=jnp.float32)
        up_val = jnp.dot(picked[held], up_held[slot, :, :size], preferred_element_type=jnp.float32)
        hidden[:, low : low + size] = silu_times(gate_val, up_val)
        if number + DEPTH < len(chunks):
            for copy in gate_up_copies(number + DEPTH):
                copy.start()
        if number == len(chunks) // 2:
            down_copy(1).start()
        if with_shared and number == len(chunks) - DEPTH:
            for copy in s_copies:
                copy.start()
        if low + size == FF_E:
            down_copy(expert).wait()
            for start in range(0, width, WIDE):
                lanes = slice(start, start + WIDE)
                result = jnp.dot(
                    hidden[...], down_held[expert, :, lanes], preferred_element_type=jnp.float32
                )
                picked[held, lanes] = (result * slot_weight[group, held]).astype(jnp.bfloat16)

    if with_shared:
        upper = place[1] % 2 == 1
        s_rows[0:ROWS] = rows[0:ROWS]
        s_rows[ROWS : 2 * ROWS] = rows[PIECE : PIECE + ROWS]
        base = pl.multiple_of(jnp.where(upper, 2, 5) * PIECE, PIECE)
        s_rows[2 * ROWS : 3 * ROWS] = rows[pl.ds(base, ROWS), :]
        s_rows[3 * ROWS : 4 * ROWS] = rows[pl.ds(base + PIECE, ROWS), :]
        for copy in s_copies:
            copy.wait()
        turned = (((1,), (1,)), ((), ()))
        units = s_gate.shape[0]
        for low in range(0, units, CHUNK):
            size = min(CHUNK, units - low)
            gate_val, up_val = [
                lax.dot_general(
                    s_rows[...], weight[low : low + size, :], turned, preferred_element_type=jnp.float32
                )
                for weight in (s_gate, s_up)
            ]
            s_hidden[:, low : low + size] = silu_times(gate_val, up_val)

    for low in range(0, width, CHUNK):
        lanes = slice(low, low + CHUNK)
        value = jnp.dot(spread[group], picked[:, lanes], preferred_element_type=jnp.float32)
        if with_shared:
            s_result = jnp.dot(s_hidden[...], s_down[:, lanes], preferred_element_type=jnp.float32)
        for part, target in enumerate(targets):
            mine = value[part * PIECE : (part + 1) * PIECE]
            if with_shared and part in (0, 1, 2, 3, 5, 6):
                if part < 2:
                    term = s_result[part * ROWS : (part + 1) * ROWS]
                else:
                    start = (2 + (part - 2) % 3) * ROWS
                    here = upper if part < 4 else jnp.logical_not(upper)
                    term = jnp.where(here, s_result[start : start + ROWS], 0.0)
                target[:ROWS, lanes] = (mine[:ROWS] + term).astype(jnp.bfloat16)
                target[ROWS:, lanes] = mine[ROWS:].astype(jnp.bfloat16)
            else:
                target[:, lanes] = mine.astype(jnp.bfloat16)


def experts(place, group, matrices, pieces, weights, shared):
    width = pieces[0].shape[1]
    hbm, vmem = whole(pl.ANY), whole()
    scratch = [
        pltpu.VMEM((GROUP_ROWS, width), jnp.bfloat16),
        pltpu.VMEM((2 * SLOTS, width), jnp.bfloat16),
        pltpu.VMEM((SLOTS, FF_E), jnp.bfloat16),
        pltpu.VMEM((DEPTH, width, CHUNK), jnp.bfloat16),
        pltpu.VMEM((DEPTH, width, CHUNK), jnp.bfloat16),
        pltpu.VMEM((2, FF_E, width), jnp.bfloat16),
        pltpu.SemaphoreType.DMA((PIECES,)),
        pltpu.SemaphoreType.DMA((DEPTH, 2)),
        pltpu.SemaphoreType.DMA((2,)),
    ]
    operands = [place, *matrices, *pieces, *weights]
    if shared is not None:
        operands += list(shared)
        scratch += [pltpu.VMEM(array.shape, array.dtype) for array in shared]
        scratch += [
            pltpu.SemaphoreType.DMA((3,)),
            pltpu.VMEM((BLOCK, width), jnp.bfloat16),
            pltpu.VMEM((BLOCK, shared[2].shape[0]), jnp.bfloat16),
        ]
    in_specs = [whole(pltpu.SMEM)] + [vmem] * 3
    in_specs += [hbm] * (len(operands) - len(in_specs))
    return pl.pallas_call(
        lambda *refs: experts_kernel(group, shared is not None, *refs),
        out_shape=(jax.ShapeDtypeStruct((PIECE, width), jnp.bfloat16),) * PIECES,
        in_specs=in_specs,
        out_specs=(vmem,) * PIECES,
        scratch_shapes=scratch,
        compiler_params=pltpu.CompilerParams(vmem_limit_bytes=SCOPED[shared is not None] * 2**20),
        cost_estimate=pl.CostEstimate(
            flops=10**10, bytes_accessed=44 * 10**6, transcendentals=10**6
        ),
    )(*operands)


SCOPED = {True: 50, False: 40}


def gather_plane(rows):
    mate = send(rows, CORE_SWAP)
    near = send(rows, X_THEN_Y)
    near_mate = send(mate, X_THEN_Y)
    corner = send(near, Y_THEN_X)
    fetched = (near, near_mate, corner)
    return (rows, mate, *fetched, *[send(piece, CORE_SWAP) for piece in fetched])


def sum_plane(own, mate, near, near_mate, corner, mate_near, mate_near_mate, mate_corner):
    corner = added(corner, send(mate_corner, CORE_SWAP))
    from_corner = send(corner, Y_THEN_X)
    near_mate = added(near_mate, send(mate_near_mate, CORE_SWAP))
    from_near_mate = send(near_mate, X_THEN_Y)
    near = near.astype(jnp.float32) + send(mate_near, CORE_SWAP).astype(jnp.float32)
    from_near = send(added(near, from_corner), X_THEN_Y)
    return (
        own.astype(jnp.float32)
        + send(mate, CORE_SWAP).astype(jnp.float32)
        + send(from_near_mate, CORE_SWAP).astype(jnp.float32)
        + from_near.astype(jnp.float32)
    )


def routing_tables(expert_ids, route_weight, place):
    count = expert_ids.shape[1]
    packed = jnp.concatenate([expert_ids.T.astype(jnp.float32), route_weight.T], axis=0)
    pair = jnp.stack([packed, send(packed, X_SWAP)])
    steps = [pair, send(pair, Z_ON), send(pair, Z_TWO), send(pair, Z_BACK)]
    slices = jnp.stack(steps).reshape(NZ, 2, 2 * count, 4, ROWS).transpose(0, 1, 3, 2, 4)
    slices = slices.reshape(-1, 2 * count, ROWS)
    order = lax.dynamic_index_in_dim(jnp.asarray(slice_order()), place[1], 0, keepdims=False)
    listed = slices[order.reshape(-1)].reshape(2, 16, 2 * count, ROWS)
    first_expert = 2 * (place[0] * 4 + place[1])
    local = (first_expert + lax.iota(jnp.int32, 2)).astype(jnp.float32)
    match = listed[:, None, :, :count] == local[None, :, None, None, None]
    hit = jnp.any(match, axis=3).reshape(2, 2, GROUP_ROWS)
    weight = jnp.sum(jnp.where(match, listed[:, None, :, count:], 0.0), axis=3)
    weight = weight.reshape(2, 2, GROUP_ROWS)
    ones = hit.astype(jnp.int32)
    slot = jnp.where(hit, jnp.cumsum(ones, axis=2) - 1, -1)
    return routing_matrices(slot.reshape(4, GROUP_ROWS), weight.reshape(4, GROUP_ROWS))


def block_pairs(target):
    pairs = []
    for z in range(NZ):
        for x in range(2):
            aim = target(z, x)
            if aim is not None and aim[0] < NZ:
                pairs.append((z * 2 + x, aim[0] * 2 + aim[1]))
    return pairs


def sliced_body(
    residual_in,
    queries,
    keys,
    values,
    segment_ids,
    out_proj,
    norm_gain,
    shared_gate,
    shared_up,
    shared_down,
    expert_gate,
    expert_up,
    expert_down,
    expert_ids,
    route_weight,
    block_table,
):
    tok_here = lax.axis_index("tok")
    hd_here = lax.axis_index("hd")
    place = jnp.stack([tok_here, hd_here]).astype(jnp.int32)
    own, kv_pages = write_pages(keys, values, block_table, place)

    def move(array, target):
        return lax.ppermute(array, "tok", block_pairs(target))

    near_z = move(own, lambda z, x: (z + 1, x))
    own_later, _ = lax.optimization_barrier((own, near_z))
    near_x = move(own_later, lambda z, x: (z, 1) if x == 0 else None)
    weights = (expert_gate, expert_up, expert_down)
    shared = (shared_gate.T, shared_up.T, shared_down)
    touched = touch((*weights, *shared), own)
    near_z, touched = lax.optimization_barrier((near_z, touched))
    cross = move(near_z, lambda z, x: (z, 1 - x))
    far = move(near_z, lambda z, x: (z + 1, x))
    far_cross = move(near_z, lambda z, x: (z + 1, 0) if x == 1 else None)

    tables = routing_tables(expert_ids, route_weight, place)
    query_segment = lax.dynamic_slice_in_dim(segment_ids, tok_here * BLOCK, BLOCK, 0)[:, None]
    sent, kept = attention(
        place, segment_ids, query_segment, queries, own, near_x, near_z, cross, far, far_cross, out_proj,
        (touched, touched),
    )
    kept = kept + send(sent, CORE_SWAP).astype(jnp.float32)
    resid_rows = (
        lax.dynamic_slice_in_dim(residual_in, hd_here * ROWS, ROWS, 0).astype(jnp.float32)
        + kept[:ROWS]
        + send(kept[ROWS:].astype(jnp.bfloat16), Y_SWAP).astype(jnp.float32)
    )
    normed = rms_normed(resid_rows, norm_gain)

    steps = [normed]
    for _ in range(3):
        steps.append(send(steps[-1], Z_ON))
    sums = []
    for group in range(2):
        gathered = gather_plane(jnp.concatenate(steps[2 * group : 2 * group + 2], axis=0))
        terms = experts(place, group, tables, gathered, weights, shared if group == 0 else None)
        sums.append(sum_plane(*terms))
    returned = [
        send(part.astype(jnp.bfloat16), pairs).astype(jnp.float32)
        for part, pairs in ((sums[0][ROWS:], Z_BACK), (sums[1][:ROWS], Z_TWO), (sums[1][ROWS:], Z_ON))
    ]
    output = resid_rows + sums[0][:ROWS] + returned[0] + returned[1] + returned[2]
    return (output.astype(jnp.bfloat16), kv_pages)


def solution(mesh):
    placed = (
        P("tok", None),
        P("tok", "hd"),
        P("tok", "hd"),
        P("tok", "hd"),
        P(),
        P("hd", None),
        P(),
        P(None, "hd"),
        P(None, "hd"),
        P("hd", None),
        P(None, ("tok", "hd")),
        P(None, ("tok", "hd")),
        P(("tok", "hd"), None),
        P("tok", None),
        P("tok", None),
        P("tok"),
    )
    return jax.shard_map(
        sliced_body if dict(mesh.shape) == {"tok": 2 * NZ, "hd": 4} else general_body,
        mesh=mesh,
        in_specs=placed,
        out_specs=(P(("tok", "hd"), None), P("tok", None, "hd")),
        check_vma=False,
    )
```

```python
import math

import jax
import jax.numpy as jnp
import numpy as np
from jax import lax
from jax.experimental import pallas as pl
from jax.experimental.pallas import tpu as pltpu
from jax.sharding import PartitionSpec as P

HD = 128
EXPERTS = 64
FF_E = 1408
PAGE = 16
CAP = 48


MASKED_SCORE = -1e30
NORM_EPSILON = 1e-06


def from_behind(array, axis, by):
    length = lax.axis_size(axis)
    pairs = [(i, i + by) for i in range(length) if 0 <= i + by < length]
    return lax.ppermute(array, axis, pairs)


def rms_normed(resid_state, norm_gain):
    mean_square = jnp.mean(resid_state * resid_state, axis=1, keepdims=True)
    return (resid_state * lax.rsqrt(mean_square + NORM_EPSILON) * norm_gain).astype(jnp.bfloat16)


def general_body(
    residual_in,
    queries,
    keys,
    values,
    segment_ids,
    out_proj,
    norm_gain,
    shared_gate,
    shared_up,
    shared_down,
    expert_gate,
    expert_up,
    expert_down,
    expert_ids,
    route_weight,
    block_table,
):
    block_len = residual_in.shape[0]
    model_width = residual_in.shape[1]
    tok_count = lax.axis_size("tok")
    hd_count = lax.axis_size("hd")
    tok_here = lax.axis_index("tok")
    hd_here = lax.axis_index("hd")
    heads_here = queries.shape[1] // HD
    query_three = queries.reshape(block_len, heads_here, HD)
    offsets = lax.iota(jnp.int32, block_len)
    query_pos = tok_here * block_len + offsets
    query_seg = lax.dynamic_slice_in_dim(segment_ids, tok_here * block_len, block_len, 0)

    def attend(carried, key_blk, value_blk, source):
        safe_source = jnp.maximum(source, 0)
        key_seg = lax.dynamic_slice_in_dim(segment_ids, safe_source * block_len, block_len, 0)
        key_pos = source * block_len + offsets

        def compute(current):
            running_max, denom_sum, weighted_sum = current
            scores = jnp.einsum(
                "qhd,khd->hqk",
                query_three,
                key_blk.reshape(block_len, heads_here, HD),
                preferred_element_type=jnp.float32,
            ) / math.sqrt(HD)
            allowed = (key_seg[None, :] == query_seg[:, None]) & (
                key_pos[None, :] <= query_pos[:, None]
            )
            scores = jnp.where(allowed[None], scores, MASKED_SCORE)
            new_max = jnp.maximum(running_max, jnp.max(scores, axis=2))
            shrink = jnp.exp(running_max - new_max)
            exp_scores = jnp.where(allowed[None], jnp.exp(scores - new_max[:, :, None]), 0.0)
            denom_sum = denom_sum * shrink + jnp.sum(exp_scores, axis=2)
            update = jnp.einsum(
                "hqk,khd->qhd",
                exp_scores.astype(jnp.bfloat16),
                value_blk.reshape(block_len, heads_here, HD),
                preferred_element_type=jnp.float32,
            )
            weighted_sum = weighted_sum * jnp.transpose(shrink)[:, :, None] + update
            return (new_max, denom_sum, weighted_sum)

        is_live = (source >= 0) & (
            segment_ids[safe_source * block_len + block_len - 1] >= query_seg[0]
        )
        return lax.cond(is_live, compute, lambda unchanged: unchanged, carried)

    initial = (
        jnp.full((heads_here, block_len), MASKED_SCORE, jnp.float32),
        jnp.zeros((heads_here, block_len), jnp.float32),
        jnp.zeros((block_len, heads_here, HD), jnp.float32),
    )
    carried = attend(initial, keys, values, tok_here)

    def relay(relay_step, loop_carry):
        moving, inner_state = loop_carry
        moving = from_behind(moving, "tok", 1)
        inner_state = attend(inner_state, moving[0], moving[1], tok_here - relay_step - 1)
        return (moving, inner_state)

    _, final_state = lax.fori_loop(0, tok_count // 2, relay, (jnp.stack([keys, values]), carried))
    weighted_sum = final_state[2]
    denom_sum = final_state[1]
    attended = (
        (weighted_sum / jnp.transpose(denom_sum)[:, :, None])
        .astype(jnp.bfloat16)
        .reshape(block_len, heads_here * HD)
    )
    row_count = block_len // hd_count
    row_start = hd_here * row_count
    head_terms = jnp.dot(attended, out_proj, preferred_element_type=jnp.float32)
    resid_full = residual_in.astype(jnp.float32) + lax.psum(
        head_terms.astype(jnp.bfloat16), "hd"
    ).astype(jnp.float32)
    normed = rms_normed(resid_full, norm_gain)
    resid_rows = lax.dynamic_slice_in_dim(resid_full, row_start, row_count, 0)
    shared_gate_val = jnp.dot(normed, shared_gate, preferred_element_type=jnp.float32)
    shared_up_val = jnp.dot(normed, shared_up, preferred_element_type=jnp.float32)
    shared_hidden = (jax.nn.silu(shared_gate_val) * shared_up_val).astype(jnp.bfloat16)
    partial_out = jnp.dot(shared_hidden, shared_down, preferred_element_type=jnp.float32)
    slice_width = expert_gate.shape[1]
    held_count = max(1, slice_width // FF_E)
    part_width = slice_width // held_count
    per_group = slice_width * hd_count // FF_E
    first_local = hd_here * slice_width // FF_E
    expert_range = lax.iota(jnp.int32, EXPERTS)
    onehot = jnp.sum(
        (expert_ids[:, :, None] == expert_range[None, None, :]).astype(jnp.int32), axis=1
    )
    earlier = jnp.cumsum(onehot, axis=0) - onehot
    slot_index = jnp.take_along_axis(earlier, expert_ids, axis=1)
    flat_expert = expert_ids.reshape(-1)
    flat_slot = slot_index.reshape(-1)
    row_source = jnp.repeat(offsets, expert_ids.shape[1])
    row_table = (
        jnp.full((EXPERTS, CAP), block_len, jnp.int32).at[flat_expert, flat_slot].set(row_source)
    )
    weight_table = (
        jnp.zeros((EXPERTS, CAP), jnp.float32)
        .at[flat_expert, flat_slot]
        .set(route_weight.reshape(-1))
    )
    send_rows = lax.dynamic_slice_in_dim(
        row_table.reshape(tok_count, per_group, CAP), first_local, held_count, 1
    )
    send_weight = lax.dynamic_slice_in_dim(
        weight_table.reshape(tok_count, per_group, CAP), first_local, held_count, 1
    )
    padded_rows = jnp.concatenate([normed, jnp.zeros((1, model_width), jnp.bfloat16)], axis=0)
    outgoing = padded_rows[send_rows]
    gate_three = expert_gate.reshape(model_width, held_count, part_width)
    up_three = expert_up.reshape(model_width, held_count, part_width)
    down_three = expert_down.reshape(held_count, part_width, model_width)
    incoming = lax.all_to_all(outgoing, "tok", split_axis=0, concat_axis=0, tiled=True)
    gate_val = jnp.einsum(
        "secd,def->secf", incoming, gate_three, preferred_element_type=jnp.float32
    )
    up_val = jnp.einsum("secd,def->secf", incoming, up_three, preferred_element_type=jnp.float32)
    hidden = (jax.nn.silu(gate_val) * up_val).astype(jnp.bfloat16)
    result = jnp.einsum(
        "secf,efd->secd", hidden, down_three, preferred_element_type=jnp.float32
    ).astype(jnp.bfloat16)
    returned_rows = lax.all_to_all(result, "tok", split_axis=0, concat_axis=0, tiled=True)
    weighted_rows = returned_rows.astype(jnp.float32) * send_weight[:, :, :, None]
    routed = (
        jnp.zeros((block_len + 1, model_width), jnp.float32)
        .at[send_rows.reshape(-1)]
        .add(weighted_rows.reshape(-1, model_width))[:block_len]
    )
    summed_rows = lax.psum_scatter(
        (partial_out + routed).astype(jnp.bfloat16), "hd", scatter_dimension=0, tiled=True
    ).astype(jnp.float32)
    output = (resid_rows + summed_rows).astype(jnp.bfloat16)
    page_count = block_len // PAGE
    page_data = jnp.stack(
        [keys.reshape(block_len, heads_here, HD), values.reshape(block_len, heads_here, HD)], axis=2
    )
    page_data = page_data.reshape(page_count, PAGE, heads_here * 2 * HD)
    local_pages = block_table - tok_here * page_count
    kv_pages = jnp.zeros_like(page_data).at[local_pages].set(page_data)
    return (output, kv_pages)


NZ = 4
BOTH = ("tok", "hd")
ROWS = 64
BLOCK = 256
GROUP_ROWS = 1024
SLOTS = 4 * CAP
NEXT_Z = {0: 1, 1: 3, 3: 2, 2: 0}
BACK_Z = {after: before for before, after in NEXT_Z.items()}
DEVICES = [(z, x, y, c) for z in range(NZ) for x in range(2) for y in range(2) for c in range(2)]


def flat_index(z, x, y, c):
    return (z * 2 + x) * 4 + y * 2 + c


def pairs_of(target):
    return [(flat_index(*device), flat_index(*target(*device))) for device in DEVICES]


Z_ON = pairs_of(lambda z, x, y, c: (NEXT_Z[z], x, y, c))
Z_BACK = pairs_of(lambda z, x, y, c: (BACK_Z[z], x, y, c))
Z_TWO = pairs_of(lambda z, x, y, c: (NEXT_Z[NEXT_Z[z]], x, y, c))
CORE_SWAP = pairs_of(lambda z, x, y, c: (z, x, y, 1 - c))
X_SWAP = pairs_of(lambda z, x, y, c: (z, 1 - x, y, c))
Y_SWAP = pairs_of(lambda z, x, y, c: (z, x, 1 - y, c))
X_THEN_Y = pairs_of(lambda z, x, y, c: (z, 1 - x, y, c) if c == 0 else (z, x, 1 - y, c))
Y_THEN_X = pairs_of(lambda z, x, y, c: (z, x, 1 - y, c) if c == 0 else (z, 1 - x, y, c))


def slice_order():
    order = np.zeros((len(DEVICES), 32), np.int32)
    for z, x, y, c in DEVICES:
        at_step = [z]
        for _ in range(3):
            at_step.append(BACK_Z[at_step[-1]])
        mine = {
            0: [(1 - x, y, 0), (1 - x, y, 1), (1 - x, 1 - y, 0)],
            1: [(x, 1 - y, 1), (x, 1 - y, 0), (1 - x, 1 - y, 1)],
        }
        places = [(x, y, c), (x, y, 1 - c)] + mine[c] + mine[1 - c]
        order[flat_index(z, x, y, c)] = [
            flat_index(at_step[2 * group + part], *place)
            for group in range(2)
            for place in places
            for part in range(2)
        ]
    return order


def send(array, pairs):
    return lax.ppermute(array, BOTH, pairs)


def added(first, second):
    return (first.astype(jnp.float32) + second.astype(jnp.float32)).astype(jnp.bfloat16)


def whole(space=pltpu.VMEM):
    return pl.BlockSpec(memory_space=space)


def pages_kernel(table, place, keys, values, joined, pages):
    heads = keys.shape[1] // HD
    for head in range(heads):
        lanes = slice(head * HD, (head + 1) * HD)
        joined[:, 2 * head * HD : (2 * head + 1) * HD] = keys[:, lanes]
        joined[:, (2 * head + 1) * HD : (2 * head + 2) * HD] = values[:, lanes]
    for page in range(keys.shape[0] // PAGE):
        pages[table[page] - place[0] * (keys.shape[0] // PAGE)] = joined[page * PAGE : (page + 1) * PAGE, :]


def write_pages(keys, values, block_table, place):
    rows, width = keys.shape
    return pl.pallas_call(
        pages_kernel,
        out_shape=(
            jax.ShapeDtypeStruct((rows, 2 * width), keys.dtype),
            jax.ShapeDtypeStruct((rows // PAGE, PAGE, 2 * width), keys.dtype),
        ),
        in_specs=[whole(pltpu.SMEM), whole(pltpu.SMEM), whole(), whole()],
        out_specs=(whole(), whole()),
    )(block_table, place, keys, values)


HEADS_HERE = 4


def attend(place, segments, query_segment, queries, blocks):
    offsets = lax.broadcasted_iota(jnp.int32, (1, BLOCK), 1)
    key_segment, key_place = [], []
    for _, source in blocks:
        line = segments[pl.ds(jnp.maximum(source, 0), 1), :]
        key_segment.append(jnp.where(source >= 0, line, -1))
        key_place.append(source * BLOCK + offsets)
    query_place = place[0] * BLOCK + lax.broadcasted_iota(jnp.int32, (BLOCK, 1), 0)
    allowed = (jnp.concatenate(key_segment, axis=1) == query_segment[...]) & (
        jnp.concatenate(key_place, axis=1) <= query_place
    )
    results = []
    for head in range(HEADS_HERE):
        key, value = [
            jnp.concatenate(
                [block[:, (2 * head + part) * HD : (2 * head + part + 1) * HD] for block, _ in blocks], axis=0
            )
            for part in range(2)
        ]
        scores = lax.dot_general(
            queries[:, head * HD : (head + 1) * HD],
            key,
            (((1,), (1,)), ((), ())),
            preferred_element_type=jnp.float32,
        ) * (1.0 / math.sqrt(HD))
        scores = jnp.where(allowed, scores, MASKED_SCORE)
        largest = jnp.max(scores, axis=1, keepdims=True)
        exp_scores = jnp.where(allowed, jnp.exp(scores - largest), 0.0)
        mixed = jnp.dot(exp_scores.astype(jnp.bfloat16), value, preferred_element_type=jnp.float32)
        results.append((largest, jnp.sum(exp_scores, axis=1, keepdims=True), mixed))
    return results


def attention_first(
    place, segments, query_segment, queries, own, near_x, near_z, top, total, mixed
):
    here = place[0]
    blocks = [(own, here), (near_x, jnp.where(here % 2 == 1, here - 1, -1)), (near_z, here - 2)]
    results = attend(place, segments, query_segment, queries, blocks)
    top[...] = jnp.concatenate([result[0] for result in results], axis=1)
    total[...] = jnp.concatenate([result[1] for result in results], axis=1)
    for head in range(HEADS_HERE):
        mixed[head] = results[head][2]


def attention_second(
    place, segments, query_segment, queries, cross, far, far_cross, projection,
    top, total, mixed, sent, kept, attended,
):
    here, hd = place[0], place[1]
    odd = here % 2
    blocks = [
        (cross, jnp.where(odd == 1, here - 3, here - 1)),
        (far, here - 4),
        (far_cross, jnp.where(odd == 1, -1, here - 3)),
    ]
    results = attend(place, segments, query_segment, queries, blocks)
    for head, (largest, added_up, update) in enumerate(results):
        before = top[:, head : head + 1]
        both = jnp.maximum(before, largest)
        old, new = jnp.exp(before - both), jnp.exp(largest - both)
        denom = total[:, head : head + 1] * old + added_up * new
        attended[:, head * HD : (head + 1) * HD] = (
            (mixed[head] * old + update * new) / denom
        ).astype(jnp.bfloat16)
    mate, across = hd ^ 1, hd ^ 2

    def rows_of(first, second):
        return jnp.concatenate(
            [
                attended[pl.ds(pl.multiple_of(quarter * ROWS, ROWS), ROWS), :]
                for quarter in (first, second)
            ],
            axis=0,
        )

    sent[...] = jnp.dot(
        rows_of(mate, mate ^ 2), projection[...], preferred_element_type=jnp.float32
    ).astype(jnp.bfloat16)
    kept[...] = jnp.dot(rows_of(hd, across), projection[...], preferred_element_type=jnp.float32)


def attention(
    place, segment_ids, query_segment, queries, own, near_x, near_z, cross, far, far_cross, out_proj
):
    segments = segment_ids.reshape(-1, BLOCK)
    state = (
        jax.ShapeDtypeStruct((BLOCK, HEADS_HERE), jnp.float32),
        jax.ShapeDtypeStruct((BLOCK, HEADS_HERE), jnp.float32),
        jax.ShapeDtypeStruct((HEADS_HERE, BLOCK, HD), jnp.float32),
    )
    smem, vmem = whole(pltpu.SMEM), whole()
    limit = pltpu.CompilerParams(vmem_limit_bytes=24 * 2**20)
    first = pl.pallas_call(
        attention_first,
        out_shape=state,
        in_specs=[smem] + [vmem] * 6,
        out_specs=(vmem, vmem, vmem),
        compiler_params=limit,
        cost_estimate=pl.CostEstimate(flops=8 * 10**8, bytes_accessed=4 * 10**6, transcendentals=8 * 10**5),
    )(place, segments, query_segment, queries, own, near_x, near_z)
    return pl.pallas_call(
        attention_second,
        out_shape=(
            jax.ShapeDtypeStruct((2 * ROWS, out_proj.shape[1]), jnp.bfloat16),
            jax.ShapeDtypeStruct((2 * ROWS, out_proj.shape[1]), jnp.float32),
        ),
        in_specs=[smem] + [vmem] * 10,
        out_specs=(vmem, vmem),
        scratch_shapes=[pltpu.VMEM((BLOCK, HEADS_HERE * HD), jnp.bfloat16)],
        compiler_params=limit,
        cost_estimate=pl.CostEstimate(flops=10**9, bytes_accessed=6 * 10**6, transcendentals=8 * 10**5),
    )(
        place, segments, query_segment, queries, cross, far, far_cross, out_proj, *first
    )


CHUNK = 256
WIDE = 512
PIECE = 2 * ROWS
PIECES = 8
DEPTH = 3


def silu_times(gate_val, up_val):
    return (gate_val / (1.0 + jnp.exp(-gate_val)) * up_val).astype(jnp.bfloat16)


def routing_kernel(place, order, slices, pick, spread, slot_weight, listed):
    count = slices.shape[1] // 2
    for number in range(32):
        listed[:, number * ROWS : (number + 1) * ROWS] = slices[order[number]]
    first_expert = (2 * (place[0] * 4 + place[1])).astype(jnp.float32)
    hits, weights = [], []
    for group in range(2):
        lanes = slice(group * GROUP_ROWS, (group + 1) * GROUP_ROWS)
        for expert in range(2):
            match = listed[:count, lanes] == first_expert + float(expert)
            hits.append(jnp.max(jnp.where(match, 1.0, 0.0), axis=0, keepdims=True))
            weights.append(jnp.sum(jnp.where(match, listed[count:, lanes], 0.0), axis=0, keepdims=True))
    hits = jnp.concatenate(hits + hits, axis=0)
    earlier = lax.broadcasted_iota(jnp.int32, (GROUP_ROWS, GROUP_ROWS), 0) < lax.broadcasted_iota(
        jnp.int32, (GROUP_ROWS, GROUP_ROWS), 1
    )
    before = jnp.dot(
        hits.astype(jnp.bfloat16),
        jnp.where(earlier, 1.0, 0.0).astype(jnp.bfloat16),
        preferred_element_type=jnp.float32,
    )
    slot = jnp.where(hits > 0.0, before, -1.0)
    slot_column = slot.T
    slot_numbers = lax.broadcasted_iota(jnp.int32, (SLOTS, GROUP_ROWS), 0).astype(jnp.float32)
    slot_lanes = lax.broadcasted_iota(jnp.int32, (GROUP_ROWS, 2 * SLOTS), 1).astype(jnp.float32)
    for group in range(2):
        for expert in range(2):
            line = 2 * group + expert
            held = slice(expert * SLOTS, (expert + 1) * SLOTS)
            hit = slot[line : line + 1] == slot_numbers
            pick[group, held] = jnp.where(hit, 1.0, 0.0).astype(jnp.bfloat16)
            slot_weight[group, held] = jnp.sum(jnp.where(hit, weights[line], 0.0), axis=1, keepdims=True)
        first, second = [slot_column[:, 2 * group + e : 2 * group + e + 1] for e in range(2)]
        hit = (first == slot_lanes) | ((second >= 0.0) & (second + float(SLOTS) == slot_lanes))
        spread[group] = jnp.where(hit, 1.0, 0.0).astype(jnp.bfloat16)


def experts_kernel(*refs):
    place, pick, spread, slot_weight = refs[:4]
    pieces, refs = refs[4 : 4 + 2 * PIECES], refs[4 + 2 * PIECES :]
    gate, up, down = refs[:3]
    shared = refs[3:6]
    targets, refs = refs[6 : 6 + 2 * PIECES], refs[6 + 2 * PIECES :]
    rows, picked, hidden, gate_held, up_held, down_held, arrived, gate_up_arrived, down_arrived = refs[:9]
    width = rows.shape[1]
    chunks = [
        (expert, low, min(CHUNK, FF_E - low)) for expert in range(2) for low in range(0, FF_E, CHUNK)
    ]

    def gate_up_copies(number):
        expert, low, size = chunks[number]
        lanes, slot = pl.ds(expert * FF_E + low, size), number % DEPTH
        return [
            pltpu.make_async_copy(
                source.at[:, lanes], held.at[slot, :, pl.ds(0, size)], gate_up_arrived.at[slot, which]
            )
            for which, (source, held) in enumerate(((gate, gate_held), (up, up_held)))
        ]

    def down_copy(expert):
        return pltpu.make_async_copy(
            down.at[pl.ds(expert * FF_E, FF_E), :], down_held.at[expert], down_arrived.at[expert]
        )

    copies = [
        pltpu.make_async_copy(piece, rows.at[pl.ds(number * PIECE, PIECE), :], arrived.at[number])
        for number, piece in enumerate(pieces)
    ]
    for copy in copies:
        copy.start()
    for number in range(DEPTH):
        for copy in gate_up_copies(number):
            copy.start()
    down_copy(0).start()
    s_gate, s_up, s_down, s_arrived, s_rows, s_hidden = refs[9:]
    s_copies = [
        pltpu.make_async_copy(source, target, s_arrived.at[number])
        for number, (source, target) in enumerate(zip(shared, (s_gate, s_up, s_down)))
    ]

    def slots(expert, group):
        return slice((2 * expert + group) * SLOTS, (2 * expert + group + 1) * SLOTS)

    for group in range(2):
        for copy in copies[group * PIECES : (group + 1) * PIECES]:
            copy.wait()
        for low in range(0, width, WIDE):
            lanes = slice(low, low + WIDE)
            both = jnp.dot(
                pick[group],
                rows[group * GROUP_ROWS : (group + 1) * GROUP_ROWS, lanes],
                preferred_element_type=jnp.float32,
            ).astype(jnp.bfloat16)
            for expert in range(2):
                picked[slots(expert, group), lanes] = both[expert * SLOTS : (expert + 1) * SLOTS]
    for number, (expert, low, size) in enumerate(chunks):
        held, slot = slice(2 * expert * SLOTS, 2 * (expert + 1) * SLOTS), number % DEPTH
        for copy in gate_up_copies(number):
            copy.wait()
        gate_val = jnp.dot(picked[held], gate_held[slot, :, :size], preferred_element_type=jnp.float32)
        up_val = jnp.dot(picked[held], up_held[slot, :, :size], preferred_element_type=jnp.float32)
        hidden[:, low : low + size] = silu_times(gate_val, up_val)
        if number + DEPTH < len(chunks):
            for copy in gate_up_copies(number + DEPTH):
                copy.start()
        if number == len(chunks) // 2:
            down_copy(1).start()
        if number == len(chunks) - DEPTH:
            for copy in s_copies:
                copy.start()
        if low + size == FF_E:
            down_copy(expert).wait()
            scale = jnp.concatenate(
                [slot_weight[group, expert * SLOTS : (expert + 1) * SLOTS] for group in range(2)], axis=0
            )
            for start in range(0, width, WIDE):
                lanes = slice(start, start + WIDE)
                result = jnp.dot(
                    hidden[...], down_held[expert, :, lanes], preferred_element_type=jnp.float32
                )
                picked[held, lanes] = (result * scale).astype(jnp.bfloat16)

    upper = place[1] % 2 == 1
    s_rows[0:ROWS] = rows[0:ROWS]
    s_rows[ROWS : 2 * ROWS] = rows[PIECE : PIECE + ROWS]
    base = pl.multiple_of(jnp.where(upper, 2, 5) * PIECE, PIECE)
    s_rows[2 * ROWS : 3 * ROWS] = rows[pl.ds(base, ROWS), :]
    s_rows[3 * ROWS : 4 * ROWS] = rows[pl.ds(base + PIECE, ROWS), :]
    for copy in s_copies:
        copy.wait()
    turned = (((1,), (1,)), ((), ()))
    units = s_gate.shape[0]
    for low in range(0, units, CHUNK):
        size = min(CHUNK, units - low)
        gate_val, up_val = [
            lax.dot_general(
                s_rows[...], weight[low : low + size, :], turned, preferred_element_type=jnp.float32
            )
            for weight in (s_gate, s_up)
        ]
        s_hidden[:, low : low + size] = silu_times(gate_val, up_val)

    for low in range(0, width, CHUNK):
        lanes = slice(low, low + CHUNK)
        s_result = jnp.dot(s_hidden[...], s_down[:, lanes], preferred_element_type=jnp.float32)
        for group in range(2):
            value = jnp.dot(
                spread[group],
                jnp.concatenate([picked[slots(expert, group), lanes] for expert in range(2)], axis=0),
                preferred_element_type=jnp.float32,
            )
            for part, target in enumerate(targets[group * PIECES : (group + 1) * PIECES]):
                mine = value[part * PIECE : (part + 1) * PIECE]
                if group == 0 and part in (0, 1, 2, 3, 5, 6):
                    if part < 2:
                        term = s_result[part * ROWS : (part + 1) * ROWS]
                    else:
                        start = (2 + (part - 2) % 3) * ROWS
                        here = upper if part < 4 else jnp.logical_not(upper)
                        term = jnp.where(here, s_result[start : start + ROWS], 0.0)
                    target[:ROWS, lanes] = (mine[:ROWS] + term).astype(jnp.bfloat16)
                    target[ROWS:, lanes] = mine[ROWS:].astype(jnp.bfloat16)
                else:
                    target[:, lanes] = mine.astype(jnp.bfloat16)


def experts(place, matrices, pieces, weights, shared):
    width = pieces[0].shape[1]
    hbm, vmem = whole(pl.ANY), whole()
    scratch = [
        pltpu.VMEM((2 * GROUP_ROWS, width), jnp.bfloat16),
        pltpu.VMEM((4 * SLOTS, width), jnp.bfloat16),
        pltpu.VMEM((2 * SLOTS, FF_E), jnp.bfloat16),
        pltpu.VMEM((DEPTH, width, CHUNK), jnp.bfloat16),
        pltpu.VMEM((DEPTH, width, CHUNK), jnp.bfloat16),
        pltpu.VMEM((2, FF_E, width), jnp.bfloat16),
        pltpu.SemaphoreType.DMA((2 * PIECES,)),
        pltpu.SemaphoreType.DMA((DEPTH, 2)),
        pltpu.SemaphoreType.DMA((2,)),
        *[pltpu.VMEM(array.shape, array.dtype) for array in shared],
        pltpu.SemaphoreType.DMA((3,)),
        pltpu.VMEM((BLOCK, width), jnp.bfloat16),
        pltpu.VMEM((BLOCK, shared[2].shape[0]), jnp.bfloat16),
    ]
    operands = [place, *matrices, *pieces, *weights, *shared]
    in_specs = [whole(pltpu.SMEM)] + [vmem] * 3
    in_specs += [hbm] * (len(operands) - len(in_specs))
    return pl.pallas_call(
        experts_kernel,
        out_shape=(jax.ShapeDtypeStruct((PIECE, width), jnp.bfloat16),) * (2 * PIECES),
        in_specs=in_specs,
        out_specs=(vmem,) * (2 * PIECES),
        scratch_shapes=scratch,
        compiler_params=pltpu.CompilerParams(vmem_limit_bytes=60 * 2**20),
        cost_estimate=pl.CostEstimate(
            flops=2 * 10**10, bytes_accessed=60 * 10**6, transcendentals=2 * 10**6
        ),
    )(*operands)


def gather_plane(rows):
    mate = send(rows, CORE_SWAP)
    near = send(rows, X_THEN_Y)
    near_mate = send(mate, X_THEN_Y)
    corner = send(near, Y_THEN_X)
    fetched = (near, near_mate, corner)
    return (rows, mate, *fetched, *[send(piece, CORE_SWAP) for piece in fetched])


def sum_plane(own, mate, near, near_mate, corner, mate_near, mate_near_mate, mate_corner):
    corner = added(corner, send(mate_corner, CORE_SWAP))
    from_corner = send(corner, Y_THEN_X)
    near_mate = added(near_mate, send(mate_near_mate, CORE_SWAP))
    from_near_mate = send(near_mate, X_THEN_Y)
    near = near.astype(jnp.float32) + send(mate_near, CORE_SWAP).astype(jnp.float32)
    from_near = send(added(near, from_corner), X_THEN_Y)
    return (
        own.astype(jnp.float32)
        + send(mate, CORE_SWAP).astype(jnp.float32)
        + send(from_near_mate, CORE_SWAP).astype(jnp.float32)
        + from_near.astype(jnp.float32)
    )


def routing_slices(expert_ids, route_weight):
    packed = jnp.concatenate([expert_ids.T.astype(jnp.float32), route_weight.T], axis=0)
    packed = packed.reshape(-1, 4, ROWS).transpose(1, 0, 2)
    blocks = 2 * NZ
    slices = lax.all_to_all(
        jnp.broadcast_to(packed[None], (blocks, *packed.shape)), "tok", split_axis=0, concat_axis=0, tiled=True
    ).reshape(-1, *packed.shape[1:])
    return slices


def routing_tables(slices, place, device):
    order = lax.dynamic_index_in_dim(jnp.asarray(slice_order()), device, 0, keepdims=False)
    return pl.pallas_call(
        routing_kernel,
        out_shape=(
            jax.ShapeDtypeStruct((2, 2 * SLOTS, GROUP_ROWS), jnp.bfloat16),
            jax.ShapeDtypeStruct((2, GROUP_ROWS, 2 * SLOTS), jnp.bfloat16),
            jax.ShapeDtypeStruct((2, 2 * SLOTS, 1), jnp.float32),
        ),
        in_specs=[whole(pltpu.SMEM), whole(pltpu.SMEM), whole()],
        out_specs=(whole(),) * 3,
        scratch_shapes=[pltpu.VMEM((slices.shape[1], 2 * GROUP_ROWS), jnp.float32)],
        compiler_params=pltpu.CompilerParams(vmem_limit_bytes=24 * 2**20),
    )(place, order, slices)


def block_pairs(target):
    pairs = []
    for z in range(NZ):
        for x in range(2):
            aim = target(z, x)
            if aim is not None and aim[0] < NZ:
                pairs.append((z * 2 + x, aim[0] * 2 + aim[1]))
    return pairs


def sliced_body(
    residual_in,
    queries,
    keys,
    values,
    segment_ids,
    out_proj,
    norm_gain,
    shared_gate,
    shared_up,
    shared_down,
    expert_gate,
    expert_up,
    expert_down,
    expert_ids,
    route_weight,
    block_table,
):
    tok_here = lax.axis_index("tok")
    hd_here = lax.axis_index("hd")
    place = jnp.stack([tok_here, hd_here]).astype(jnp.int32)
    own, kv_pages = write_pages(keys, values, block_table, place)

    def move(array, target):
        return lax.ppermute(array, "tok", block_pairs(target))

    near_z = move(own, lambda z, x: (z + 1, x))
    own_later, _ = lax.optimization_barrier((own, near_z))
    near_x = move(own_later, lambda z, x: (z, 1) if x == 0 else None)
    weights = (expert_gate, expert_up, expert_down)
    shared = (shared_gate.T, shared_up.T, shared_down)
    near_z, slices = lax.optimization_barrier((near_z, routing_slices(expert_ids, route_weight)))
    cross = move(near_z, lambda z, x: (z, 1 - x))
    far = move(near_z, lambda z, x: (z + 1, x))
    far_cross = move(near_z, lambda z, x: (z + 1, 0) if x == 1 else None)

    tables = routing_tables(slices, place, tok_here * 4 + hd_here)
    query_segment = lax.dynamic_slice_in_dim(segment_ids, tok_here * BLOCK, BLOCK, 0)[:, None]
    queries, tables = lax.optimization_barrier((queries, tables))
    sent, kept = attention(
        place, segment_ids, query_segment, queries, own, near_x, near_z, cross, far, far_cross, out_proj
    )
    kept = kept + send(sent, CORE_SWAP).astype(jnp.float32)
    resid_rows = (
        lax.dynamic_slice_in_dim(residual_in, hd_here * ROWS, ROWS, 0).astype(jnp.float32)
        + kept[:ROWS]
        + send(kept[ROWS:].astype(jnp.bfloat16), Y_SWAP).astype(jnp.float32)
    )
    normed = rms_normed(resid_rows, norm_gain)

    steps = [normed]
    for _ in range(3):
        steps.append(send(steps[-1], Z_ON))
    pieces = []
    for group in range(2):
        pieces += gather_plane(jnp.concatenate(steps[2 * group : 2 * group + 2], axis=0))
    terms = experts(place, tables, pieces, weights, shared)
    sums = [sum_plane(*terms[group * PIECES : (group + 1) * PIECES]) for group in range(2)]
    returned = [
        send(part.astype(jnp.bfloat16), pairs).astype(jnp.float32)
        for part, pairs in ((sums[0][ROWS:], Z_BACK), (sums[1][:ROWS], Z_TWO), (sums[1][ROWS:], Z_ON))
    ]
    output = resid_rows + sums[0][:ROWS] + returned[0] + returned[1] + returned[2]
    return (output.astype(jnp.bfloat16), kv_pages)


def solution(mesh):
    placed = (
        P("tok", None),
        P("tok", "hd"),
        P("tok", "hd"),
        P("tok", "hd"),
        P(),
        P("hd", None),
        P(),
        P(None, "hd"),
        P(None, "hd"),
        P("hd", None),
        P(None, ("tok", "hd")),
        P(None, ("tok", "hd")),
        P(("tok", "hd"), None),
        P("tok", None),
        P("tok", None),
        P("tok"),
    )
    return jax.shard_map(
        sliced_body if dict(mesh.shape) == {"tok": 2 * NZ, "hd": 4} else general_body,
        mesh=mesh,
        in_specs=placed,
        out_specs=(P(("tok", "hd"), None), P("tok", None, "hd")),
        check_vma=False,
    )
```

```python
import math

import jax
import jax.numpy as jnp
import numpy as np
from jax import lax
from jax.experimental import pallas as pl
from jax.experimental.pallas import tpu as pltpu
from jax.sharding import PartitionSpec as P

HD = 128
EXPERTS = 64
FF_E = 1408
PAGE = 16
CAP = 48


MASKED_SCORE = -1e30
NORM_EPSILON = 1e-06


def from_behind(array, axis, by):
    length = lax.axis_size(axis)
    pairs = [(i, i + by) for i in range(length) if 0 <= i + by < length]
    return lax.ppermute(array, axis, pairs)


def rms_normed(resid_state, norm_gain):
    mean_square = jnp.mean(resid_state * resid_state, axis=1, keepdims=True)
    return (resid_state * lax.rsqrt(mean_square + NORM_EPSILON) * norm_gain).astype(jnp.bfloat16)


def general_body(
    residual_in,
    queries,
    keys,
    values,
    segment_ids,
    out_proj,
    norm_gain,
    shared_gate,
    shared_up,
    shared_down,
    expert_gate,
    expert_up,
    expert_down,
    expert_ids,
    route_weight,
    block_table,
):
    block_len = residual_in.shape[0]
    model_width = residual_in.shape[1]
    tok_count = lax.axis_size("tok")
    hd_count = lax.axis_size("hd")
    tok_here = lax.axis_index("tok")
    hd_here = lax.axis_index("hd")
    heads_here = queries.shape[1] // HD
    query_three = queries.reshape(block_len, heads_here, HD)
    offsets = lax.iota(jnp.int32, block_len)
    query_pos = tok_here * block_len + offsets
    query_seg = lax.dynamic_slice_in_dim(segment_ids, tok_here * block_len, block_len, 0)

    def attend(carried, key_blk, value_blk, source):
        safe_source = jnp.maximum(source, 0)
        key_seg = lax.dynamic_slice_in_dim(segment_ids, safe_source * block_len, block_len, 0)
        key_pos = source * block_len + offsets

        def compute(current):
            running_max, denom_sum, weighted_sum = current
            scores = jnp.einsum(
                "qhd,khd->hqk",
                query_three,
                key_blk.reshape(block_len, heads_here, HD),
                preferred_element_type=jnp.float32,
            ) / math.sqrt(HD)
            allowed = (key_seg[None, :] == query_seg[:, None]) & (
                key_pos[None, :] <= query_pos[:, None]
            )
            scores = jnp.where(allowed[None], scores, MASKED_SCORE)
            new_max = jnp.maximum(running_max, jnp.max(scores, axis=2))
            shrink = jnp.exp(running_max - new_max)
            exp_scores = jnp.where(allowed[None], jnp.exp(scores - new_max[:, :, None]), 0.0)
            denom_sum = denom_sum * shrink + jnp.sum(exp_scores, axis=2)
            update = jnp.einsum(
                "hqk,khd->qhd",
                exp_scores.astype(jnp.bfloat16),
                value_blk.reshape(block_len, heads_here, HD),
                preferred_element_type=jnp.float32,
            )
            weighted_sum = weighted_sum * jnp.transpose(shrink)[:, :, None] + update
            return (new_max, denom_sum, weighted_sum)

        is_live = (source >= 0) & (
            segment_ids[safe_source * block_len + block_len - 1] >= query_seg[0]
        )
        return lax.cond(is_live, compute, lambda unchanged: unchanged, carried)

    initial = (
        jnp.full((heads_here, block_len), MASKED_SCORE, jnp.float32),
        jnp.zeros((heads_here, block_len), jnp.float32),
        jnp.zeros((block_len, heads_here, HD), jnp.float32),
    )
    carried = attend(initial, keys, values, tok_here)

    def relay(relay_step, loop_carry):
        moving, inner_state = loop_carry
        moving = from_behind(moving, "tok", 1)
        inner_state = attend(inner_state, moving[0], moving[1], tok_here - relay_step - 1)
        return (moving, inner_state)

    _, final_state = lax.fori_loop(0, tok_count // 2, relay, (jnp.stack([keys, values]), carried))
    weighted_sum = final_state[2]
    denom_sum = final_state[1]
    attended = (
        (weighted_sum / jnp.transpose(denom_sum)[:, :, None])
        .astype(jnp.bfloat16)
        .reshape(block_len, heads_here * HD)
    )
    row_count = block_len // hd_count
    row_start = hd_here * row_count
    head_terms = jnp.dot(attended, out_proj, preferred_element_type=jnp.float32)
    resid_full = residual_in.astype(jnp.float32) + lax.psum(
        head_terms.astype(jnp.bfloat16), "hd"
    ).astype(jnp.float32)
    normed = rms_normed(resid_full, norm_gain)
    resid_rows = lax.dynamic_slice_in_dim(resid_full, row_start, row_count, 0)
    shared_gate_val = jnp.dot(normed, shared_gate, preferred_element_type=jnp.float32)
    shared_up_val = jnp.dot(normed, shared_up, preferred_element_type=jnp.float32)
    shared_hidden = (jax.nn.silu(shared_gate_val) * shared_up_val).astype(jnp.bfloat16)
    partial_out = jnp.dot(shared_hidden, shared_down, preferred_element_type=jnp.float32)
    slice_width = expert_gate.shape[1]
    held_count = max(1, slice_width // FF_E)
    part_width = slice_width // held_count
    per_group = slice_width * hd_count // FF_E
    first_local = hd_here * slice_width // FF_E
    expert_range = lax.iota(jnp.int32, EXPERTS)
    onehot = jnp.sum(
        (expert_ids[:, :, None] == expert_range[None, None, :]).astype(jnp.int32), axis=1
    )
    earlier = jnp.cumsum(onehot, axis=0) - onehot
    slot_index = jnp.take_along_axis(earlier, expert_ids, axis=1)
    flat_expert = expert_ids.reshape(-1)
    flat_slot = slot_index.reshape(-1)
    row_source = jnp.repeat(offsets, expert_ids.shape[1])
    row_table = (
        jnp.full((EXPERTS, CAP), block_len, jnp.int32).at[flat_expert, flat_slot].set(row_source)
    )
    weight_table = (
        jnp.zeros((EXPERTS, CAP), jnp.float32)
        .at[flat_expert, flat_slot]
        .set(route_weight.reshape(-1))
    )
    send_rows = lax.dynamic_slice_in_dim(
        row_table.reshape(tok_count, per_group, CAP), first_local, held_count, 1
    )
    send_weight = lax.dynamic_slice_in_dim(
        weight_table.reshape(tok_count, per_group, CAP), first_local, held_count, 1
    )
    padded_rows = jnp.concatenate([normed, jnp.zeros((1, model_width), jnp.bfloat16)], axis=0)
    outgoing = padded_rows[send_rows]
    gate_three = expert_gate.reshape(model_width, held_count, part_width)
    up_three = expert_up.reshape(model_width, held_count, part_width)
    down_three = expert_down.reshape(held_count, part_width, model_width)
    incoming = lax.all_to_all(outgoing, "tok", split_axis=0, concat_axis=0, tiled=True)
    gate_val = jnp.einsum(
        "secd,def->secf", incoming, gate_three, preferred_element_type=jnp.float32
    )
    up_val = jnp.einsum("secd,def->secf", incoming, up_three, preferred_element_type=jnp.float32)
    hidden = (jax.nn.silu(gate_val) * up_val).astype(jnp.bfloat16)
    result = jnp.einsum(
        "secf,efd->secd", hidden, down_three, preferred_element_type=jnp.float32
    ).astype(jnp.bfloat16)
    returned_rows = lax.all_to_all(result, "tok", split_axis=0, concat_axis=0, tiled=True)
    weighted_rows = returned_rows.astype(jnp.float32) * send_weight[:, :, :, None]
    routed = (
        jnp.zeros((block_len + 1, model_width), jnp.float32)
        .at[send_rows.reshape(-1)]
        .add(weighted_rows.reshape(-1, model_width))[:block_len]
    )
    summed_rows = lax.psum_scatter(
        (partial_out + routed).astype(jnp.bfloat16), "hd", scatter_dimension=0, tiled=True
    ).astype(jnp.float32)
    output = (resid_rows + summed_rows).astype(jnp.bfloat16)
    page_count = block_len // PAGE
    page_data = jnp.stack(
        [keys.reshape(block_len, heads_here, HD), values.reshape(block_len, heads_here, HD)], axis=2
    )
    page_data = page_data.reshape(page_count, PAGE, heads_here * 2 * HD)
    local_pages = block_table - tok_here * page_count
    kv_pages = jnp.zeros_like(page_data).at[local_pages].set(page_data)
    return (output, kv_pages)


NZ = 4
BOTH = ("tok", "hd")
ROWS = 64
BLOCK = 256
GROUP_ROWS = 1024
SLOTS = 4 * CAP
NEXT_Z = {0: 1, 1: 3, 3: 2, 2: 0}
BACK_Z = {after: before for before, after in NEXT_Z.items()}
DEVICES = [(z, x, y, c) for z in range(NZ) for x in range(2) for y in range(2) for c in range(2)]


def flat_index(z, x, y, c):
    return (z * 2 + x) * 4 + y * 2 + c


def pairs_of(target):
    return [(flat_index(*device), flat_index(*target(*device))) for device in DEVICES]


Z_ON = pairs_of(lambda z, x, y, c: (NEXT_Z[z], x, y, c))
Z_BACK = pairs_of(lambda z, x, y, c: (BACK_Z[z], x, y, c))
Z_TWO = pairs_of(lambda z, x, y, c: (NEXT_Z[NEXT_Z[z]], x, y, c))
CORE_SWAP = pairs_of(lambda z, x, y, c: (z, x, y, 1 - c))
X_SWAP = pairs_of(lambda z, x, y, c: (z, 1 - x, y, c))
Y_SWAP = pairs_of(lambda z, x, y, c: (z, x, 1 - y, c))
X_THEN_Y = pairs_of(lambda z, x, y, c: (z, 1 - x, y, c) if c == 0 else (z, x, 1 - y, c))
Y_THEN_X = pairs_of(lambda z, x, y, c: (z, x, 1 - y, c) if c == 0 else (z, 1 - x, y, c))


def slice_order():
    order = np.zeros((len(DEVICES), 32), np.int32)
    for z, x, y, c in DEVICES:
        at_step = [z]
        for _ in range(3):
            at_step.append(BACK_Z[at_step[-1]])
        mine = {
            0: [(1 - x, y, 0), (1 - x, y, 1), (1 - x, 1 - y, 0)],
            1: [(x, 1 - y, 1), (x, 1 - y, 0), (1 - x, 1 - y, 1)],
        }
        places = [(x, y, c), (x, y, 1 - c)] + mine[c] + mine[1 - c]
        order[flat_index(z, x, y, c)] = [
            flat_index(at_step[2 * group + part], *place)
            for group in range(2)
            for place in places
            for part in range(2)
        ]
    return order


def send(array, pairs):
    return lax.ppermute(array, BOTH, pairs)


def added(first, second):
    return (first.astype(jnp.float32) + second.astype(jnp.float32)).astype(jnp.bfloat16)


def whole(space=pltpu.VMEM):
    return pl.BlockSpec(memory_space=space)


def pages_kernel(table, place, keys, values, joined, pages):
    heads = keys.shape[1] // HD
    for head in range(heads):
        lanes = slice(head * HD, (head + 1) * HD)
        joined[:, 2 * head * HD : (2 * head + 1) * HD] = keys[:, lanes]
        joined[:, (2 * head + 1) * HD : (2 * head + 2) * HD] = values[:, lanes]
    for page in range(keys.shape[0] // PAGE):
        pages[table[page] - place[0] * (keys.shape[0] // PAGE)] = joined[page * PAGE : (page + 1) * PAGE, :]


def write_pages(keys, values, block_table, place):
    rows, width = keys.shape
    return pl.pallas_call(
        pages_kernel,
        out_shape=(
            jax.ShapeDtypeStruct((rows, 2 * width), keys.dtype),
            jax.ShapeDtypeStruct((rows // PAGE, PAGE, 2 * width), keys.dtype),
        ),
        in_specs=[whole(pltpu.SMEM), whole(pltpu.SMEM), whole(), whole()],
        out_specs=(whole(), whole()),
    )(block_table, place, keys, values)


HEADS_HERE = 4


def attend(place, segments, query_segment, queries, blocks):
    offsets = lax.broadcasted_iota(jnp.int32, (1, BLOCK), 1)
    key_segment, key_place = [], []
    for _, source in blocks:
        line = segments[pl.ds(jnp.maximum(source, 0), 1), :]
        key_segment.append(jnp.where(source >= 0, line, -1))
        key_place.append(source * BLOCK + offsets)
    query_place = place[0] * BLOCK + lax.broadcasted_iota(jnp.int32, (BLOCK, 1), 0)
    allowed = (jnp.concatenate(key_segment, axis=1) == query_segment[...]) & (
        jnp.concatenate(key_place, axis=1) <= query_place
    )
    results = []
    for head in range(HEADS_HERE):
        key, value = [
            jnp.concatenate(
                [block[:, (2 * head + part) * HD : (2 * head + part + 1) * HD] for block, _ in blocks], axis=0
            )
            for part in range(2)
        ]
        scores = lax.dot_general(
            queries[:, head * HD : (head + 1) * HD],
            key,
            (((1,), (1,)), ((), ())),
            preferred_element_type=jnp.float32,
        ) * (1.0 / math.sqrt(HD))
        scores = jnp.where(allowed, scores, MASKED_SCORE)
        largest = jnp.max(scores, axis=1, keepdims=True)
        exp_scores = jnp.where(allowed, jnp.exp(scores - largest), 0.0)
        mixed = jnp.dot(exp_scores.astype(jnp.bfloat16), value, preferred_element_type=jnp.float32)
        results.append((largest, jnp.sum(exp_scores, axis=1, keepdims=True), mixed))
    return results


def attention_first(
    place, segments, query_segment, queries, own, near_x, near_z, top, total, mixed
):
    here = place[0]
    blocks = [(own, here), (near_x, jnp.where(here % 2 == 1, here - 1, -1)), (near_z, here - 2)]
    results = attend(place, segments, query_segment, queries, blocks)
    top[...] = jnp.concatenate([result[0] for result in results], axis=1)
    total[...] = jnp.concatenate([result[1] for result in results], axis=1)
    for head in range(HEADS_HERE):
        mixed[head] = results[head][2]


def attention_second(
    place, segments, query_segment, queries, cross, far, far_cross, projection,
    top, total, mixed, sent, kept, attended,
):
    here, hd = place[0], place[1]
    odd = here % 2
    blocks = [
        (cross, jnp.where(odd == 1, here - 3, here - 1)),
        (far, here - 4),
        (far_cross, jnp.where(odd == 1, -1, here - 3)),
    ]
    results = attend(place, segments, query_segment, queries, blocks)
    for head, (largest, added_up, update) in enumerate(results):
        before = top[:, head : head + 1]
        both = jnp.maximum(before, largest)
        old, new = jnp.exp(before - both), jnp.exp(largest - both)
        denom = total[:, head : head + 1] * old + added_up * new
        attended[:, head * HD : (head + 1) * HD] = (
            (mixed[head] * old + update * new) / denom
        ).astype(jnp.bfloat16)
    mate, across = hd ^ 1, hd ^ 2

    def rows_of(first, second):
        return jnp.concatenate(
            [
                attended[pl.ds(pl.multiple_of(quarter * ROWS, ROWS), ROWS), :]
                for quarter in (first, second)
            ],
            axis=0,
        )

    sent[...] = jnp.dot(
        rows_of(mate, mate ^ 2), projection[...], preferred_element_type=jnp.float32
    ).astype(jnp.bfloat16)
    kept[...] = jnp.dot(rows_of(hd, across), projection[...], preferred_element_type=jnp.float32)


def attention(
    place, segment_ids, query_segment, queries, own, near_x, near_z, cross, far, far_cross, out_proj
):
    segments = segment_ids.reshape(-1, BLOCK)
    state = (
        jax.ShapeDtypeStruct((BLOCK, HEADS_HERE), jnp.float32),
        jax.ShapeDtypeStruct((BLOCK, HEADS_HERE), jnp.float32),
        jax.ShapeDtypeStruct((HEADS_HERE, BLOCK, HD), jnp.float32),
    )
    smem, vmem = whole(pltpu.SMEM), whole()
    limit = pltpu.CompilerParams(vmem_limit_bytes=24 * 2**20)
    first = pl.pallas_call(
        attention_first,
        out_shape=state,
        in_specs=[smem] + [vmem] * 6,
        out_specs=(vmem, vmem, vmem),
        compiler_params=limit,
        cost_estimate=pl.CostEstimate(flops=8 * 10**8, bytes_accessed=4 * 10**6, transcendentals=8 * 10**5),
    )(place, segments, query_segment, queries, own, near_x, near_z)
    return pl.pallas_call(
        attention_second,
        out_shape=(
            jax.ShapeDtypeStruct((2 * ROWS, out_proj.shape[1]), jnp.bfloat16),
            jax.ShapeDtypeStruct((2 * ROWS, out_proj.shape[1]), jnp.float32),
        ),
        in_specs=[smem] + [vmem] * 10,
        out_specs=(vmem, vmem),
        scratch_shapes=[pltpu.VMEM((BLOCK, HEADS_HERE * HD), jnp.bfloat16)],
        compiler_params=limit,
        cost_estimate=pl.CostEstimate(flops=10**9, bytes_accessed=6 * 10**6, transcendentals=8 * 10**5),
    )(
        place, segments, query_segment, queries, cross, far, far_cross, out_proj, *first
    )


CHUNK = 512
WIDE = 512
PIECE = 2 * ROWS
PIECES = 8
DEPTH = 2


def silu_times(gate_val, up_val):
    return (gate_val / (1.0 + jnp.exp(-gate_val)) * up_val).astype(jnp.bfloat16)


def routing_kernel(place, order, slices, pick, spread, slot_weight, listed):
    count = slices.shape[1] // 2
    for number in range(32):
        listed[:, number * ROWS : (number + 1) * ROWS] = slices[order[number]]
    first_expert = (2 * (place[0] * 4 + place[1])).astype(jnp.float32)
    hits, weights = [], []
    for group in range(2):
        lanes = slice(group * GROUP_ROWS, (group + 1) * GROUP_ROWS)
        for expert in range(2):
            match = listed[:count, lanes] == first_expert + float(expert)
            hits.append(jnp.max(jnp.where(match, 1.0, 0.0), axis=0, keepdims=True))
            weights.append(jnp.sum(jnp.where(match, listed[count:, lanes], 0.0), axis=0, keepdims=True))
    hits = jnp.concatenate(hits + hits, axis=0)
    earlier = lax.broadcasted_iota(jnp.int32, (GROUP_ROWS, GROUP_ROWS), 0) < lax.broadcasted_iota(
        jnp.int32, (GROUP_ROWS, GROUP_ROWS), 1
    )
    before = jnp.dot(
        hits.astype(jnp.bfloat16),
        jnp.where(earlier, 1.0, 0.0).astype(jnp.bfloat16),
        preferred_element_type=jnp.float32,
    )
    slot = jnp.where(hits > 0.0, before, -1.0)
    slot_column = slot.T
    slot_numbers = lax.broadcasted_iota(jnp.int32, (SLOTS, GROUP_ROWS), 0).astype(jnp.float32)
    slot_lanes = lax.broadcasted_iota(jnp.int32, (GROUP_ROWS, 2 * SLOTS), 1).astype(jnp.float32)
    for group in range(2):
        for expert in range(2):
            line = 2 * group + expert
            held = slice(expert * SLOTS, (expert + 1) * SLOTS)
            hit = slot[line : line + 1] == slot_numbers
            pick[group, held] = jnp.where(hit, 1.0, 0.0).astype(jnp.bfloat16)
            slot_weight[group, held] = jnp.sum(jnp.where(hit, weights[line], 0.0), axis=1, keepdims=True)
        first, second = [slot_column[:, 2 * group + e : 2 * group + e + 1] for e in range(2)]
        hit = (first == slot_lanes) | ((second >= 0.0) & (second + float(SLOTS) == slot_lanes))
        spread[group] = jnp.where(hit, 1.0, 0.0).astype(jnp.bfloat16)


def experts_kernel(*refs):
    place, pick, spread, slot_weight = refs[:4]
    pieces, refs = refs[4 : 4 + 2 * PIECES], refs[4 + 2 * PIECES :]
    gate, up, down = refs[:3]
    shared = refs[3:6]
    targets, refs = refs[6 : 6 + 2 * PIECES], refs[6 + 2 * PIECES :]
    rows, picked, hidden, gate_held, up_held, down_held, arrived, gate_up_arrived, down_arrived = refs[:9]
    width = rows.shape[1]
    chunks = [
        (expert, low, min(CHUNK, FF_E - low)) for expert in range(2) for low in range(0, FF_E, CHUNK)
    ]

    def gate_up_copies(number):
        expert, low, size = chunks[number]
        lanes, slot = pl.ds(expert * FF_E + low, size), number % DEPTH
        return [
            pltpu.make_async_copy(
                source.at[:, lanes], held.at[slot, :, pl.ds(0, size)], gate_up_arrived.at[slot, which]
            )
            for which, (source, held) in enumerate(((gate, gate_held), (up, up_held)))
        ]

    def down_copy(expert):
        return pltpu.make_async_copy(
            down.at[pl.ds(expert * FF_E, FF_E), :], down_held.at[expert], down_arrived.at[expert]
        )

    copies = [
        pltpu.make_async_copy(piece, rows.at[pl.ds(number * PIECE, PIECE), :], arrived.at[number])
        for number, piece in enumerate(pieces)
    ]
    for copy in copies:
        copy.start()
    for number in range(DEPTH):
        for copy in gate_up_copies(number):
            copy.start()
    down_copy(0).start()
    s_gate, s_up, s_down, s_arrived, s_rows, s_hidden = refs[9:]
    s_copies = [
        pltpu.make_async_copy(source, target, s_arrived.at[number])
        for number, (source, target) in enumerate(zip(shared, (s_gate, s_up, s_down)))
    ]

    def slots(expert, group):
        return slice((2 * expert + group) * SLOTS, (2 * expert + group + 1) * SLOTS)

    for group in range(2):
        for copy in copies[group * PIECES : (group + 1) * PIECES]:
            copy.wait()
        for low in range(0, width, WIDE):
            lanes = slice(low, low + WIDE)
            both = jnp.dot(
                pick[group],
                rows[group * GROUP_ROWS : (group + 1) * GROUP_ROWS, lanes],
                preferred_element_type=jnp.float32,
            ).astype(jnp.bfloat16)
            for expert in range(2):
                picked[slots(expert, group), lanes] = both[expert * SLOTS : (expert + 1) * SLOTS]
    for number, (expert, low, size) in enumerate(chunks):
        held, slot = slice(2 * expert * SLOTS, 2 * (expert + 1) * SLOTS), number % DEPTH
        for copy in gate_up_copies(number):
            copy.wait()
        gate_val = jnp.dot(picked[held], gate_held[slot, :, :size], preferred_element_type=jnp.float32)
        up_val = jnp.dot(picked[held], up_held[slot, :, :size], preferred_element_type=jnp.float32)
        hidden[:, low : low + size] = silu_times(gate_val, up_val)
        if number + DEPTH < len(chunks):
            for copy in gate_up_copies(number + DEPTH):
                copy.start()
        if number == len(chunks) // 2:
            down_copy(1).start()
        if number == len(chunks) - DEPTH:
            for copy in s_copies:
                copy.start()
        if low + size == FF_E:
            down_copy(expert).wait()
            scale = jnp.concatenate(
                [slot_weight[group, expert * SLOTS : (expert + 1) * SLOTS] for group in range(2)], axis=0
            )
            for start in range(0, width, WIDE):
                lanes = slice(start, start + WIDE)
                result = jnp.dot(
                    hidden[...], down_held[expert, :, lanes], preferred_element_type=jnp.float32
                )
                picked[held, lanes] = (result * scale).astype(jnp.bfloat16)

    upper = place[1] % 2 == 1
    s_rows[0:ROWS] = rows[0:ROWS]
    s_rows[ROWS : 2 * ROWS] = rows[PIECE : PIECE + ROWS]
    base = pl.multiple_of(jnp.where(upper, 2, 5) * PIECE, PIECE)
    s_rows[2 * ROWS : 3 * ROWS] = rows[pl.ds(base, ROWS), :]
    s_rows[3 * ROWS : 4 * ROWS] = rows[pl.ds(base + PIECE, ROWS), :]
    for copy in s_copies:
        copy.wait()
    turned = (((1,), (1,)), ((), ()))
    units = s_gate.shape[0]
    for low in range(0, units, CHUNK):
        size = min(CHUNK, units - low)
        gate_val, up_val = [
            lax.dot_general(
                s_rows[...], weight[low : low + size, :], turned, preferred_element_type=jnp.float32
            )
            for weight in (s_gate, s_up)
        ]
        s_hidden[:, low : low + size] = silu_times(gate_val, up_val)

    for low in range(0, width, CHUNK):
        lanes = slice(low, low + CHUNK)
        s_result = jnp.dot(s_hidden[...], s_down[:, lanes], preferred_element_type=jnp.float32)
        for group in range(2):
            value = jnp.dot(
                spread[group],
                jnp.concatenate([picked[slots(expert, group), lanes] for expert in range(2)], axis=0),
                preferred_element_type=jnp.float32,
            )
            for part, target in enumerate(targets[group * PIECES : (group + 1) * PIECES]):
                mine = value[part * PIECE : (part + 1) * PIECE]
                if group == 0 and part in (0, 1, 2, 3, 5, 6):
                    if part < 2:
                        term = s_result[part * ROWS : (part + 1) * ROWS]
                    else:
                        start = (2 + (part - 2) % 3) * ROWS
                        here = upper if part < 4 else jnp.logical_not(upper)
                        term = jnp.where(here, s_result[start : start + ROWS], 0.0)
                    target[:ROWS, lanes] = (mine[:ROWS] + term).astype(jnp.bfloat16)
                    target[ROWS:, lanes] = mine[ROWS:].astype(jnp.bfloat16)
                else:
                    target[:, lanes] = mine.astype(jnp.bfloat16)


def experts(place, matrices, pieces, weights, shared):
    width = pieces[0].shape[1]
    hbm, vmem = whole(pl.ANY), whole()
    scratch = [
        pltpu.VMEM((2 * GROUP_ROWS, width), jnp.bfloat16),
        pltpu.VMEM((4 * SLOTS, width), jnp.bfloat16),
        pltpu.VMEM((2 * SLOTS, FF_E), jnp.bfloat16),
        pltpu.VMEM((DEPTH, width, CHUNK), jnp.bfloat16),
        pltpu.VMEM((DEPTH, width, CHUNK), jnp.bfloat16),
        pltpu.VMEM((2, FF_E, width), jnp.bfloat16),
        pltpu.SemaphoreType.DMA((2 * PIECES,)),
        pltpu.SemaphoreType.DMA((DEPTH, 2)),
        pltpu.SemaphoreType.DMA((2,)),
        *[pltpu.VMEM(array.shape, array.dtype) for array in shared],
        pltpu.SemaphoreType.DMA((3,)),
        pltpu.VMEM((BLOCK, width), jnp.bfloat16),
        pltpu.VMEM((BLOCK, shared[2].shape[0]), jnp.bfloat16),
    ]
    operands = [place, *matrices, *pieces, *weights, *shared]
    in_specs = [whole(pltpu.SMEM)] + [vmem] * 3
    in_specs += [hbm] * (len(operands) - len(in_specs))
    return pl.pallas_call(
        experts_kernel,
        out_shape=(jax.ShapeDtypeStruct((PIECE, width), jnp.bfloat16),) * (2 * PIECES),
        in_specs=in_specs,
        out_specs=(vmem,) * (2 * PIECES),
        scratch_shapes=scratch,
        compiler_params=pltpu.CompilerParams(vmem_limit_bytes=60 * 2**20),
        cost_estimate=pl.CostEstimate(
            flops=2 * 10**10, bytes_accessed=60 * 10**6, transcendentals=2 * 10**6
        ),
    )(*operands)


def gather_plane(rows):
    mate = send(rows, CORE_SWAP)
    near = send(rows, X_THEN_Y)
    near_mate = send(mate, X_THEN_Y)
    corner = send(near, Y_THEN_X)
    fetched = (near, near_mate, corner)
    return (rows, mate, *fetched, *[send(piece, CORE_SWAP) for piece in fetched])


def sum_plane(own, mate, near, near_mate, corner, mate_near, mate_near_mate, mate_corner):
    corner = added(corner, send(mate_corner, CORE_SWAP))
    from_corner = send(corner, Y_THEN_X)
    near_mate = added(near_mate, send(mate_near_mate, CORE_SWAP))
    from_near_mate = send(near_mate, X_THEN_Y)
    near = near.astype(jnp.float32) + send(mate_near, CORE_SWAP).astype(jnp.float32)
    from_near = send(added(near, from_corner), X_THEN_Y)
    return (
        own.astype(jnp.float32)
        + send(mate, CORE_SWAP).astype(jnp.float32)
        + send(from_near_mate, CORE_SWAP).astype(jnp.float32)
        + from_near.astype(jnp.float32)
    )


def routing_slices(expert_ids, route_weight):
    packed = jnp.concatenate([expert_ids.T.astype(jnp.float32), route_weight.T], axis=0)
    packed = packed.reshape(-1, 4, ROWS).transpose(1, 0, 2)
    blocks = 2 * NZ
    slices = lax.all_to_all(
        jnp.broadcast_to(packed[None], (blocks, *packed.shape)), "tok", split_axis=0, concat_axis=0, tiled=True
    ).reshape(-1, *packed.shape[1:])
    return slices


def routing_tables(slices, place, device):
    order = lax.dynamic_index_in_dim(jnp.asarray(slice_order()), device, 0, keepdims=False)
    return pl.pallas_call(
        routing_kernel,
        out_shape=(
            jax.ShapeDtypeStruct((2, 2 * SLOTS, GROUP_ROWS), jnp.bfloat16),
            jax.ShapeDtypeStruct((2, GROUP_ROWS, 2 * SLOTS), jnp.bfloat16),
            jax.ShapeDtypeStruct((2, 2 * SLOTS, 1), jnp.float32),
        ),
        in_specs=[whole(pltpu.SMEM), whole(pltpu.SMEM), whole()],
        out_specs=(whole(),) * 3,
        scratch_shapes=[pltpu.VMEM((slices.shape[1], 2 * GROUP_ROWS), jnp.float32)],
        compiler_params=pltpu.CompilerParams(vmem_limit_bytes=24 * 2**20),
    )(place, order, slices)


def block_pairs(target):
    pairs = []
    for z in range(NZ):
        for x in range(2):
            aim = target(z, x)
            if aim is not None and aim[0] < NZ:
                pairs.append((z * 2 + x, aim[0] * 2 + aim[1]))
    return pairs


def sliced_body(
    residual_in,
    queries,
    keys,
    values,
    segment_ids,
    out_proj,
    norm_gain,
    shared_gate,
    shared_up,
    shared_down,
    expert_gate,
    expert_up,
    expert_down,
    expert_ids,
    route_weight,
    block_table,
):
    tok_here = lax.axis_index("tok")
    hd_here = lax.axis_index("hd")
    place = jnp.stack([tok_here, hd_here]).astype(jnp.int32)
    own, kv_pages = write_pages(keys, values, block_table, place)

    def move(array, target):
        return lax.ppermute(array, "tok", block_pairs(target))

    near_z = move(own, lambda z, x: (z + 1, x))
    own_later, _ = lax.optimization_barrier((own, near_z))
    near_x = move(own_later, lambda z, x: (z, 1) if x == 0 else None)
    weights = (expert_gate, expert_up, expert_down)
    shared = (shared_gate.T, shared_up.T, shared_down)
    near_z, slices = lax.optimization_barrier((near_z, routing_slices(expert_ids, route_weight)))
    cross = move(near_z, lambda z, x: (z, 1 - x))
    far = move(near_z, lambda z, x: (z + 1, x))
    far_cross = move(near_z, lambda z, x: (z + 1, 0) if x == 1 else None)

    tables = routing_tables(slices, place, tok_here * 4 + hd_here)
    query_segment = lax.dynamic_slice_in_dim(segment_ids, tok_here * BLOCK, BLOCK, 0)[:, None]
    queries, tables = lax.optimization_barrier((queries, tables))
    sent, kept = attention(
        place, segment_ids, query_segment, queries, own, near_x, near_z, cross, far, far_cross, out_proj
    )
    kept = kept + send(sent, CORE_SWAP).astype(jnp.float32)
    resid_rows = (
        lax.dynamic_slice_in_dim(residual_in, hd_here * ROWS, ROWS, 0).astype(jnp.float32)
        + kept[:ROWS]
        + send(kept[ROWS:].astype(jnp.bfloat16), Y_SWAP).astype(jnp.float32)
    )
    normed = rms_normed(resid_rows, norm_gain)

    steps = [normed]
    for _ in range(3):
        steps.append(send(steps[-1], Z_ON))
    pieces = []
    for group in range(2):
        pieces += gather_plane(jnp.concatenate(steps[2 * group : 2 * group + 2], axis=0))
    terms = experts(place, tables, pieces, weights, shared)
    sums = [sum_plane(*terms[group * PIECES : (group + 1) * PIECES]) for group in range(2)]
    returned = [
        send(part.astype(jnp.bfloat16), pairs).astype(jnp.float32)
        for part, pairs in ((sums[0][ROWS:], Z_BACK), (sums[1][:ROWS], Z_TWO), (sums[1][ROWS:], Z_ON))
    ]
    output = resid_rows + sums[0][:ROWS] + returned[0] + returned[1] + returned[2]
    return (output.astype(jnp.bfloat16), kv_pages)


def solution(mesh):
    placed = (
        P("tok", None),
        P("tok", "hd"),
        P("tok", "hd"),
        P("tok", "hd"),
        P(),
        P("hd", None),
        P(),
        P(None, "hd"),
        P(None, "hd"),
        P("hd", None),
        P(None, ("tok", "hd")),
        P(None, ("tok", "hd")),
        P(("tok", "hd"), None),
        P("tok", None),
        P("tok", None),
        P("tok"),
    )
    return jax.shard_map(
        sliced_body if dict(mesh.shape) == {"tok": 2 * NZ, "hd": 4} else general_body,
        mesh=mesh,
        in_specs=placed,
        out_specs=(P(("tok", "hd"), None), P("tok", None, "hd")),
        check_vma=False,
    )
```
